128 devices in a mesh: lon: 8 (over x, z_lo), lat: 16 (over y, z_hi, core).
Axes of the slice: x: 4, y: 4, z: 4 (z_hi: 2, z_lo: 2; z = z_hi * 2 + z_lo), core: 2. Of those that a mesh axis runs over, the one named last changes fastest.
Arguments:
- fields: float32 [192, 192, 1, 512], P('lat', 'lon'), may hold values from -6 to 6
- cotangent: float32 [192, 192, 1, 512], P('lat', 'lon'), may hold values from -6 to 6
- encoder_gain: float32 [512], replicated, may hold values from 0.25 to 1.75
- encoder_query: bfloat16 [512, 512], replicated, may hold values from -0.25 to 0.25
- encoder_keyval: bfloat16 [512, 1024], replicated, may hold values from -0.25 to 0.25
- encoder_output: bfloat16 [512, 512], replicated, may hold values from -0.25 to 0.25
- encoder_scale: float32 [8], replicated, may hold values from 2 to 12
- merge_gain: float32 [2048], replicated, may hold values from 0.25 to 1.75
- merge_weight: bfloat16 [2048, 1024], replicated, may hold values from -0.125 to 0.125
- coarse_gain: float32 [1024], replicated, may hold values from 0.25 to 1.75
- coarse_query: bfloat16 [1024, 1024], replicated, may hold values from -0.1875 to 0.1875
- coarse_keyval: bfloat16 [1024, 2048], replicated, may hold values from -0.1875 to 0.1875
- coarse_output: bfloat16 [1024, 1024], replicated, may hold values from -0.1875 to 0.1875
- coarse_scale: float32 [16], replicated, may hold values from 2 to 12
- expand_gain: float32 [1024], replicated, may hold values from 0.25 to 1.75
- expand_weight: bfloat16 [1024, 2048], replicated, may hold values from -0.1875 to 0.1875
- decoder_gain: float32 [512], replicated, may hold values from 0.25 to 1.75
- decoder_query: bfloat16 [512, 512], replicated, may hold values from -0.25 to 0.25
- decoder_keyval: bfloat16 [512, 1024], replicated, may hold values from -0.25 to 0.25
- decoder_output: bfloat16 [512, 512], replicated, may hold values from -0.25 to 0.25
- decoder_scale: float32 [8], replicated, may hold values from 2 to 12
Outputs:
- output: float32 [192, 192, 1, 512], P('lat', 'lon')
- grad_fields: float32 [192, 192, 1, 512], P('lat', 'lon')
The draws below stay inside these ranges and needn't reach their ends.
All inputs are finite; a program needn't handle non-finite values.
Results may differ from the reference program's by a relative error of at most 0.025.
Values may be sent and summed in bfloat16 or wider, within the bound.
A program may use at most 192 MiB of HBM per device.

```python
import math
import jax
import jax.numpy as jnp
from jax import lax

D = 512
DC = 1024
HF = 8
HC = 16
WLAT = 6
WLON = 12
LEV = 1
NLAT = 192
NLON = 192


def level_of(stream_key, shape, cuts, low, top_value):
    loudness, own = 1.0, jax.random.fold_in(stream_key, 6)
    for dim, shards_of in cuts:
        draws = jnp.exp(jax.random.uniform(jax.random.fold_in(own, dim), (shards_of,), jnp.float32, low / len(cuts), top_value / len(cuts)))
        loudness = loudness * jnp.repeat(draws, shape[dim] // shards_of).reshape([-1 if axis == dim else 1 for axis in range(len(shape))])
    return loudness


def normal_values(own_key, shape, scale, reach, cuts=(), held_as=jnp.bfloat16):
    array = scale * jax.random.normal(own_key, shape, jnp.float32)
    if cuts:
        array = array * level_of(own_key, shape, cuts, -0.22, 0.18)
    return jnp.clip(array, -reach, reach).astype(held_as)


def setup_inputs(seed: int = 0) -> dict:
    arg_keys = jax.random.split(jax.random.key(seed), 22)
    fields = normal_values(arg_keys[0], (NLAT, NLON, LEV, D), 1.0, 6.0, ((0, 16), (1, 8)), jnp.float32)
    cotangent = normal_values(arg_keys[1], (NLAT, NLON, LEV, D), 1.0, 6.0, ((0, 16), (1, 8)), jnp.float32)
    encoder_gain = jnp.clip(1.0 + 0.15 * jax.random.normal(arg_keys[2], (D,), jnp.float32), 0.25, 1.75)
    encoder_query = normal_values(arg_keys[3], (D, D), D ** -0.5, 0.25)
    encoder_keyval = normal_values(arg_keys[4], (D, 2 * D), D ** -0.5, 0.25)
    encoder_output = normal_values(arg_keys[5], (D, D), D ** -0.5, 0.25)
    encoder_scale = jnp.clip(jnp.exp(jax.random.uniform(arg_keys[6], (HF,), jnp.float32, math.log(2.0), math.log(12.0))), 2.0, 12.0)
    merge_gain = jnp.clip(1.0 + 0.15 * jax.random.normal(arg_keys[7], (4 * D,), jnp.float32), 0.25, 1.75)
    merge_weight = normal_values(arg_keys[8], (4 * D, DC), (4 * D) ** -0.5, 0.125)
    coarse_gain = jnp.clip(1.0 + 0.15 * jax.random.normal(arg_keys[9], (DC,), jnp.float32), 0.25, 1.75)
    coarse_query = normal_values(arg_keys[10], (DC, DC), DC ** -0.5, 0.1875)
    coarse_keyval = normal_values(arg_keys[11], (DC, 2 * DC), DC ** -0.5, 0.1875)
    coarse_output = normal_values(arg_keys[12], (DC, DC), DC ** -0.5, 0.1875)
    coarse_scale = jnp.clip(jnp.exp(jax.random.uniform(arg_keys[13], (HC,), jnp.float32, math.log(2.0), math.log(12.0))), 2.0, 12.0)
    expand_gain = jnp.clip(1.0 + 0.15 * jax.random.normal(arg_keys[14], (DC,), jnp.float32), 0.25, 1.75)
    expand_weight = normal_values(arg_keys[15], (DC, 4 * D), DC ** -0.5, 0.1875)
    decoder_gain = jnp.clip(1.0 + 0.15 * jax.random.normal(arg_keys[16], (D,), jnp.float32), 0.25, 1.75)
    decoder_query = normal_values(arg_keys[17], (D, D), D ** -0.5, 0.25)
    decoder_keyval = normal_values(arg_keys[18], (D, 2 * D), D ** -0.5, 0.25)
    decoder_output = normal_values(arg_keys[19], (D, D), D ** -0.5, 0.25)
    decoder_scale = jnp.clip(jnp.exp(jax.random.uniform(arg_keys[20], (HF,), jnp.float32, math.log(2.0), math.log(12.0))), 2.0, 12.0)
    return dict(fields=fields, cotangent=cotangent, encoder_gain=encoder_gain, encoder_query=encoder_query, encoder_keyval=encoder_keyval, encoder_output=encoder_output, encoder_scale=encoder_scale, merge_gain=merge_gain, merge_weight=merge_weight, coarse_gain=coarse_gain, coarse_query=coarse_query, coarse_keyval=coarse_keyval, coarse_output=coarse_output, coarse_scale=coarse_scale, expand_gain=expand_gain, expand_weight=expand_weight, decoder_gain=decoder_gain, decoder_query=decoder_query, decoder_keyval=decoder_keyval, decoder_output=decoder_output, decoder_scale=decoder_scale)


EPS = 1e-05

def norm_round(tensor, scaling):
    average = lax.optimization_barrier(jnp.mean(tensor, axis=-1, keepdims=True))
    centred = tensor - average
    spread = lax.optimization_barrier(jnp.mean(centred * centred, axis=-1, keepdims=True))
    return (centred * lax.rsqrt(spread + EPS) * scaling.astype(jnp.float32)).astype(jnp.bfloat16)

def project(normed, weight):
    flattened = normed.reshape(-1, normed.shape[-1])
    result = jnp.dot(flattened, weight, preferred_element_type=jnp.float32)
    return result.reshape(normed.shape[:-1] + (weight.shape[1],))

def unit_heads(tensor, head_count):
    shaped = tensor.astype(jnp.float32).reshape(tensor.shape[:-1] + (head_count, tensor.shape[-1] // head_count))
    return (shaped * lax.rsqrt(lax.optimization_barrier(jnp.sum(shaped * shaped, axis=-1, keepdims=True)) + 1.0)).astype(jnp.bfloat16)

def to_windows(tensor):
    extent, across, levels, channels = tensor.shape
    shaped = tensor.reshape(extent // WLAT, WLAT, across // WLON, WLON, levels, channels)
    shaped = shaped.transpose(0, 2, 1, 3, 4, 5)
    return shaped.reshape(extent // WLAT, across // WLON, WLAT * WLON * levels, channels)

def from_windows(tensor, levels):
    band_count, sector_count, tokens, channels = tensor.shape
    shaped = tensor.reshape(band_count, sector_count, WLAT, WLON, levels, channels)
    shaped = shaped.transpose(0, 2, 1, 3, 4, 5)
    return shaped.reshape(band_count * WLAT, sector_count * WLON, levels, channels)

def attend(query, keyval, key_ok, scaling, head_count):
    channels = query.shape[-1]
    levels = query.shape[2]
    queries = unit_heads(to_windows(query), head_count)
    paired = to_windows(keyval)
    keys = unit_heads(paired[..., :channels], head_count)
    values = paired[..., channels:].reshape(paired.shape[:-1] + (head_count, channels // head_count))
    valid = to_windows(jnp.broadcast_to(key_ok[:, None, None, None], query.shape[:3] + (1,)))[..., 0]
    scores = jnp.einsum('abqhd,abkhd->abhqk', queries.astype(jnp.float32), keys.astype(jnp.float32))
    scores = scores * scaling[:, None, None]
    weights = jnp.exp(scores) * valid[:, :, None, None, :]
    probs = (weights / lax.optimization_barrier(jnp.sum(weights, axis=-1, keepdims=True))).astype(jnp.bfloat16)
    mixed = jnp.einsum('abhqk,abkhd->abqhd', probs.astype(jnp.float32), values.astype(jnp.float32)).astype(jnp.bfloat16)
    return from_windows(mixed.reshape(mixed.shape[:3] + (channels,)), levels)

def block(stream, scaling_gain, query_weight, keyval_weight, output_weight, logit_scale):
    head_count = logit_scale.shape[0]
    band_half = WLAT // 2
    sector_half = WLON // 2
    normed = norm_round(stream, scaling_gain)
    query = project(normed, query_weight).astype(jnp.bfloat16)
    keyval = project(normed, keyval_weight).astype(jnp.bfloat16)

    def shifted(tensor):
        rolled = jnp.roll(tensor, sector_half, axis=1)
        return jnp.pad(rolled, ((band_half, band_half), (0, 0), (0, 0), (0, 0)))
    query_moved = shifted(query)
    pairs_moved = shifted(keyval)
    extent = query_moved.shape[0]
    position = jnp.arange(extent)
    key_ok = ((position >= band_half) & (position < extent - band_half)).astype(jnp.float32)
    band_count = extent // WLAT

    def one_band(pieces):
        return attend(pieces[0], pieces[1], pieces[2], logit_scale, head_count)
    mixed = lax.map(one_band, (query_moved.reshape((band_count, WLAT) + query_moved.shape[1:]), pairs_moved.reshape((band_count, WLAT) + pairs_moved.shape[1:]), key_ok.reshape(band_count, WLAT)))
    mixed = mixed.reshape(query_moved.shape)[band_half:extent - band_half]
    mixed = jnp.roll(mixed, -sector_half, axis=1)
    return stream + project(mixed, output_weight)

def merge_patches(stream, scaling_gain, weight):
    extent, across, levels, channels = stream.shape
    grouped = stream.reshape(extent // 2, 2, across // 2, 2, levels, channels).transpose(0, 2, 4, 1, 3, 5)
    grouped = grouped.reshape(extent // 2, across // 2, levels, 4 * channels)
    return project(norm_round(grouped, scaling_gain), weight)

def expand_patches(coarse, scaling_gain, weight):
    spread_out = project(norm_round(coarse, scaling_gain), weight)
    extent, across, levels, channels = spread_out.shape
    fine_width = channels // 4
    shaped = spread_out.reshape(extent, across, levels, 2, 2, fine_width).transpose(0, 3, 1, 4, 2, 5)
    return shaped.reshape(2 * extent, 2 * across, levels, fine_width)

def reference(fields, cotangent, encoder_gain, encoder_query, encoder_keyval, encoder_output, encoder_scale, merge_gain, merge_weight, coarse_gain, coarse_query, coarse_keyval, coarse_output, coarse_scale, expand_gain, expand_weight, decoder_gain, decoder_query, decoder_keyval, decoder_output, decoder_scale):

    def forward(state):
        section_one = block(state, encoder_gain, encoder_query, encoder_keyval, encoder_output, encoder_scale)
        coarse_in = merge_patches(section_one, merge_gain, merge_weight)
        coarse_out = block(coarse_in, coarse_gain, coarse_query, coarse_keyval, coarse_output, coarse_scale)
        skipped = section_one + expand_patches(coarse_out, expand_gain, expand_weight)
        return block(skipped, decoder_gain, decoder_query, decoder_keyval, decoder_output, decoder_scale)
    output, pull_back = jax.vjp(forward, fields)
    grad_fields = pull_back(cotangent)[0]
    return (output, grad_fields)
```

```python
import functools

import jax
import jax.numpy as jnp
import numpy as np
from jax import lax
from jax.experimental import pallas as pl
from jax.experimental.pallas import tpu as pltpu
from jax.sharding import PartitionSpec as P

WLAT = 6
WLON = 12
EPS = 1e-05
ROWS, COLS = 12, 24
HOME = ROWS * COLS
PAD = 80
BODY = 4 * PAD
CELLS = WLAT * WLON
PIECES = ((0, 64), (64, 64), (128, 32))
SENT = 160
D = 512
DC = 1024
F32 = jnp.float32
BF16 = jnp.bfloat16


def fine_order(r, c):
    return PAD * (2 * (r // WLAT) + c // WLON) + (r % WLAT) * WLON + c % WLON


def plane_order(r, c):
    return PAD * (2 * (r % 2) + c % 2) + (r // 2) * WLON + c // 2


def home_order(r, c):
    return r * COLS + c


def piece_row(r, c):
    if r >= 9 and c < 18:
        return (r - 9) * 18 + c
    if r < 9 and c >= 18:
        return 64 + r * 6 + (c - 18)
    if r >= 9 and c >= 18:
        return 128 + (r - 9) * 6 + (c - 18)
    return None


def move_matrices(order_a, rows_a, order_b, rows_b):
    pick = np.zeros((SENT, rows_a), np.float32)
    own = np.zeros((rows_b, rows_a), np.float32)
    place = np.zeros((rows_b, SENT), np.float32)
    for r in range(ROWS):
        for c in range(COLS):
            piece = piece_row(r, c)
            if piece is not None:
                pick[piece, order_a(r, c)] = 1
            ra, ca = (r - 3) % ROWS, (c - 6) % COLS
            if r >= 3 and c >= 6:
                own[order_b(r, c), order_a(ra, ca)] = 1
            else:
                place[order_b(r, c), piece_row(ra, ca)] = 1
    return pick, own, place


def all_moves():
    first = move_matrices(home_order, HOME, fine_order, BODY)
    second = move_matrices(fine_order, BODY, plane_order, BODY)
    pick, own, place = first
    moves = [pick, own, place, place.T, own.T, pick.T]
    pick, own, place = second
    moves += [pick, own, place, place.T, own.T, pick.T]
    return [np.ascontiguousarray(m).astype(jnp.bfloat16) for m in moves]


def mm(a, b):
    return lax.dot_general(a, b, (((1,), (0,)), ((), ())), preferred_element_type=F32)


def mm_nt(a, b):
    return lax.dot_general(a, b, (((1,), (1,)), ((), ())), preferred_element_type=F32)


def mm_tn(a, b):
    return lax.dot_general(a, b, (((0,), (0,)), ((), ())), preferred_element_type=F32)


def row_mean(x):
    return jnp.mean(x, axis=-1, keepdims=True)


def at_rows(g, n=PAD):
    if isinstance(g, int):
        return pl.ds(g * n, n)
    return pl.ds(pl.multiple_of(g * n, n), n)


def at_lanes(j, n):
    if isinstance(j, int):
        return pl.ds(j * n, n)
    return pl.ds(pl.multiple_of(j * n, n), n)


def head_sums():
    shape = (256, 256)
    a = lax.broadcasted_iota(jnp.int32, shape, 0) // 64
    b = lax.broadcasted_iota(jnp.int32, shape, 1) // 64
    return jnp.where(a == b, 1.0, 0.0).astype(BF16)


def pair_masks():
    lane = lax.broadcasted_iota(jnp.int32, (PAD, 128), 1)
    return lane < 64


def stack_pair(x, low):
    zero = jnp.zeros_like(x)
    return jnp.concatenate([jnp.where(low, x, zero), jnp.where(low, zero, x)], axis=0)


class Block:
    def __init__(self, rows, channels, gain, wq, wkv, wo, scale, kept, sums):
        self.rows, self.channels = rows, channels
        self.gain, self.wq, self.wkv, self.wo, self.scale = gain, wq, wkv, wo, scale
        self.xhat, self.rstd, self.uq, self.uk, self.rq, self.rk, self.v, self.probs = kept
        self.sums = sums
        self.groups = rows // PAD * (channels // 512)

    def tile(self, g):
        if self.channels == 512:
            return at_rows(g), 0, 0
        return at_rows(0), g, 8 * g

    def norm_rows(self, g, x, n_ref):
        centred = x - row_mean(x)
        rstd = lax.rsqrt(row_mean(centred * centred) + EPS)
        xhat = centred * rstd
        self.xhat[at_rows(g), :] = xhat
        self.rstd[at_rows(g), :] = jnp.broadcast_to(rstd, (PAD, 128))
        n_ref[at_rows(g), :] = (xhat * self.gain[...]).astype(BF16)

    def project(self, n_ref):
        channels = self.channels

        def unit(weight, at, u_ref, r_ref):
            raw = mm(n_ref[...], weight[:, at]).astype(BF16).astype(F32)
            r = lax.rsqrt(mm((raw * raw).astype(BF16), self.sums[...]) + 1.0)
            r_ref[:, at] = r
            u_ref[:, at] = (raw * r).astype(BF16)

        def body(j, carry):
            at = at_lanes(j, 256)
            unit(self.wq, at, self.uq, self.rq)
            unit(self.wkv, at, self.uk, self.rk)
            behind = at_lanes(j + channels // 256, 256)
            self.v[:, at] = mm(n_ref[...], self.wkv[:, behind]).astype(BF16)
            return carry

        lax.fori_loop(0, channels // 256, body, 0)

    def scales(self, head):
        top = lax.broadcasted_iota(jnp.int32, (2 * PAD, 1), 0) < PAD
        return jnp.where(top, self.scale[head], self.scale[head + 1])

    def attend(self, mask_ref, mixed_ref):
        low = pair_masks()

        def body(g, carry):
            rows, block, head0 = self.tile(g)
            if self.channels == 512:
                mask = mask_ref[g // 2]
            else:
                mask = mask_ref[0]
            for p in range(4):
                lanes = at_lanes(4 * block + p, 128)
                queries = stack_pair(self.uq[rows, lanes], low)
                scores = mm_nt(queries, self.uk[rows, lanes])
                weights = jnp.exp(scores * self.scales(head0 + 2 * p)) * mask
                total = jnp.sum(weights, axis=-1, keepdims=True)
                probs = (weights * (1.0 / total)).astype(BF16)
                self.probs[4 * g + p] = probs
                both = mm(probs, self.v[rows, lanes])
                mixed_ref[rows, lanes] = jnp.where(low, both[:PAD], both[PAD:]).astype(BF16)
            return carry

        lax.fori_loop(0, self.groups, body, 0)

    def outward(self, mixed_ref, add):
        def body(j, carry):
            at = at_lanes(j, 256)
            add(at, mm(mixed_ref[...], self.wo[:, at]))
            return carry

        lax.fori_loop(0, self.channels // 256, body, 0)

    def backward(self, grad_ref, dmixed_ref, duq_ref, duk_ref, dqkv_ref, dn_ref):
        channels = self.channels
        low = pair_masks()

        def out_body(j, carry):
            at = at_lanes(j, 256)
            dmixed_ref[:, at] = mm_nt(grad_ref[...], self.wo[at, :]).astype(BF16)
            return carry

        lax.fori_loop(0, channels // 256, out_body, 0)

        def body(g, carry):
            rows, block, head0 = self.tile(g)
            for p in range(4):
                lanes = at_lanes(4 * block + p, 128)
                behind = at_lanes(4 * block + p + 2 * (channels // 128), 128)
                douts = stack_pair(dmixed_ref[rows, lanes], low)
                keys = self.uk[rows, lanes]
                queries = stack_pair(self.uq[rows, lanes], low)
                probs = self.probs[4 * g + p]
                dprobs = mm_nt(douts, self.v[rows, lanes])
                wide = probs.astype(F32)
                weighed = wide * dprobs
                total = jnp.sum(weighed, axis=-1, keepdims=True)
                scale = self.scales(head0 + 2 * p)
                dscores = ((weighed - wide * total) * scale).astype(BF16)
                dqkv_ref[rows, behind] = mm_tn(probs, douts).astype(BF16)
                both = mm(dscores, keys)
                duq_ref[rows, lanes] = jnp.where(low, both[:PAD], both[PAD:])
                duk_ref[rows, lanes] = mm_tn(dscores, queries)
            return carry

        lax.fori_loop(0, self.groups, body, 0)

        def unit_body(j, carry):
            at = at_lanes(j, 256)
            shifted = at_lanes(j + channels // 256, 256)
            for u_ref, r_ref, du_ref, to in (
                (self.uq, self.rq, duq_ref, at),
                (self.uk, self.rk, duk_ref, shifted),
            ):
                u = u_ref[:, at].astype(F32)
                du = du_ref[:, at]
                inner = mm((u * du).astype(BF16), self.sums[...])
                dqkv_ref[:, to] = (r_ref[:, at] * (du - u * inner)).astype(BF16)
            return carry

        lax.fori_loop(0, channels // 256, unit_body, 0)

        def in_body(j, carry):
            at = at_lanes(j, 256)
            dn_ref[:, at] = mm_nt(dqkv_ref[:, :channels], self.wq[at, :]) + mm_nt(
                dqkv_ref[:, channels:], self.wkv[at, :]
            )
            return carry

        lax.fori_loop(0, channels // 256, in_body, 0)

    def norm_backward(self, g, dn):
        dy = dn * self.gain[...]
        xhat = self.xhat[at_rows(g), :]
        rstd = self.rstd[at_rows(g), :][:, :1]
        return rstd * (dy - row_mean(dy) - xhat * row_mean(dy * xhat))


WEIGHTS = (
    "encoder_query",
    "encoder_keyval",
    "encoder_output",
    "merge_weight",
    "coarse_query",
    "coarse_keyval",
    "coarse_output",
    "expand_weight",
    "decoder_query",
    "decoder_keyval",
    "decoder_output",
)


def kept_shapes(rows, channels):
    units = rows // PAD * (channels // 128)
    return [
        ((rows, channels), F32),
        ((rows, 128), F32),
        ((rows, channels), BF16),
        ((rows, channels), BF16),
        ((rows, channels), F32),
        ((rows, channels), F32),
        ((rows, channels), BF16),
        ((units, 2 * PAD, PAD), BF16),
    ]


def scratch_table():
    table = {}
    for block, rows, channels in (("enc", BODY, D), ("dec", BODY, D), ("crs", PAD, DC)):
        table[block] = kept_shapes(rows, channels)
    for kind, rows, channels in (("fine", BODY, D), ("coarse", PAD, DC)):
        table[kind] = [
            ((rows, channels), BF16),
            ((rows, channels), BF16),
            ((rows, channels), F32),
            ((rows, channels), F32),
            ((rows, 3 * channels), BF16),
            ((rows, channels), F32),
            ((rows, channels), F32),
            ((rows, channels), BF16),
        ]
    table["misc"] = [
        ((HOME, D), BF16),
        ((HOME, D), BF16),
        ((BODY, D), F32),
        ((BODY, D), F32),
        ((BODY, D), F32),
        ((PAD, 4 * D), F32),
        ((PAD, 128), F32),
        ((PAD, 4 * D), BF16),
        ((PAD, DC), F32),
        ((PAD, 128), F32),
        ((PAD, 4 * D), BF16),
        ((HOME, D), F32),
        ((2, 2 * PAD, PAD), F32),
        ((256, 256), BF16),
        ((8, SENT, D), BF16),
        ((8, SENT, D), BF16),
    ]
    return table


TABLE = scratch_table()
NAMES = tuple(TABLE)


def kernel(*refs):
    refs = list(refs)

    def take(n):
        head = refs[:n]
        del refs[:n]
        return head

    fields_in, cot_in = take(2)
    weights_in = take(len(WEIGHTS))
    moves_in = take(12)
    enc_gain, merge_gain, crs_gain, exp_gain, dec_gain = take(5)
    enc_scale, crs_scale, dec_scale = take(3)
    out_ref, grad_ref = take(2)
    fields_v, cot_v = take(2)
    weights = take(len(WEIGHTS))
    moves = take(12)
    spaces = {name: take(len(TABLE[name])) for name in NAMES}
    local_sem, send_sem, recv_sem = take(3)

    lat, lon = lax.axis_index("lat"), lax.axis_index("lon")
    nlat, nlon = lax.axis_size("lat"), lax.axis_size("lon")

    loads = []
    order = [(fields_in, fields_v), (moves_in[0], moves[0]), (moves_in[1], moves[1])]
    order += [(moves_in[2], moves[2]), (cot_in, cot_v)]
    order += list(zip(weights_in[:3], weights[:3]))
    order += list(zip(moves_in[6:9], moves[6:9]))
    order += list(zip(weights_in[3:8], weights[3:8]))
    order += list(zip(moves_in[9:], moves[9:]))
    order += list(zip(weights_in[8:], weights[8:]))
    order += list(zip(moves_in[3:6], moves[3:6]))
    for k, (src, dst) in enumerate(order):
        copy = pltpu.make_async_copy(src, dst, local_sem.at[k])
        copy.start()
        loads.append(copy)
    waited = [0]

    def loaded(upto):
        while waited[0] < upto:
            loads[waited[0]].wait()
            waited[0] += 1

    def device(dlat, dlon):
        return {
            "lat": lax.rem(lat + dlat + nlat, nlat),
            "lon": lax.rem(lon + dlon + nlon, nlon),
        }

    onward = (device(1, 0), device(0, 1), device(1, 1))
    back = (device(-1, 0), device(0, -1), device(-1, -1))
    barrier = pltpu.get_barrier_semaphore()
    for target in onward + back:
        pl.semaphore_signal(
            barrier, inc=1, device_id=target, device_id_type=pl.DeviceIdType.MESH
        )

    (
        fields_b,
        cot_b,
        cot_f,
        gskip,
        planes,
        m_xhat,
        m_rstd,
        merged,
        e_xhat,
        e_rstd,
        dexp,
        home,
        mask_ref,
        sums,
        sent,
        received,
    ) = spaces["misc"]

    shape = (2 * PAD, PAD)
    q = lax.broadcasted_iota(jnp.int32, shape, 0)
    q = jnp.where(q >= PAD, q - PAD, q)
    k = lax.broadcasted_iota(jnp.int32, shape, 1)
    there = jnp.where(k < CELLS, 1, 0)
    apart = jnp.where((q < CELLS // 2) == (k < CELLS // 2), 0, 1)
    first = jnp.where(lat == 0, 1, 0)
    mask_ref[0] = (there * (1 - apart * first)).astype(F32)
    mask_ref[1] = there.astype(F32)
    sums[...] = head_sums()

    started = []

    def send(t, source, pick, targets):
        sent[t] = mm(pick[...], source[...]).astype(BF16)
        for n, (start, size) in enumerate(PIECES):
            copy = pltpu.make_async_remote_copy(
                src_ref=sent.at[t, pl.ds(start, size)],
                dst_ref=received.at[t, pl.ds(start, size)],
                send_sem=send_sem.at[t, n],
                recv_sem=recv_sem.at[t, n],
                device_id=targets[n],
                device_id_type=pl.DeviceIdType.MESH,
            )
            copy.start()
            started.append(copy)

    def arrive(t):
        for copy in started[3 * t : 3 * t + 3]:
            copy.wait_recv()

    def rows_loop(body, count=4):
        def step(g, carry):
            body(g)
            return carry

        lax.fori_loop(0, count, step, 0)

    def flat(ref, to):
        for n in range(4):
            part = ref[pl.ds(n, HOME, stride=4), :]
            to[:, pl.ds(128 * n, 128)] = part.astype(BF16)

    def unflat(ref, frm):
        for n in range(4):
            ref[pl.ds(n, HOME, stride=4), :] = frm[:, 128 * n : 128 * (n + 1)]

    encoder = Block(
        BODY, D, enc_gain, weights[0], weights[1], weights[2], enc_scale, spaces["enc"], sums
    )
    coarse = Block(
        PAD, DC, crs_gain, weights[4], weights[5], weights[6], crs_scale, spaces["crs"], sums
    )
    decoder = Block(
        BODY, D, dec_gain, weights[8], weights[9], weights[10], dec_scale, spaces["dec"], sums
    )
    merge_w, expand_w = weights[3], weights[7]
    fn, fmixed, fduq, fduk, fdqkv, fdn, fx, fb = spaces["fine"]
    cn, cmixed, cduq, cduk, cdqkv, cdn, cx, cb = spaces["coarse"]

    loaded(2)
    flat(fields_v, fields_b)
    pl.semaphore_wait(barrier, 6)
    send(0, fields_b, moves[0], onward)
    loaded(5)
    flat(cot_v, cot_b)
    send(1, cot_b, moves[0], onward)

    def own_fields(g):
        fx[at_rows(g), :] = mm(moves[1][at_rows(g), :], fields_b[...])
        cot_f[at_rows(g), :] = mm(moves[1][at_rows(g), :], cot_b[...])

    rows_loop(own_fields)
    loaded(11)
    arrive(0)

    def enter_encoder(g):
        x = fx[at_rows(g), :] + mm(moves[2][at_rows(g), :], received[0])
        fx[at_rows(g), :] = x
        encoder.norm_rows(g, x, fn)

    rows_loop(enter_encoder)
    encoder.project(fn)
    encoder.attend(mask_ref, fmixed)

    def add_encoder(at, branch):
        x = fx[:, at] + branch
        fx[:, at] = x
        fb[:, at] = x.astype(BF16)

    encoder.outward(fmixed, add_encoder)

    send(2, fb, moves[6], onward)

    def own_section(g):
        planes[at_rows(g), :] = mm(moves[7][at_rows(g), :], fb[...])

    rows_loop(own_section)
    loaded(len(loads))
    arrive(2)
    total = jnp.zeros((PAD, D), F32)
    for p in range(4):
        x = planes[at_rows(p), :] + mm(moves[8][at_rows(p), :], received[2])
        planes[at_rows(p), :] = x
        total += x
    mean = jnp.sum(total, axis=-1, keepdims=True) * (1.0 / (4 * D))
    total = jnp.zeros((PAD, D), F32)
    for p in range(4):
        centred = planes[at_rows(p), :] - mean
        total += centred * centred
    rstd = lax.rsqrt(jnp.sum(total, axis=-1, keepdims=True) * (1.0 / (4 * D)) + EPS)
    m_rstd[...] = jnp.broadcast_to(rstd, (PAD, 128))
    for p in range(4):
        lanes = at_lanes(p, D)
        xhat = (planes[at_rows(p), :] - mean) * rstd
        m_xhat[:, lanes] = xhat
        merged[:, lanes] = (xhat * merge_gain[:, lanes]).astype(BF16)

    def merge_body(j):
        at = at_lanes(j, 256)
        cx[:, at] = mm(merged[...], merge_w[:, at])

    rows_loop(merge_body)
    coarse.norm_rows(0, cx[...], cn)
    coarse.project(cn)
    coarse.attend(mask_ref, cmixed)

    def add_coarse(at, branch):
        cx[:, at] = cx[:, at] + branch

    coarse.outward(cmixed, add_coarse)

    x = cx[...]
    centred = x - row_mean(x)
    rstd = lax.rsqrt(row_mean(centred * centred) + EPS)
    xhat = centred * rstd
    e_xhat[...] = xhat
    e_rstd[...] = jnp.broadcast_to(rstd, (PAD, 128))
    cb[...] = (xhat * exp_gain[...]).astype(BF16)

    def expand_body(p):
        fb[at_rows(p), :] = mm(cb[...], expand_w[:, at_lanes(p, D)]).astype(BF16)

    rows_loop(expand_body)

    send(3, fb, moves[9], back)

    def own_expanded(g):
        fx[at_rows(g), :] = fx[at_rows(g), :] + mm(moves[10][at_rows(g), :], fb[...])

    rows_loop(own_expanded)
    arrive(3)

    def enter_decoder(g):
        x = fx[at_rows(g), :] + mm(moves[11][at_rows(g), :], received[3])
        fx[at_rows(g), :] = x
        decoder.norm_rows(g, x, fn)

    rows_loop(enter_decoder)
    decoder.project(fn)
    decoder.attend(mask_ref, fmixed)

    def add_decoder(at, branch):
        fb[:, at] = (fx[:, at] + branch).astype(BF16)

    decoder.outward(fmixed, add_decoder)

    send(4, fb, moves[3], back)
    home[...] = mm(moves[4][...], fb[...])

    arrive(1)

    def enter_gradient(g):
        x = cot_f[at_rows(g), :] + mm(moves[2][at_rows(g), :], received[1])
        cot_f[at_rows(g), :] = x
        fb[at_rows(g), :] = x.astype(BF16)

    rows_loop(enter_gradient)
    decoder.backward(fb, fn, fduq, fduk, fdqkv, fdn)

    def leave_decoder(g):
        x = cot_f[at_rows(g), :] + decoder.norm_backward(g, fdn[at_rows(g), :])
        gskip[at_rows(g), :] = x
        fb[at_rows(g), :] = x.astype(BF16)

    rows_loop(leave_decoder)

    send(5, fb, moves[6], onward)
    rows_loop(own_section)
    arrive(4)
    unflat(out_ref, home[...] + mm(moves[5][...], received[4]))
    arrive(5)
    for p in range(4):
        x = planes[at_rows(p), :] + mm(moves[8][at_rows(p), :], received[5])
        dexp[:, at_lanes(p, D)] = x.astype(BF16)

    def expand_back(j):
        at = at_lanes(j, 256)
        cdn[:, at] = mm_nt(dexp[...], expand_w[at, :])

    rows_loop(expand_back)
    dy = cdn[...] * exp_gain[...]
    xhat = e_xhat[...]
    x = e_rstd[:, :1] * (dy - row_mean(dy) - xhat * row_mean(dy * xhat))
    cx[...] = x
    cb[...] = x.astype(BF16)
    coarse.backward(cb, cn, cduq, cduk, cdqkv, cdn)
    cb[...] = (cx[...] + coarse.norm_backward(0, cdn[...])).astype(BF16)

    def merge_back(p):
        planes[at_rows(p), :] = mm_nt(cb[...], merge_w[at_rows(p, D), :])

    rows_loop(merge_back)
    total = jnp.zeros((PAD, D), F32)
    weighed = jnp.zeros((PAD, D), F32)
    for p in range(4):
        lanes = at_lanes(p, D)
        dy = planes[at_rows(p), :] * merge_gain[:, lanes]
        total += dy
        weighed += dy * m_xhat[:, lanes]
    mean = jnp.sum(total, axis=-1, keepdims=True) * (1.0 / (4 * D))
    tilt = jnp.sum(weighed, axis=-1, keepdims=True) * (1.0 / (4 * D))
    rstd = m_rstd[:, :1]
    for p in range(4):
        lanes = at_lanes(p, D)
        dy = planes[at_rows(p), :] * merge_gain[:, lanes]
        fb[at_rows(p), :] = (rstd * (dy - mean - m_xhat[:, lanes] * tilt)).astype(BF16)

    send(6, fb, moves[9], back)

    def own_gradient(g):
        gskip[at_rows(g), :] = gskip[at_rows(g), :] + mm(moves[10][at_rows(g), :], fb[...])

    rows_loop(own_gradient)
    arrive(6)

    def enter_encoder_gradient(g):
        x = gskip[at_rows(g), :] + mm(moves[11][at_rows(g), :], received[6])
        gskip[at_rows(g), :] = x
        fb[at_rows(g), :] = x.astype(BF16)

    rows_loop(enter_encoder_gradient)
    encoder.backward(fb, fn, fduq, fduk, fdqkv, fdn)

    def leave_encoder(g):
        x = gskip[at_rows(g), :] + encoder.norm_backward(g, fdn[at_rows(g), :])
        fb[at_rows(g), :] = x.astype(BF16)

    rows_loop(leave_encoder)

    send(7, fb, moves[3], back)
    home[...] = mm(moves[4][...], fb[...])
    arrive(7)
    unflat(grad_ref, home[...] + mm(moves[5][...], received[7]))
    for copy in started:
        copy.wait_send()


def shards(
    fields,
    cotangent,
    encoder_gain,
    encoder_query,
    encoder_keyval,
    encoder_output,
    encoder_scale,
    merge_gain,
    merge_weight,
    coarse_gain,
    coarse_query,
    coarse_keyval,
    coarse_output,
    coarse_scale,
    expand_gain,
    expand_weight,
    decoder_gain,
    decoder_query,
    decoder_keyval,
    decoder_output,
    decoder_scale,
):
    shape = fields.shape
    weights = (
        encoder_query,
        encoder_keyval,
        encoder_output,
        merge_weight,
        coarse_query,
        coarse_keyval,
        coarse_output,
        expand_weight,
        decoder_query,
        decoder_keyval,
        decoder_output,
    )
    moves = [jnp.asarray(m) for m in all_moves()]
    gains = [
        g.reshape(1, -1)
        for g in (encoder_gain, merge_gain, coarse_gain, expand_gain, decoder_gain)
    ]
    scales = (encoder_scale, coarse_scale, decoder_scale)
    flat = (HOME * 4, 128)
    anywhere = pl.BlockSpec(memory_space=pl.ANY)
    in_vmem = pl.BlockSpec(memory_space=pltpu.VMEM)
    in_smem = pl.BlockSpec(memory_space=pltpu.SMEM)
    scratch = [pltpu.VMEM(flat, F32)] * 2
    scratch += [pltpu.VMEM(w.shape, BF16) for w in weights]
    scratch += [pltpu.VMEM(m.shape, BF16) for m in moves]
    for name in NAMES:
        scratch += [pltpu.VMEM(s, t) for s, t in TABLE[name]]
    scratch += [
        pltpu.SemaphoreType.DMA((2 + len(weights) + len(moves),)),
        pltpu.SemaphoreType.DMA((8, 3)),
        pltpu.SemaphoreType.DMA((8, 3)),
    ]
    output, grad = pl.pallas_call(
        kernel,
        out_shape=(jax.ShapeDtypeStruct(flat, F32),) * 2,
        in_specs=[anywhere] * (2 + len(weights) + len(moves)) + [in_vmem] * 5 + [in_smem] * 3,
        out_specs=(in_vmem, in_vmem),
        scratch_shapes=scratch,
        compiler_params=pltpu.CompilerParams(
            collective_id=0, has_side_effects=True, vmem_limit_bytes=60 * 1024 * 1024
        ),
    )(
        fields.reshape(flat),
        cotangent.reshape(flat),
        *weights,
        *moves,
        *gains,
        *scales,
    )
    return (output.reshape(shape), grad.reshape(shape))


def solution(mesh):
    along = P("lat", "lon", None, None)
    return jax.shard_map(
        shards,
        mesh=mesh,
        in_specs=(along, along) + (P(),) * 19,
        out_specs=(along, along),
        check_vma=False,
    )
```

```python
import functools

import jax
import jax.numpy as jnp
import numpy as np
from jax import lax
from jax.experimental import pallas as pl
from jax.experimental.pallas import tpu as pltpu
from jax.sharding import PartitionSpec as P

WLAT = 6
WLON = 12
EPS = 1e-05
ROWS, COLS = 12, 24
HOME = ROWS * COLS
PAD = 80
BODY = 4 * PAD
CELLS = WLAT * WLON
PIECES = ((0, 64), (64, 64), (128, 32))
SENT = 160
D = 512
DC = 1024
F32 = jnp.float32
BF16 = jnp.bfloat16
LOG2E = 1.4426950408889634


def fine_order(r, c):
    return PAD * (2 * (r // WLAT) + c // WLON) + (r % WLAT) * WLON + c % WLON


def plane_order(r, c):
    return PAD * (2 * (r % 2) + c % 2) + (r // 2) * WLON + c // 2


def home_order(r, c):
    return r * COLS + c


def piece_row(r, c):
    if r >= 9 and c < 18:
        return (r - 9) * 18 + c
    if r < 9 and c >= 18:
        return 64 + r * 6 + (c - 18)
    if r >= 9 and c >= 18:
        return 128 + (r - 9) * 6 + (c - 18)
    return None


def move_matrices(order_a, rows_a, order_b, rows_b):
    pick = np.zeros((SENT, rows_a), np.float32)
    own = np.zeros((rows_b, rows_a), np.float32)
    place = np.zeros((rows_b, SENT), np.float32)
    for r in range(ROWS):
        for c in range(COLS):
            piece = piece_row(r, c)
            if piece is not None:
                pick[piece, order_a(r, c)] = 1
            ra, ca = (r - 3) % ROWS, (c - 6) % COLS
            if r >= 3 and c >= 6:
                own[order_b(r, c), order_a(ra, ca)] = 1
            else:
                place[order_b(r, c), piece_row(ra, ca)] = 1
    return pick, own, place


def all_moves():
    first = move_matrices(home_order, HOME, fine_order, BODY)
    second = move_matrices(fine_order, BODY, plane_order, BODY)
    pick, own, place = first
    moves = [pick, own, place, place.T, own.T, pick.T]
    pick, own, place = second
    moves += [pick, own, place, place.T, own.T, pick.T]
    return [np.ascontiguousarray(m).astype(jnp.bfloat16) for m in moves]


def mm(a, b):
    return lax.dot_general(a, b, (((1,), (0,)), ((), ())), preferred_element_type=F32)


def mm_nt(a, b):
    return lax.dot_general(a, b, (((1,), (1,)), ((), ())), preferred_element_type=F32)


def mm_tn(a, b):
    return lax.dot_general(a, b, (((0,), (0,)), ((), ())), preferred_element_type=F32)


def row_mean(x):
    return jnp.mean(x, axis=-1, keepdims=True)


def at_rows(g, n=PAD):
    if isinstance(g, int):
        return pl.ds(g * n, n)
    return pl.ds(pl.multiple_of(g * n, n), n)


def at_lanes(j, n):
    if isinstance(j, int):
        return pl.ds(j * n, n)
    return pl.ds(pl.multiple_of(j * n, n), n)


def head_sums():
    shape = (256, 256)
    a = lax.broadcasted_iota(jnp.int32, shape, 0) // 64
    b = lax.broadcasted_iota(jnp.int32, shape, 1) // 64
    return jnp.where(a == b, 1.0, 0.0).astype(BF16)


def pair_masks():
    lane = lax.broadcasted_iota(jnp.int32, (PAD, 128), 1)
    return lane < 64


def stack_pair(x, low):
    zero = jnp.zeros_like(x)
    return jnp.concatenate([jnp.where(low, x, zero), jnp.where(low, zero, x)], axis=0)


def pick_pair(x, low):
    return jnp.where(low, x[:PAD], x[PAD:])


def beside(a, b):
    return jnp.concatenate([a, b], axis=1)


def bar_queries(first):
    shape = (2 * PAD, 128)
    q = lax.broadcasted_iota(jnp.int32, shape, 0)
    q = jnp.where(q >= PAD, q - PAD, q)
    lane = lax.broadcasted_iota(jnp.int32, shape, 1)
    upper = jnp.where(q < CELLS // 2, first, 0)
    lower = jnp.where(q < CELLS // 2, 0, first)
    value = jnp.where(lane == 0, upper, jnp.where(lane == 1, lower, 0))
    return jnp.where(lane == 2, 1, value).astype(F32).astype(BF16)


def bar_keys():
    shape = (PAD, 128)
    k = lax.broadcasted_iota(jnp.int32, shape, 0)
    lane = lax.broadcasted_iota(jnp.int32, shape, 1)
    upper = jnp.where(k < CELLS // 2, 1, 0)
    there = jnp.where(k < CELLS, 1, 0)
    value = jnp.where(lane == 0, there - upper, jnp.where(lane == 1, upper, 0))
    value = jnp.where(lane == 2, 1 - there, value)
    return (value * -1024).astype(F32).astype(BF16)


class Block:
    def __init__(self, rows, channels, gain, wq, wkv, wo, scale, kept, sums):
        self.rows, self.channels = rows, channels
        self.gain, self.wq, self.wkv, self.wo, self.scale = gain, wq, wkv, wo, scale
        self.xhat, self.rstd, self.uq, self.uk, self.rq, self.rk = kept[:6]
        self.v, self.weights, self.inverse, self.mixed = kept[6:]
        self.sums = sums
        pairs = channels // 128
        self.units = [(g, p) for g in range(rows // PAD) for p in range(pairs)]

    def chunks(self):
        return [pl.ds(at, 512) for at in range(0, self.channels, 512)]

    def tiles(self, ref):
        return [ref[at_rows(g), at_lanes(p, 128)] for g, p in self.units]

    def norm_rows(self, g, x, n_ref):
        centred = x - row_mean(x)
        rstd = lax.rsqrt(row_mean(centred * centred) + EPS)
        xhat = centred * rstd
        self.xhat[at_rows(g), :] = xhat
        self.rstd[at_rows(g), :] = jnp.broadcast_to(rstd, (PAD, 128))
        n_ref[at_rows(g), :] = (xhat * self.gain[...]).astype(BF16)

    def head_total(self, x):
        sums = self.sums[...]
        return beside(mm(x[:, :256], sums), mm(x[:, 256:], sums))

    def project(self, n_ref):
        def unit(weight, at, u_ref, r_ref):
            raw = mm(n_ref[...], weight[:, at]).astype(BF16).astype(F32)
            r = lax.rsqrt(self.head_total((raw * raw).astype(BF16)) + 1.0)
            r_ref[:, at] = r
            u_ref[:, at] = (raw * r).astype(BF16)

        for at in self.chunks():
            unit(self.wq, at, self.uq, self.rq)
            unit(self.wkv, at, self.uk, self.rk)
            behind = pl.ds(at.start + self.channels, 512)
            self.v[:, at] = mm(n_ref[...], self.wkv[:, behind]).astype(BF16)

    def scales(self, p, factor):
        top = lax.broadcasted_iota(jnp.int32, (2 * PAD, 1), 0) < PAD
        return jnp.where(top, self.scale[2 * p] * factor, self.scale[2 * p + 1] * factor)

    def attend(self, barred, bar_key):
        low = pair_masks()
        ones = jnp.ones((PAD, 128), BF16)
        queries = [stack_pair(q, low) for q in self.tiles(self.uq)]
        keys, values = self.tiles(self.uk), self.tiles(self.v)
        scores = [
            mm_nt(beside(q, barred(g)), beside(k, bar_key))
            for q, k, (g, p) in zip(queries, keys, self.units)
        ]
        weights = [
            jnp.exp2(s * self.scales(p, LOG2E)).astype(BF16)
            for s, (g, p) in zip(scores, self.units)
        ]
        both = [mm(w, beside(v, ones)) for w, v in zip(weights, values)]
        for n, (g, p) in enumerate(self.units):
            at = (at_rows(g), at_lanes(p, 128))
            self.weights[n] = weights[n]
            inverse = 1.0 / pick_pair(both[n][:, 128:], low)
            self.inverse[at] = inverse
            self.mixed[at] = (pick_pair(both[n][:, :128], low) * inverse).astype(BF16)

    def mixed_back(self, grad_ref, dmixed_ref):
        for at in self.chunks():
            dmixed_ref[:, at] = mm_nt(grad_ref[...], self.wo[at, :]).astype(BF16)

    def attend_back(self, dmixed_ref, duq_ref, duk_ref, dqkv_ref):
        low = pair_masks()
        ones = jnp.ones((PAD, 128), BF16)
        divided = [
            d.astype(F32) * i for d, i in zip(self.tiles(dmixed_ref), self.tiles(self.inverse))
        ]
        shift = [
            stack_pair((-(d * m.astype(F32))).astype(BF16), low)
            for d, m in zip(divided, self.tiles(self.mixed))
        ]
        douts = [stack_pair(d.astype(BF16), low) for d in divided]
        queries = [stack_pair(q, low) for q in self.tiles(self.uq)]
        keys, values = self.tiles(self.uk), self.tiles(self.v)
        weights = [self.weights[n] for n in range(len(self.units))]
        dprobs = [
            mm_nt(beside(d, s), beside(v, ones)) for d, s, v in zip(douts, shift, values)
        ]
        dscores = [
            (w.astype(F32) * (d * self.scales(p, 1.0))).astype(BF16)
            for w, d, (g, p) in zip(weights, dprobs, self.units)
        ]
        dvalues = [mm_tn(w, d) for w, d in zip(weights, douts)]
        dkeys = [mm_tn(d, q) for d, q in zip(dscores, queries)]
        dqueries = [mm(d, k) for d, k in zip(dscores, keys)]
        for n, (g, p) in enumerate(self.units):
            at = (at_rows(g), at_lanes(p, 128))
            behind = at_lanes(p + 2 * (self.channels // 128), 128)
            dqkv_ref[at_rows(g), behind] = dvalues[n].astype(BF16)
            duk_ref[at] = dkeys[n].astype(BF16)
            duq_ref[at] = pick_pair(dqueries[n], low).astype(BF16)

    def project_back(self, duq_ref, duk_ref, dqkv_ref, dn_ref):
        channels = self.channels
        for at in self.chunks():
            shifted = pl.ds(at.start + channels, 512)
            for u_ref, r_ref, du_ref, to in (
                (self.uq, self.rq, duq_ref, at),
                (self.uk, self.rk, duk_ref, shifted),
            ):
                u = u_ref[:, at].astype(F32)
                du = du_ref[:, at].astype(F32)
                inner = self.head_total((u * du).astype(BF16))
                dqkv_ref[:, to] = (r_ref[:, at] * (du - u * inner)).astype(BF16)
        for at in self.chunks():
            dn_ref[:, at] = mm_nt(dqkv_ref[:, :channels], self.wq[at, :]) + mm_nt(
                dqkv_ref[:, channels:], self.wkv[at, :]
            )

    def norm_backward(self, g, dn):
        dy = dn * self.gain[...]
        xhat = self.xhat[at_rows(g), :]
        rstd = self.rstd[at_rows(g), :][:, :1]
        return rstd * (dy - row_mean(dy) - xhat * row_mean(dy * xhat))


WEIGHTS = (
    "encoder_query",
    "encoder_keyval",
    "encoder_output",
    "merge_weight",
    "coarse_query",
    "coarse_keyval",
    "coarse_output",
    "expand_weight",
    "decoder_query",
    "decoder_keyval",
    "decoder_output",
)


def kept_shapes(rows, channels):
    units = rows // PAD * (channels // 128)
    return [
        ((rows, channels), F32),
        ((rows, 128), F32),
        ((rows, channels), BF16),
        ((rows, channels), BF16),
        ((rows, channels), F32),
        ((rows, channels), F32),
        ((rows, channels), BF16),
        ((units, 2 * PAD, PAD), BF16),
        ((rows, channels), F32),
        ((rows, channels), BF16),
    ]


def scratch_table():
    table = {}
    for block, rows, channels in (("enc", BODY, D), ("dec", BODY, D), ("crs", PAD, DC)):
        table[block] = kept_shapes(rows, channels)
    for kind, rows, channels in (("fine", BODY, D), ("coarse", PAD, DC)):
        table[kind] = [
            ((rows, channels), BF16),
            ((rows, channels), BF16),
            ((rows, channels), BF16),
            ((rows, channels), BF16),
            ((rows, 3 * channels), BF16),
            ((rows, channels), F32),
            ((rows, channels), F32),
            ((rows, channels), BF16),
        ]
    table["misc"] = [
        ((HOME, D), BF16),
        ((HOME, D), BF16),
        ((HOME, D), BF16),
        ((HOME, D), BF16),
        ((BODY, D), F32),
        ((BODY, D), F32),
        ((BODY, D), F32),
        ((PAD, 4 * D), F32),
        ((PAD, 128), F32),
        ((PAD, 4 * D), BF16),
        ((PAD, DC), F32),
        ((PAD, 128), F32),
        ((PAD, 4 * D), BF16),
        ((BODY, D), BF16),
        ((HOME, D), F32),
        ((HOME, D), F32),
        ((HOME * 4, 128), F32),
        ((HOME * 4, 128), BF16),
        ((HOME * 4, 128), BF16),
        ((2, 2 * PAD, 128), BF16),
        ((PAD, 128), BF16),
        ((256, 256), BF16),
        ((8, SENT, D), BF16),
        ((8, SENT, D), BF16),
    ]
    return table


TABLE = scratch_table()
NAMES = tuple(TABLE)


def kernel(*refs):
    refs = list(refs)

    def take(n):
        head = refs[:n]
        del refs[:n]
        return head

    fields_in, cot_in = take(2)
    weights_in = take(len(WEIGHTS))
    moves_in = take(12)
    enc_gain, merge_gain, crs_gain, exp_gain, dec_gain = take(5)
    enc_scale, crs_scale, dec_scale = take(3)
    out_hbm, grad_hbm = take(2)
    fields_v, cot_v = take(2)
    weights = take(len(WEIGHTS))
    moves = take(12)
    spaces = {name: take(len(TABLE[name])) for name in NAMES}
    local_sem, out_sem, send_sem, recv_sem = take(4)

    lat, lon = lax.axis_index("lat"), lax.axis_index("lon")
    nlat, nlon = lax.axis_size("lat"), lax.axis_size("lon")

    loads = []
    waited = [0]

    def load(*pairs):
        for src, dst in pairs:
            copy = pltpu.make_async_copy(src, dst, local_sem.at[len(loads)])
            copy.start()
            loads.append(copy)

    def loaded(upto):
        while waited[0] < upto:
            loads[waited[0]].wait()
            waited[0] += 1

    def weight(*which):
        return [(weights_in[n], weights[n]) for n in which]

    def move(*which):
        return [(moves_in[n], moves[n]) for n in which]

    load((fields_in, fields_v), *move(0))

    def device(dlat, dlon):
        return {
            "lat": lax.rem(lat + dlat + nlat, nlat),
            "lon": lax.rem(lon + dlon + nlon, nlon),
        }

    onward = (device(1, 0), device(0, 1), device(1, 1))
    back = (device(-1, 0), device(0, -1), device(-1, -1))
    barrier = pltpu.get_barrier_semaphore()
    for target in onward + back:
        pl.semaphore_signal(
            barrier, inc=1, device_id=target, device_id_type=pl.DeviceIdType.MESH
        )

    (
        fields_b,
        fields_rest,
        cot_b,
        cot_rest,
        cot_f,
        gskip,
        planes,
        m_xhat,
        m_rstd,
        merged,
        e_xhat,
        e_rstd,
        dexp,
        out_b,
        out_home,
        grad_home,
        by_cell,
        out_cells,
        grad_cells,
        bar_q,
        bar_k,
        sums,
        sent,
        received,
    ) = spaces["misc"]

    bar_q[0] = bar_queries(jnp.where(lat == 0, 1, 0))
    bar_q[1] = bar_queries(0)
    bar_k[...] = bar_keys()
    sums[...] = head_sums()

    started = {}

    def prepare(t, source, pick):
        sent[t] = mm(pick[...], source[...]).astype(BF16)

    def launch(t, targets):
        started[t] = []
        for n, (start, size) in enumerate(PIECES):
            copy = pltpu.make_async_remote_copy(
                src_ref=sent.at[t, pl.ds(start, size)],
                dst_ref=received.at[t, pl.ds(start, size)],
                send_sem=send_sem.at[t, n],
                recv_sem=recv_sem.at[t, n],
                device_id=targets[n],
                device_id_type=pl.DeviceIdType.MESH,
            )
            copy.start()
            started[t].append(copy)

    def arrive(t):
        for copy in started[t]:
            copy.wait_recv()

    def by_rows(body):
        for g in range(4):
            body(g, at_rows(g))

    def flat(ref, to, rest):
        for n in range(4):
            part = ref[pl.ds(n, HOME, stride=4), :]
            rounded = part.astype(BF16)
            to[:, at_lanes(n, 128)] = rounded
            rest[:, at_lanes(n, 128)] = (part - rounded.astype(F32)).astype(BF16)

    outs = []

    def deliver(x, cells, ref):
        for n in range(4):
            by_cell[pl.ds(n, HOME, stride=4), :] = x[:, 128 * n : 128 * (n + 1)]
        cells[...] = by_cell[...].astype(BF16)
        copy = pltpu.make_async_copy(cells, ref, out_sem.at[len(outs)])
        copy.start()
        outs.append(copy)

    encoder = Block(
        BODY, D, enc_gain, weights[0], weights[1], weights[2], enc_scale, spaces["enc"], sums
    )
    coarse = Block(
        PAD, DC, crs_gain, weights[4], weights[5], weights[6], crs_scale, spaces["crs"], sums
    )
    decoder = Block(
        BODY, D, dec_gain, weights[8], weights[9], weights[10], dec_scale, spaces["dec"], sums
    )
    merge_w, expand_w = weights[3], weights[7]
    fn, fdmixed, fduq, fduk, fdqkv, fdn, fx, fb = spaces["fine"]
    cn, cdmixed, cduq, cduk, cdqkv, cdn, cx, cb = spaces["coarse"]

    def fine_bar(g):
        return bar_q[g // 2]

    def coarse_bar(g):
        return bar_q[0]

    loaded(2)
    flat(fields_v, fields_b, fields_rest)
    prepare(0, fields_b, moves[0])
    pl.semaphore_wait(barrier, 6)
    launch(0, onward)
    load(*move(1), (cot_in, cot_v), *move(2), *weight(0, 1, 2))
    loaded(4)
    fx[...] = mm(moves[1][...], fields_b[...]) + mm(moves[1][...], fields_rest[...])
    flat(cot_v, cot_b, cot_rest)
    prepare(1, cot_b, moves[0])
    cot_f[...] = mm(moves[1][...], cot_b[...]) + mm(moves[1][...], cot_rest[...])
    loaded(8)
    arrive(0)
    launch(1, onward)
    load(*move(6, 7, 8), *weight(3, 4, 5, 6, 7), *move(9, 10, 11), *weight(8, 9, 10))
    load(*move(3, 4, 5))

    def enter_encoder(g, at):
        x = fx[at, :] + mm(moves[2][at, :], received[0])
        fx[at, :] = x
        encoder.norm_rows(g, x, fn)

    by_rows(enter_encoder)
    encoder.project(fn)
    encoder.attend(fine_bar, bar_k[...])
    section = fx[...] + mm(encoder.mixed[...], encoder.wo[...])
    fx[...] = section
    fb[...] = section.astype(BF16)

    loaded(11)
    prepare(2, fb, moves[6])
    launch(2, onward)
    planes[...] = mm(moves[7][...], fb[...])
    arrive(1)
    cot = cot_f[...] + mm(moves[2][...], received[1])
    cot_f[...] = cot
    out_b[...] = cot.astype(BF16)
    loaded(len(loads))
    decoder.mixed_back(out_b, fdmixed)
    arrive(2)
    total = jnp.zeros((PAD, D), F32)
    for p in range(4):
        x = planes[at_rows(p), :] + mm(moves[8][at_rows(p), :], received[2])
        planes[at_rows(p), :] = x
        total += x
    mean = jnp.sum(total, axis=-1, keepdims=True) * (1.0 / (4 * D))
    total = jnp.zeros((PAD, D), F32)
    for p in range(4):
        centred = planes[at_rows(p), :] - mean
        total += centred * centred
    rstd = lax.rsqrt(jnp.sum(total, axis=-1, keepdims=True) * (1.0 / (4 * D)) + EPS)
    m_rstd[...] = jnp.broadcast_to(rstd, (PAD, 128))
    for p in range(4):
        lanes = at_lanes(p, D)
        xhat = (planes[at_rows(p), :] - mean) * rstd
        m_xhat[:, lanes] = xhat
        merged[:, lanes] = (xhat * merge_gain[:, lanes]).astype(BF16)
    cx[...] = mm(merged[...], merge_w[...])
    coarse.norm_rows(0, cx[...], cn)
    coarse.project(cn)
    coarse.attend(coarse_bar, bar_k[...])
    x = cx[...] + mm(coarse.mixed[...], coarse.wo[...])
    centred = x - row_mean(x)
    rstd = lax.rsqrt(row_mean(centred * centred) + EPS)
    xhat = centred * rstd
    e_xhat[...] = xhat
    e_rstd[...] = jnp.broadcast_to(rstd, (PAD, 128))
    cb[...] = (xhat * exp_gain[...]).astype(BF16)
    for p in range(4):
        fb[at_rows(p), :] = mm(cb[...], expand_w[:, at_lanes(p, D)]).astype(BF16)

    prepare(3, fb, moves[9])
    launch(3, back)
    fx[...] = fx[...] + mm(moves[10][...], fb[...])
    arrive(3)

    def enter_decoder(g, at):
        x = fx[at, :] + mm(moves[11][at, :], received[3])
        fx[at, :] = x
        decoder.norm_rows(g, x, fn)

    by_rows(enter_decoder)
    decoder.project(fn)
    decoder.attend(fine_bar, bar_k[...])
    out_b[...] = (fx[...] + mm(decoder.mixed[...], decoder.wo[...])).astype(BF16)

    decoder.attend_back(fdmixed, fduq, fduk, fdqkv)
    decoder.project_back(fduq, fduk, fdqkv, fdn)

    def leave_decoder(g, at):
        x = cot_f[at, :] + decoder.norm_backward(g, fdn[at, :])
        gskip[at, :] = x
        fb[at, :] = x.astype(BF16)

    by_rows(leave_decoder)

    prepare(5, fb, moves[6])
    launch(5, onward)
    planes[...] = mm(moves[7][...], fb[...])
    prepare(4, out_b, moves[3])
    out_home[...] = mm(moves[4][...], out_b[...])
    arrive(5)
    launch(4, back)
    for p in range(4):
        x = planes[at_rows(p), :] + mm(moves[8][at_rows(p), :], received[5])
        dexp[:, at_lanes(p, D)] = x.astype(BF16)
    dy = mm_nt(dexp[...], expand_w[...]) * exp_gain[...]
    xhat = e_xhat[...]
    x = e_rstd[:, :1] * (dy - row_mean(dy) - xhat * row_mean(dy * xhat))
    cx[...] = x
    cb[...] = x.astype(BF16)
    coarse.mixed_back(cb, cdmixed)
    coarse.attend_back(cdmixed, cduq, cduk, cdqkv)
    coarse.project_back(cduq, cduk, cdqkv, cdn)
    cb[...] = (cx[...] + coarse.norm_backward(0, cdn[...])).astype(BF16)
    for p in range(4):
        planes[at_rows(p), :] = mm_nt(cb[...], merge_w[at_rows(p, D), :])
    total = jnp.zeros((PAD, D), F32)
    weighed = jnp.zeros((PAD, D), F32)
    for p in range(4):
        lanes = at_lanes(p, D)
        dy = planes[at_rows(p), :] * merge_gain[:, lanes]
        total += dy
        weighed += dy * m_xhat[:, lanes]
    mean = jnp.sum(total, axis=-1, keepdims=True) * (1.0 / (4 * D))
    tilt = jnp.sum(weighed, axis=-1, keepdims=True) * (1.0 / (4 * D))
    rstd = m_rstd[:, :1]
    for p in range(4):
        lanes = at_lanes(p, D)
        dy = planes[at_rows(p), :] * merge_gain[:, lanes]
        fb[at_rows(p), :] = (rstd * (dy - mean - m_xhat[:, lanes] * tilt)).astype(BF16)

    prepare(6, fb, moves[9])
    launch(6, back)
    gskip[...] = gskip[...] + mm(moves[10][...], fb[...])
    arrive(4)
    deliver(out_home[...] + mm(moves[5][...], received[4]), out_cells, out_hbm)
    arrive(6)
    x = gskip[...] + mm(moves[11][...], received[6])
    gskip[...] = x
    fb[...] = x.astype(BF16)
    encoder.mixed_back(fb, fdmixed)
    encoder.attend_back(fdmixed, fduq, fduk, fdqkv)
    encoder.project_back(fduq, fduk, fdqkv, fdn)

    def leave_encoder(g, at):
        x = gskip[at, :] + encoder.norm_backward(g, fdn[at, :])
        fb[at, :] = x.astype(BF16)

    by_rows(leave_encoder)

    prepare(7, fb, moves[3])
    launch(7, back)
    grad_home[...] = mm(moves[4][...], fb[...])
    arrive(7)
    deliver(grad_home[...] + mm(moves[5][...], received[7]), grad_cells, grad_hbm)
    for t in started:
        for copy in started[t]:
            copy.wait_send()
    for copy in outs:
        copy.wait()


def shards(
    fields,
    cotangent,
    encoder_gain,
    encoder_query,
    encoder_keyval,
    encoder_output,
    encoder_scale,
    merge_gain,
    merge_weight,
    coarse_gain,
    coarse_query,
    coarse_keyval,
    coarse_output,
    coarse_scale,
    expand_gain,
    expand_weight,
    decoder_gain,
    decoder_query,
    decoder_keyval,
    decoder_output,
    decoder_scale,
):
    shape = fields.shape
    weights = (
        encoder_query,
        encoder_keyval,
        encoder_output,
        merge_weight,
        coarse_query,
        coarse_keyval,
        coarse_output,
        expand_weight,
        decoder_query,
        decoder_keyval,
        decoder_output,
    )
    moves = [jnp.asarray(m) for m in all_moves()]
    gains = [
        g.reshape(1, -1)
        for g in (encoder_gain, merge_gain, coarse_gain, expand_gain, decoder_gain)
    ]
    scales = (encoder_scale, coarse_scale, decoder_scale)
    flat = (HOME * 4, 128)
    anywhere = pl.BlockSpec(memory_space=pl.ANY)
    in_vmem = pl.BlockSpec(memory_space=pltpu.VMEM)
    in_smem = pl.BlockSpec(memory_space=pltpu.SMEM)
    scratch = [pltpu.VMEM(flat, F32)] * 2
    scratch += [pltpu.VMEM(w.shape, BF16) for w in weights]
    scratch += [pltpu.VMEM(m.shape, BF16) for m in moves]
    for name in NAMES:
        scratch += [pltpu.VMEM(s, t) for s, t in TABLE[name]]
    scratch += [
        pltpu.SemaphoreType.DMA((2 + len(weights) + len(moves),)),
        pltpu.SemaphoreType.DMA((2,)),
        pltpu.SemaphoreType.DMA((8, 3)),
        pltpu.SemaphoreType.DMA((8, 3)),
    ]
    output, grad = pl.pallas_call(
        kernel,
        out_shape=(jax.ShapeDtypeStruct(flat, BF16),) * 2,
        in_specs=[anywhere] * (2 + len(weights) + len(moves)) + [in_vmem] * 5 + [in_smem] * 3,
        out_specs=(anywhere, anywhere),
        scratch_shapes=scratch,
        compiler_params=pltpu.CompilerParams(
            collective_id=0, has_side_effects=True, vmem_limit_bytes=60 * 1024 * 1024
        ),
    )(
        fields.reshape(flat),
        cotangent.reshape(flat),
        *weights,
        *moves,
        *gains,
        *scales,
    )
    return (output.astype(F32).reshape(shape), grad.astype(F32).reshape(shape))


def solution(mesh):
    along = P("lat", "lon", None, None)
    return jax.shard_map(
        shards,
        mesh=mesh,
        in_specs=(along, along) + (P(),) * 19,
        out_specs=(along, along),
        check_vma=False,
    )
```

```python
import functools

import jax
import jax.numpy as jnp
import numpy as np
from jax import lax
from jax.experimental import pallas as pl
from jax.experimental.pallas import tpu as pltpu
from jax.sharding import PartitionSpec as P

WLAT = 6
WLON = 12
EPS = 1e-05
ROWS, COLS = 12, 24
HOME = ROWS * COLS
PAD = 80
BODY = 4 * PAD
CELLS = WLAT * WLON
PIECES = ((0, 64), (64, 64), (128, 32))
SENT = 160
D = 512
DC = 1024
F32 = jnp.float32
BF16 = jnp.bfloat16
LOG2E = 1.4426950408889634


def fine_order(r, c):
    return PAD * (2 * (r // WLAT) + c // WLON) + (r % WLAT) * WLON + c % WLON


def plane_order(r, c):
    return PAD * (2 * (r % 2) + c % 2) + (r // 2) * WLON + c // 2


def home_order(r, c):
    return r * COLS + c


def piece_row(r, c):
    if r >= 9 and c < 18:
        return (r - 9) * 18 + c
    if r < 9 and c >= 18:
        return 64 + r * 6 + (c - 18)
    if r >= 9 and c >= 18:
        return 128 + (r - 9) * 6 + (c - 18)
    return None


def move_matrices(order_a, rows_a, order_b, rows_b):
    pick = np.zeros((SENT, rows_a), np.float32)
    own = np.zeros((rows_b, rows_a), np.float32)
    place = np.zeros((rows_b, SENT), np.float32)
    for r in range(ROWS):
        for c in range(COLS):
            piece = piece_row(r, c)
            if piece is not None:
                pick[piece, order_a(r, c)] = 1
            ra, ca = (r - 3) % ROWS, (c - 6) % COLS
            if r >= 3 and c >= 6:
                own[order_b(r, c), order_a(ra, ca)] = 1
            else:
                place[order_b(r, c), piece_row(ra, ca)] = 1
    return pick, own, place


def all_moves():
    first = move_matrices(home_order, HOME, fine_order, BODY)
    second = move_matrices(fine_order, BODY, plane_order, BODY)
    pick, own, place = first
    moves = [pick, own, place, place.T[:, : 3 * PAD], own.T, pick.T]
    pick, own, place = second
    moves += [pick[:, PAD:], own, place, place.T, own.T, pick.T]
    return [np.ascontiguousarray(m).astype(jnp.bfloat16) for m in moves]


def mm(a, b):
    return lax.dot_general(a, b, (((1,), (0,)), ((), ())), preferred_element_type=F32)


def mm_nt(a, b):
    return lax.dot_general(a, b, (((1,), (1,)), ((), ())), preferred_element_type=F32)


def mm_tn(a, b):
    return lax.dot_general(a, b, (((0,), (0,)), ((), ())), preferred_element_type=F32)


def row_mean(x):
    return jnp.mean(x, axis=-1, keepdims=True)


def at_rows(g, n=PAD):
    if isinstance(g, int):
        return pl.ds(g * n, n)
    return pl.ds(pl.multiple_of(g * n, n), n)


def at_lanes(j, n):
    if isinstance(j, int):
        return pl.ds(j * n, n)
    return pl.ds(pl.multiple_of(j * n, n), n)


def head_sums():
    shape = (256, 256)
    a = lax.broadcasted_iota(jnp.int32, shape, 0) // 64
    b = lax.broadcasted_iota(jnp.int32, shape, 1) // 64
    return jnp.where(a == b, 1.0, 0.0).astype(BF16)


def pair_masks():
    lane = lax.broadcasted_iota(jnp.int32, (PAD, 128), 1)
    return lane < 64


def stack_pair(x, low):
    zero = jnp.zeros_like(x)
    return jnp.concatenate([jnp.where(low, x, zero), jnp.where(low, zero, x)], axis=0)


def pick_pair(x, low):
    return jnp.where(low, x[:PAD], x[PAD:])


def beside(a, b):
    return jnp.concatenate([a, b], axis=1)


def bar_queries(first):
    shape = (2 * PAD, 128)
    q = lax.broadcasted_iota(jnp.int32, shape, 0)
    q = jnp.where(q >= PAD, q - PAD, q)
    lane = lax.broadcasted_iota(jnp.int32, shape, 1)
    upper = jnp.where(q < CELLS // 2, first, 0)
    lower = jnp.where(q < CELLS // 2, 0, first)
    value = jnp.where(lane == 0, upper, jnp.where(lane == 1, lower, 0))
    return jnp.where(lane == 2, 1, value).astype(F32).astype(BF16)


def bar_keys():
    shape = (PAD, 128)
    k = lax.broadcasted_iota(jnp.int32, shape, 0)
    lane = lax.broadcasted_iota(jnp.int32, shape, 1)
    upper = jnp.where(k < CELLS // 2, 1, 0)
    there = jnp.where(k < CELLS, 1, 0)
    value = jnp.where(lane == 0, there - upper, jnp.where(lane == 1, upper, 0))
    value = jnp.where(lane == 2, 1 - there, value)
    return (value * -1024).astype(F32).astype(BF16)


class Block:
    def __init__(self, rows, channels, gain, wq, wkv, wo, scale, kept, sums):
        self.rows, self.channels = rows, channels
        self.gain, self.wq, self.wkv, self.wo, self.scale = gain, wq, wkv, wo, scale
        self.xhat, self.rstd, self.uq, self.uk, self.rq, self.rk = kept[:6]
        self.v, self.weights, self.inverse, self.mixed = kept[6:]
        self.sums = sums
        self.pairs = channels // 128
        self.every = range(rows // PAD)

    def chunks(self):
        return [pl.ds(at, 512) for at in range(0, self.channels, 512)]

    def rows_of(self, windows):
        return pl.ds(PAD * windows.start, PAD * len(windows))

    def units(self, windows):
        return [(g, p) for g in windows for p in range(self.pairs)]

    def tiles(self, ref, units):
        return [ref[at_rows(g), at_lanes(p, 128)] for g, p in units]

    def norm_rows(self, g, x, n_ref):
        centred = x - row_mean(x)
        rstd = lax.rsqrt(row_mean(centred * centred) + EPS)
        xhat = centred * rstd
        self.xhat[at_rows(g), :] = xhat
        self.rstd[at_rows(g), :] = jnp.broadcast_to(rstd, (PAD, 128))
        n_ref[at_rows(g), :] = (xhat * self.gain[...]).astype(BF16)

    def head_total(self, x):
        sums = self.sums[...]
        return beside(mm(x[:, :256], sums), mm(x[:, 256:], sums))

    def project(self, windows, n_ref):
        rows = self.rows_of(windows)

        def unit(weight, at, u_ref, r_ref):
            raw = mm(n_ref[rows, :], weight[:, at]).astype(BF16).astype(F32)
            r = lax.rsqrt(self.head_total((raw * raw).astype(BF16)) + 1.0)
            r_ref[rows, at] = r
            u_ref[rows, at] = (raw * r).astype(BF16)

        for at in self.chunks():
            unit(self.wq, at, self.uq, self.rq)
            unit(self.wkv, at, self.uk, self.rk)
            behind = pl.ds(at.start + self.channels, 512)
            self.v[rows, at] = mm(n_ref[rows, :], self.wkv[:, behind]).astype(BF16)

    def scales(self, p, factor):
        top = lax.broadcasted_iota(jnp.int32, (2 * PAD, 1), 0) < PAD
        return jnp.where(top, self.scale[2 * p] * factor, self.scale[2 * p + 1] * factor)

    def attend(self, windows, barred, bar_key):
        low = pair_masks()
        ones = jnp.ones((PAD, 128), BF16)
        units = self.units(windows)
        queries = [stack_pair(q, low) for q in self.tiles(self.uq, units)]
        keys, values = self.tiles(self.uk, units), self.tiles(self.v, units)
        scores = [
            mm_nt(beside(q, barred(g)), beside(k, bar_key))
            for q, k, (g, p) in zip(queries, keys, units)
        ]
        weights = [
            jnp.exp2(s * self.scales(p, LOG2E)).astype(BF16)
            for s, (g, p) in zip(scores, units)
        ]
        both = [mm(w, beside(v, ones)) for w, v in zip(weights, values)]
        for n, (g, p) in enumerate(units):
            at = (at_rows(g), at_lanes(p, 128))
            self.weights[self.pairs * g + p] = weights[n]
            inverse = 1.0 / pick_pair(both[n][:, 128:], low)
            self.inverse[at] = inverse
            self.mixed[at] = (pick_pair(both[n][:, :128], low) * inverse).astype(BF16)

    def branch(self, windows):
        return mm(self.mixed[self.rows_of(windows), :], self.wo[...])

    def mixed_back(self, windows, grad_ref, dmixed_ref):
        rows = self.rows_of(windows)
        for at in self.chunks():
            dmixed_ref[rows, at] = mm_nt(grad_ref[rows, :], self.wo[at, :]).astype(BF16)

    def attend_back(self, windows, dmixed_ref, duq_ref, duk_ref, dqkv_ref):
        low = pair_masks()
        ones = jnp.ones((PAD, 128), BF16)
        units = self.units(windows)
        divided = [
            d.astype(F32) * i
            for d, i in zip(self.tiles(dmixed_ref, units), self.tiles(self.inverse, units))
        ]
        shift = [
            stack_pair((-(d * m.astype(F32))).astype(BF16), low)
            for d, m in zip(divided, self.tiles(self.mixed, units))
        ]
        douts = [stack_pair(d.astype(BF16), low) for d in divided]
        queries = [stack_pair(q, low) for q in self.tiles(self.uq, units)]
        keys, values = self.tiles(self.uk, units), self.tiles(self.v, units)
        weights = [self.weights[self.pairs * g + p] for g, p in units]
        dprobs = [
            mm_nt(beside(d, s), beside(v, ones)) for d, s, v in zip(douts, shift, values)
        ]
        dscores = [
            (w.astype(F32) * (d * self.scales(p, 1.0))).astype(BF16)
            for w, d, (g, p) in zip(weights, dprobs, units)
        ]
        dvalues = [mm_tn(w, d) for w, d in zip(weights, douts)]
        dkeys = [mm_tn(d, q) for d, q in zip(dscores, queries)]
        dqueries = [mm(d, k) for d, k in zip(dscores, keys)]
        for n, (g, p) in enumerate(units):
            at = (at_rows(g), at_lanes(p, 128))
            behind = at_lanes(p + 2 * self.pairs, 128)
            dqkv_ref[at_rows(g), behind] = dvalues[n].astype(BF16)
            duk_ref[at] = dkeys[n].astype(BF16)
            duq_ref[at] = pick_pair(dqueries[n], low).astype(BF16)

    def project_back(self, windows, duq_ref, duk_ref, dqkv_ref, dn_ref):
        channels = self.channels
        rows = self.rows_of(windows)
        for at in self.chunks():
            shifted = pl.ds(at.start + channels, 512)
            for u_ref, r_ref, du_ref, to in (
                (self.uq, self.rq, duq_ref, at),
                (self.uk, self.rk, duk_ref, shifted),
            ):
                u = u_ref[rows, at].astype(F32)
                du = du_ref[rows, at].astype(F32)
                inner = self.head_total((u * du).astype(BF16))
                dqkv_ref[rows, to] = (r_ref[rows, at] * (du - u * inner)).astype(BF16)
        for at in self.chunks():
            dn_ref[rows, at] = mm_nt(dqkv_ref[rows, :channels], self.wq[at, :]) + mm_nt(
                dqkv_ref[rows, channels:], self.wkv[at, :]
            )

    def norm_backward(self, g, dn):
        dy = dn * self.gain[...]
        xhat = self.xhat[at_rows(g), :]
        rstd = self.rstd[at_rows(g), :][:, :1]
        return rstd * (dy - row_mean(dy) - xhat * row_mean(dy * xhat))


WEIGHTS = (
    "encoder_query",
    "encoder_keyval",
    "encoder_output",
    "merge_weight",
    "coarse_query",
    "coarse_keyval",
    "coarse_output",
    "expand_weight",
    "decoder_query",
    "decoder_keyval",
    "decoder_output",
)


def kept_shapes(rows, channels):
    units = rows // PAD * (channels // 128)
    return [
        ((rows, channels), F32),
        ((rows, 128), F32),
        ((rows, channels), BF16),
        ((rows, channels), BF16),
        ((rows, channels), F32),
        ((rows, channels), F32),
        ((rows, channels), BF16),
        ((units, 2 * PAD, PAD), BF16),
        ((rows, channels), F32),
        ((rows, channels), BF16),
    ]


def scratch_table():
    table = {}
    for block, rows, channels in (("enc", BODY, D), ("dec", BODY, D), ("crs", PAD, DC)):
        table[block] = kept_shapes(rows, channels)
    for kind, rows, channels in (("fine", BODY, D), ("coarse", PAD, DC)):
        table[kind] = [
            ((rows, channels), BF16),
            ((rows, channels), BF16),
            ((rows, channels), BF16),
            ((rows, channels), BF16),
            ((rows, 3 * channels), BF16),
            ((rows, channels), F32),
            ((rows, channels), F32),
            ((rows, channels), BF16),
        ]
    table["misc"] = [
        ((HOME, D), BF16),
        ((HOME, D), BF16),
        ((HOME, D), BF16),
        ((HOME, D), BF16),
        ((BODY, D), F32),
        ((BODY, D), F32),
        ((BODY, D), F32),
        ((PAD, 4 * D), F32),
        ((PAD, 128), F32),
        ((PAD, 4 * D), BF16),
        ((PAD, DC), F32),
        ((PAD, 128), F32),
        ((PAD, 4 * D), BF16),
        ((BODY, D), BF16),
        ((HOME, D), F32),
        ((HOME, D), F32),
        ((HOME * 4, 128), F32),
        ((2, HOME * 4, 128), BF16),
        ((2, 2 * PAD, 128), BF16),
        ((PAD, 128), BF16),
        ((256, 256), BF16),
        ((8, SENT, D), BF16),
        ((8, SENT, D), BF16),
    ]
    return table


TABLE = scratch_table()
NAMES = tuple(TABLE)


def kernel(*refs):
    refs = list(refs)

    def take(n):
        head = refs[:n]
        del refs[:n]
        return head

    fields_in, cot_in = take(2)
    weights_in = take(len(WEIGHTS))
    moves_in = take(12)
    enc_gain, merge_gain, crs_gain, exp_gain, dec_gain = take(5)
    enc_scale, crs_scale, dec_scale = take(3)
    (out_hbm,) = take(1)
    fields_v, cot_v = take(2)
    weights = take(len(WEIGHTS))
    moves = take(12)
    spaces = {name: take(len(TABLE[name])) for name in NAMES}
    local_sem, out_sem, send_sem, recv_sem = take(4)

    lat, lon = lax.axis_index("lat"), lax.axis_index("lon")
    nlat, nlon = lax.axis_size("lat"), lax.axis_size("lon")

    loads = []
    waited = [0]

    def load(*pairs):
        for src, dst in pairs:
            copy = pltpu.make_async_copy(src, dst, local_sem.at[len(loads)])
            copy.start()
            loads.append(copy)

    def loaded(upto):
        while waited[0] < upto:
            loads[waited[0]].wait()
            waited[0] += 1

    def weight(*which):
        return [(weights_in[n], weights[n]) for n in which]

    def move(*which):
        return [(moves_in[n], moves[n]) for n in which]

    load((fields_in, fields_v), *move(0, 1), (cot_in, cot_v), *weight(0, 1, 2))

    def device(dlat, dlon):
        return {
            "lat": lax.rem(lat + dlat + nlat, nlat),
            "lon": lax.rem(lon + dlon + nlon, nlon),
        }

    onward = (device(1, 0), device(0, 1), device(1, 1))
    back = (device(-1, 0), device(0, -1), device(-1, -1))
    barrier = pltpu.get_barrier_semaphore()
    for target in onward + back:
        pl.semaphore_signal(
            barrier, inc=1, device_id=target, device_id_type=pl.DeviceIdType.MESH
        )

    (
        fields_b,
        fields_rest,
        cot_b,
        cot_rest,
        cot_f,
        gskip,
        planes,
        m_xhat,
        m_rstd,
        merged,
        e_xhat,
        e_rstd,
        dexp,
        out_b,
        out_home,
        grad_home,
        by_cell,
        out_cells,
        bar_q,
        bar_k,
        sums,
        sent,
        received,
    ) = spaces["misc"]

    bar_q[0] = bar_queries(jnp.where(lat == 0, 1, 0))
    bar_q[1] = bar_queries(0)
    bar_k[...] = bar_keys()
    sums[...] = head_sums()

    started = {}

    def prepare(t, source, pick):
        sent[t] = mm(pick[...], source).astype(BF16)

    def launch(t, targets):
        started[t] = []
        for n, (start, size) in enumerate(PIECES):
            copy = pltpu.make_async_remote_copy(
                src_ref=sent.at[t, pl.ds(start, size)],
                dst_ref=received.at[t, pl.ds(start, size)],
                send_sem=send_sem.at[t, n],
                recv_sem=recv_sem.at[t, n],
                device_id=targets[n],
                device_id_type=pl.DeviceIdType.MESH,
            )
            copy.start()
            started[t].append(copy)

    def arrive(t):
        for copy in started[t]:
            copy.wait_recv()

    def flat(ref, to, rest):
        for n in range(4):
            part = ref[pl.ds(n, HOME, stride=4), :]
            rounded = part.astype(BF16)
            to[:, at_lanes(n, 128)] = rounded
            rest[:, at_lanes(n, 128)] = (part - rounded.astype(F32)).astype(BF16)

    outs = []

    def deliver(x, which):
        for n in range(4):
            by_cell[pl.ds(n, HOME, stride=4), :] = x[:, 128 * n : 128 * (n + 1)]
        out_cells[which] = by_cell[...].astype(BF16)
        copy = pltpu.make_async_copy(out_cells.at[which], out_hbm.at[which], out_sem.at[which])
        copy.start()
        outs.append(copy)

    encoder = Block(
        BODY, D, enc_gain, weights[0], weights[1], weights[2], enc_scale, spaces["enc"], sums
    )
    coarse = Block(
        PAD, DC, crs_gain, weights[4], weights[5], weights[6], crs_scale, spaces["crs"], sums
    )
    decoder = Block(
        BODY, D, dec_gain, weights[8], weights[9], weights[10], dec_scale, spaces["dec"], sums
    )
    merge_w, expand_w = weights[3], weights[7]
    fn, fdmixed, fduq, fduk, fdqkv, fdn, fx, fb = spaces["fine"]
    cn, cdmixed, cduq, cduk, cdqkv, cdn, cx, cb = spaces["coarse"]

    def fine_bar(g):
        return bar_q[g // 2]

    def coarse_bar(g):
        return bar_q[0]

    def encode(windows):
        rows = encoder.rows_of(windows)
        encoder.project(windows, fn)
        encoder.attend(windows, fine_bar, bar_k[...])
        section = fx[rows, :] + encoder.branch(windows)
        fx[rows, :] = section
        fb[rows, :] = section.astype(BF16)

    def decode(windows):
        rows = decoder.rows_of(windows)
        for g in windows:
            decoder.norm_rows(g, fx[at_rows(g), :], fn)
        decoder.project(windows, fn)
        decoder.attend(windows, fine_bar, bar_k[...])
        out_b[rows, :] = (fx[rows, :] + decoder.branch(windows)).astype(BF16)
        decoder.attend_back(windows, fdmixed, fduq, fduk, fdqkv)
        decoder.project_back(windows, fduq, fduk, fdqkv, fdn)
        for g in windows:
            at = at_rows(g)
            x = cot_f[at, :] + decoder.norm_backward(g, fdn[at, :])
            gskip[at, :] = x
            fb[at, :] = x.astype(BF16)

    def encode_back(windows):
        encoder.mixed_back(windows, fb, fdmixed)
        encoder.attend_back(windows, fdmixed, fduq, fduk, fdqkv)
        encoder.project_back(windows, fduq, fduk, fdqkv, fdn)
        for g in windows:
            at = at_rows(g)
            x = gskip[at, :] + encoder.norm_backward(g, fdn[at, :])
            fb[at, :] = x.astype(BF16)

    loaded(2)
    flat(fields_v, fields_b, fields_rest)
    prepare(0, fields_b[...], moves[0])
    pl.semaphore_wait(barrier, 6)
    launch(0, onward)
    load(*move(2, 6, 7, 8), *weight(3, 4, 5, 6, 7), *move(9, 10, 11), *weight(8, 9, 10))
    load(*move(3, 4, 5))
    loaded(4)
    fx[...] = mm(moves[1][...], fields_b[...]) + mm(moves[1][...], fields_rest[...])
    flat(cot_v, cot_b, cot_rest)
    prepare(1, cot_b[...], moves[0])
    cot_f[...] = mm(moves[1][...], cot_b[...]) + mm(moves[1][...], cot_rest[...])
    loaded(7)
    encoder.norm_rows(3, fx[at_rows(3), :], fn)
    encode(range(3, 4))
    loaded(8)
    arrive(0)
    launch(1, onward)
    for g in range(3):
        at = at_rows(g)
        x = fx[at, :] + mm(moves[2][at, :], received[0])
        fx[at, :] = x
        encoder.norm_rows(g, x, fn)
    encode(range(1, 3))

    loaded(11)
    prepare(2, fb[PAD:, :], moves[6])
    launch(2, onward)
    encode(range(0, 1))
    planes[...] = mm(moves[7][...], fb[...])
    arrive(1)
    cot = cot_f[...] + mm(moves[2][...], received[1])
    cot_f[...] = cot
    out_b[...] = cot.astype(BF16)
    loaded(len(loads))
    arrive(2)
    total = jnp.zeros((PAD, D), F32)
    for p in range(4):
        x = planes[at_rows(p), :] + mm(moves[8][at_rows(p), :], received[2])
        planes[at_rows(p), :] = x
        total += x
    mean = jnp.sum(total, axis=-1, keepdims=True) * (1.0 / (4 * D))
    total = jnp.zeros((PAD, D), F32)
    for p in range(4):
        centred = planes[at_rows(p), :] - mean
        total += centred * centred
    rstd = lax.rsqrt(jnp.sum(total, axis=-1, keepdims=True) * (1.0 / (4 * D)) + EPS)
    m_rstd[...] = jnp.broadcast_to(rstd, (PAD, 128))
    for p in range(4):
        lanes = at_lanes(p, D)
        xhat = (planes[at_rows(p), :] - mean) * rstd
        m_xhat[:, lanes] = xhat
        merged[:, lanes] = (xhat * merge_gain[:, lanes]).astype(BF16)
    cx[...] = mm(merged[...], merge_w[...])
    coarse.norm_rows(0, cx[...], cn)
    coarse.project(coarse.every, cn)
    coarse.attend(coarse.every, coarse_bar, bar_k[...])
    x = cx[...] + coarse.branch(coarse.every)
    centred = x - row_mean(x)
    rstd = lax.rsqrt(row_mean(centred * centred) + EPS)
    xhat = centred * rstd
    e_xhat[...] = xhat
    e_rstd[...] = jnp.broadcast_to(rstd, (PAD, 128))
    cb[...] = (xhat * exp_gain[...]).astype(BF16)
    for p in range(4):
        fb[at_rows(p), :] = mm(cb[...], expand_w[:, at_lanes(p, D)]).astype(BF16)

    prepare(3, fb[...], moves[9])
    launch(3, back)
    fx[...] = fx[...] + mm(moves[10][...], fb[...])
    decoder.mixed_back(decoder.every, out_b, fdmixed)
    decode(range(0, 1))
    arrive(3)
    later = pl.ds(PAD, 3 * PAD)
    fx[later, :] = fx[later, :] + mm(moves[11][later, :], received[3])
    decode(range(1, 4))

    prepare(5, fb[PAD:, :], moves[6])
    launch(5, onward)
    planes[...] = mm(moves[7][...], fb[...])
    prepare(4, out_b[: 3 * PAD, :], moves[3])
    out_home[...] = mm(moves[4][...], out_b[...])
    arrive(5)
    launch(4, back)
    for p in range(4):
        x = planes[at_rows(p), :] + mm(moves[8][at_rows(p), :], received[5])
        dexp[:, at_lanes(p, D)] = x.astype(BF16)
    dy = mm_nt(dexp[...], expand_w[...]) * exp_gain[...]
    xhat = e_xhat[...]
    x = e_rstd[:, :1] * (dy - row_mean(dy) - xhat * row_mean(dy * xhat))
    cx[...] = x
    cb[...] = x.astype(BF16)
    coarse.mixed_back(coarse.every, cb, cdmixed)
    coarse.attend_back(coarse.every, cdmixed, cduq, cduk, cdqkv)
    coarse.project_back(coarse.every, cduq, cduk, cdqkv, cdn)
    cb[...] = (cx[...] + coarse.norm_backward(0, cdn[...])).astype(BF16)
    for p in range(4):
        planes[at_rows(p), :] = mm_nt(cb[...], merge_w[at_rows(p, D), :])
    total = jnp.zeros((PAD, D), F32)
    weighed = jnp.zeros((PAD, D), F32)
    for p in range(4):
        lanes = at_lanes(p, D)
        dy = planes[at_rows(p), :] * merge_gain[:, lanes]
        total += dy
        weighed += dy * m_xhat[:, lanes]
    mean = jnp.sum(total, axis=-1, keepdims=True) * (1.0 / (4 * D))
    tilt = jnp.sum(weighed, axis=-1, keepdims=True) * (1.0 / (4 * D))
    rstd = m_rstd[:, :1]
    for p in range(4):
        lanes = at_lanes(p, D)
        dy = planes[at_rows(p), :] * merge_gain[:, lanes]
        fb[at_rows(p), :] = (rstd * (dy - mean - m_xhat[:, lanes] * tilt)).astype(BF16)

    prepare(6, fb[...], moves[9])
    launch(6, back)
    x = gskip[...] + mm(moves[10][...], fb[...])
    gskip[...] = x
    fb[at_rows(0), :] = x[:PAD].astype(BF16)
    encode_back(range(0, 1))
    arrive(4)
    deliver(out_home[...] + mm(moves[5][...], received[4]), 0)
    arrive(6)
    x = gskip[later, :] + mm(moves[11][later, :], received[6])
    gskip[later, :] = x
    fb[later, :] = x.astype(BF16)
    encode_back(range(1, 3))

    prepare(7, fb[: 3 * PAD, :], moves[3])
    launch(7, back)
    encode_back(range(3, 4))
    grad_home[...] = mm(moves[4][...], fb[...])
    arrive(7)
    deliver(grad_home[...] + mm(moves[5][...], received[7]), 1)
    for t in started:
        for copy in started[t]:
            copy.wait_send()
    for copy in outs:
        copy.wait()


def shards(
    fields,
    cotangent,
    encoder_gain,
    encoder_query,
    encoder_keyval,
    encoder_output,
    encoder_scale,
    merge_gain,
    merge_weight,
    coarse_gain,
    coarse_query,
    coarse_keyval,
    coarse_output,
    coarse_scale,
    expand_gain,
    expand_weight,
    decoder_gain,
    decoder_query,
    decoder_keyval,
    decoder_output,
    decoder_scale,
):
    shape = fields.shape
    weights = (
        encoder_query,
        encoder_keyval,
        encoder_output,
        merge_weight,
        coarse_query,
        coarse_keyval,
        coarse_output,
        expand_weight,
        decoder_query,
        decoder_keyval,
        decoder_output,
    )
    moves = [jnp.asarray(m) for m in all_moves()]
    gains = [
        g.reshape(1, -1)
        for g in (encoder_gain, merge_gain, coarse_gain, expand_gain, decoder_gain)
    ]
    scales = (encoder_scale, coarse_scale, decoder_scale)
    flat = (HOME * 4, 128)
    anywhere = pl.BlockSpec(memory_space=pl.ANY)
    in_vmem = pl.BlockSpec(memory_space=pltpu.VMEM)
    in_smem = pl.BlockSpec(memory_space=pltpu.SMEM)
    scratch = [pltpu.VMEM(flat, F32)] * 2
    scratch += [pltpu.VMEM(w.shape, BF16) for w in weights]
    scratch += [pltpu.VMEM(m.shape, BF16) for m in moves]
    for name in NAMES:
        scratch += [pltpu.VMEM(s, t) for s, t in TABLE[name]]
    scratch += [
        pltpu.SemaphoreType.DMA((2 + len(weights) + len(moves),)),
        pltpu.SemaphoreType.DMA((2,)),
        pltpu.SemaphoreType.DMA((8, 3)),
        pltpu.SemaphoreType.DMA((8, 3)),
    ]
    results = pl.pallas_call(
        kernel,
        out_shape=jax.ShapeDtypeStruct((2,) + flat, BF16),
        in_specs=[anywhere] * (2 + len(weights) + len(moves)) + [in_vmem] * 5 + [in_smem] * 3,
        out_specs=anywhere,
        scratch_shapes=scratch,
        compiler_params=pltpu.CompilerParams(
            collective_id=0, has_side_effects=True, vmem_limit_bytes=60 * 1024 * 1024
        ),
    )(
        fields.reshape(flat),
        cotangent.reshape(flat),
        *weights,
        *moves,
        *gains,
        *scales,
    )
    return tuple(results[n].astype(F32).reshape(shape) for n in range(2))


def solution(mesh):
    along = P("lat", "lon", None, None)
    return jax.shard_map(
        shards,
        mesh=mesh,
        in_specs=(along, along) + (P(),) * 19,
        out_specs=(along, along),
        check_vma=False,
    )
```

```python
import functools

import jax
import jax.numpy as jnp
import numpy as np
from jax import lax
from jax.experimental import pallas as pl
from jax.experimental.pallas import tpu as pltpu
from jax.sharding import PartitionSpec as P

WLAT = 6
WLON = 12
EPS = 1e-05
ROWS, COLS = 12, 24
HOME = ROWS * COLS
PAD = 80
BODY = 4 * PAD
CELLS = WLAT * WLON
PIECES = ((0, 64), (64, 64), (128, 32))
SENT = 160
D = 512
DC = 1024
F32 = jnp.float32
BF16 = jnp.bfloat16
LOG2E = 1.4426950408889634


def fine_order(r, c):
    return PAD * (2 * (r // WLAT) + c // WLON) + (r % WLAT) * WLON + c % WLON


def plane_order(r, c):
    return PAD * (2 * (r % 2) + c % 2) + (r // 2) * WLON + c // 2


def home_order(r, c):
    return r * COLS + c


def piece_row(r, c):
    if r >= 9 and c < 18:
        return (r - 9) * 18 + c
    if r < 9 and c >= 18:
        return 64 + r * 6 + (c - 18)
    if r >= 9 and c >= 18:
        return 128 + (r - 9) * 6 + (c - 18)
    return None


def move_matrices(order_a, rows_a, order_b, rows_b):
    pick = np.zeros((SENT, rows_a), np.float32)
    own = np.zeros((rows_b, rows_a), np.float32)
    place = np.zeros((rows_b, SENT), np.float32)
    for r in range(ROWS):
        for c in range(COLS):
            piece = piece_row(r, c)
            if piece is not None:
                pick[piece, order_a(r, c)] = 1
            ra, ca = (r - 3) % ROWS, (c - 6) % COLS
            if r >= 3 and c >= 6:
                own[order_b(r, c), order_a(ra, ca)] = 1
            else:
                place[order_b(r, c), piece_row(ra, ca)] = 1
    return pick, own, place


def all_moves():
    first = move_matrices(home_order, HOME, fine_order, BODY)
    second = move_matrices(fine_order, BODY, plane_order, BODY)
    pick, own, place = first
    moves = [pick, own, place, place.T[:, : 3 * PAD], own.T, pick.T]
    pick, own, place = second
    moves += [pick[:, PAD:], own, place, place.T, own.T, pick.T]
    return [np.ascontiguousarray(m).astype(jnp.bfloat16) for m in moves]


def mm(a, b):
    return lax.dot_general(a, b, (((1,), (0,)), ((), ())), preferred_element_type=F32)


def mm_nt(a, b):
    return lax.dot_general(a, b, (((1,), (1,)), ((), ())), preferred_element_type=F32)


def mm_tn(a, b):
    return lax.dot_general(a, b, (((0,), (0,)), ((), ())), preferred_element_type=F32)


def row_mean(x):
    return jnp.mean(x, axis=-1, keepdims=True)


def at_rows(g, n=PAD):
    if isinstance(g, int):
        return pl.ds(g * n, n)
    return pl.ds(pl.multiple_of(g * n, n), n)


def at_lanes(j, n):
    if isinstance(j, int):
        return pl.ds(j * n, n)
    return pl.ds(pl.multiple_of(j * n, n), n)


def head_sums():
    shape = (256, 256)
    a = lax.broadcasted_iota(jnp.int32, shape, 0) // 64
    b = lax.broadcasted_iota(jnp.int32, shape, 1) // 64
    return jnp.where(a == b, 1.0, 0.0).astype(BF16)


def pair_masks():
    lane = lax.broadcasted_iota(jnp.int32, (PAD, 128), 1)
    return lane < 64


def stack_pair(x, low):
    zero = jnp.zeros_like(x)
    return jnp.concatenate([jnp.where(low, x, zero), jnp.where(low, zero, x)], axis=0)


def pick_pair(x, low):
    return jnp.where(low, x[:PAD], x[PAD:])


def beside(a, b):
    return jnp.concatenate([a, b], axis=1)


def bar_queries(first):
    shape = (2 * PAD, 128)
    q = lax.broadcasted_iota(jnp.int32, shape, 0)
    q = jnp.where(q >= PAD, q - PAD, q)
    lane = lax.broadcasted_iota(jnp.int32, shape, 1)
    upper = jnp.where(q < CELLS // 2, first, 0)
    lower = jnp.where(q < CELLS // 2, 0, first)
    value = jnp.where(lane == 0, upper, jnp.where(lane == 1, lower, 0))
    return jnp.where(lane == 2, 1, value).astype(F32).astype(BF16)


def bar_keys():
    shape = (PAD, 128)
    k = lax.broadcasted_iota(jnp.int32, shape, 0)
    lane = lax.broadcasted_iota(jnp.int32, shape, 1)
    upper = jnp.where(k < CELLS // 2, 1, 0)
    there = jnp.where(k < CELLS, 1, 0)
    value = jnp.where(lane == 0, there - upper, jnp.where(lane == 1, upper, 0))
    value = jnp.where(lane == 2, 1 - there, value)
    return (value * -1024).astype(F32).astype(BF16)


def turn(src, dst):
    rows, cols = src.shape
    for a in range(0, rows, 256):
        for b in range(0, cols, 256):
            dst[pl.ds(b, 256), pl.ds(a, 256)] = src[pl.ds(a, 256), pl.ds(b, 256)].T


class Block:
    def __init__(self, rows, channels, gain, wq, wkv, wo, scale, kept, sums):
        self.rows, self.channels = rows, channels
        self.gain, self.wq, self.wkv, self.wo, self.scale = gain, wq, wkv, wo, scale
        self.xhat, self.rstd, self.uq, self.uk, self.rq, self.rk = kept[:6]
        self.v, self.weights, self.inverse, self.mixed = kept[6:]
        self.sums = sums
        self.wq_t = self.wkv_t = self.wo_t = None
        self.pairs = channels // 128
        self.every = range(rows // PAD)

    def chunks(self):
        return [pl.ds(at, 512) for at in range(0, self.channels, 512)]

    def rows_of(self, windows):
        return pl.ds(PAD * windows.start, PAD * len(windows))

    def units(self, windows):
        return [(g, p) for g in windows for p in range(self.pairs)]

    def tiles(self, ref, units):
        return [ref[at_rows(g), at_lanes(p, 128)] for g, p in units]

    def norm_rows(self, g, x, n_ref):
        centred = x - row_mean(x)
        rstd = lax.rsqrt(row_mean(centred * centred) + EPS)
        xhat = centred * rstd
        self.xhat[at_rows(g), :] = xhat
        self.rstd[at_rows(g), :] = jnp.broadcast_to(rstd, (PAD, 128))
        n_ref[at_rows(g), :] = (xhat * self.gain[...]).astype(BF16)

    def head_total(self, x):
        sums = self.sums[...]
        return beside(mm(x[:, :256], sums), mm(x[:, 256:], sums))

    def project(self, windows, n_ref):
        rows = self.rows_of(windows)

        def unit(weight, at, u_ref, r_ref):
            raw = mm(n_ref[rows, :], weight[:, at]).astype(BF16).astype(F32)
            r = lax.rsqrt(self.head_total((raw * raw).astype(BF16)) + 1.0)
            r_ref[rows, at] = r
            u_ref[rows, at] = (raw * r).astype(BF16)

        for at in self.chunks():
            unit(self.wq, at, self.uq, self.rq)
            unit(self.wkv, at, self.uk, self.rk)
            behind = pl.ds(at.start + self.channels, 512)
            self.v[rows, at] = mm(n_ref[rows, :], self.wkv[:, behind]).astype(BF16)

    def scales(self, p, factor):
        top = lax.broadcasted_iota(jnp.int32, (2 * PAD, 1), 0) < PAD
        return jnp.where(top, self.scale[2 * p] * factor, self.scale[2 * p + 1] * factor)

    def attend(self, windows, barred, bar_key):
        low = pair_masks()
        ones = jnp.ones((PAD, 128), BF16)
        units = self.units(windows)
        queries = [stack_pair(q, low) for q in self.tiles(self.uq, units)]
        keys, values = self.tiles(self.uk, units), self.tiles(self.v, units)
        scores = [
            mm_nt(beside(q, barred(g)), beside(k, bar_key))
            for q, k, (g, p) in zip(queries, keys, units)
        ]
        weights = [
            jnp.exp2(s * self.scales(p, LOG2E)).astype(BF16)
            for s, (g, p) in zip(scores, units)
        ]
        both = [mm(w, beside(v, ones)) for w, v in zip(weights, values)]
        for n, (g, p) in enumerate(units):
            at = (at_rows(g), at_lanes(p, 128))
            self.weights[self.pairs * g + p] = weights[n]
            inverse = 1.0 / pick_pair(both[n][:, 128:], low)
            self.inverse[at] = inverse
            self.mixed[at] = (pick_pair(both[n][:, :128], low) * inverse).astype(BF16)

    def branch(self, windows):
        return mm(self.mixed[self.rows_of(windows), :], self.wo[...])

    def mixed_back(self, windows, grad_ref, dmixed_ref):
        rows = self.rows_of(windows)
        for at in self.chunks():
            if self.wo_t is None:
                back = mm_nt(grad_ref[rows, :], self.wo[at, :])
            else:
                back = mm(grad_ref[rows, :], self.wo_t[:, at])
            dmixed_ref[rows, at] = back.astype(BF16)

    def attend_back(self, windows, dmixed_ref, duq_ref, duk_ref, dqkv_ref):
        low = pair_masks()
        ones = jnp.ones((PAD, 128), BF16)
        units = self.units(windows)
        divided = [
            d.astype(F32) * i
            for d, i in zip(self.tiles(dmixed_ref, units), self.tiles(self.inverse, units))
        ]
        shift = [
            stack_pair((-(d * m.astype(F32))).astype(BF16), low)
            for d, m in zip(divided, self.tiles(self.mixed, units))
        ]
        douts = [stack_pair(d.astype(BF16), low) for d in divided]
        queries = [stack_pair(q, low) for q in self.tiles(self.uq, units)]
        keys, values = self.tiles(self.uk, units), self.tiles(self.v, units)
        weights = [self.weights[self.pairs * g + p] for g, p in units]
        dprobs = [
            mm_nt(beside(d, s), beside(v, ones)) for d, s, v in zip(douts, shift, values)
        ]
        dscores = [
            (w.astype(F32) * (d * self.scales(p, 1.0))).astype(BF16)
            for w, d, (g, p) in zip(weights, dprobs, units)
        ]
        dvalues = [mm_tn(w, d) for w, d in zip(weights, douts)]
        dkeys = [mm_tn(d, q) for d, q in zip(dscores, queries)]
        dqueries = [mm(d, k) for d, k in zip(dscores, keys)]
        for n, (g, p) in enumerate(units):
            at = (at_rows(g), at_lanes(p, 128))
            behind = at_lanes(p + 2 * self.pairs, 128)
            dqkv_ref[at_rows(g), behind] = dvalues[n].astype(BF16)
            duk_ref[at] = dkeys[n].astype(BF16)
            duq_ref[at] = pick_pair(dqueries[n], low).astype(BF16)

    def project_back(self, windows, duq_ref, duk_ref, dqkv_ref, dn_ref):
        channels = self.channels
        rows = self.rows_of(windows)
        for at in self.chunks():
            shifted = pl.ds(at.start + channels, 512)
            for u_ref, r_ref, du_ref, to in (
                (self.uq, self.rq, duq_ref, at),
                (self.uk, self.rk, duk_ref, shifted),
            ):
                u = u_ref[rows, at].astype(F32)
                du = du_ref[rows, at].astype(F32)
                inner = self.head_total((u * du).astype(BF16))
                dqkv_ref[rows, to] = (r_ref[rows, at] * (du - u * inner)).astype(BF16)
        for at in self.chunks():
            dquery, dkeyval = dqkv_ref[rows, :channels], dqkv_ref[rows, channels:]
            if self.wq_t is None:
                back = mm_nt(dquery, self.wq[at, :]) + mm_nt(dkeyval, self.wkv[at, :])
            else:
                back = mm(dquery, self.wq_t[:, at]) + mm(dkeyval, self.wkv_t[:, at])
            dn_ref[rows, at] = back

    def norm_backward(self, g, dn):
        dy = dn * self.gain[...]
        xhat = self.xhat[at_rows(g), :]
        rstd = self.rstd[at_rows(g), :][:, :1]
        return rstd * (dy - row_mean(dy) - xhat * row_mean(dy * xhat))


WEIGHTS = (
    "encoder_query",
    "encoder_keyval",
    "encoder_output",
    "merge_weight",
    "coarse_query",
    "coarse_keyval",
    "coarse_output",
    "expand_weight",
    "decoder_query",
    "decoder_keyval",
    "decoder_output",
)


def kept_shapes(rows, channels):
    units = rows // PAD * (channels // 128)
    return [
        ((rows, channels), F32),
        ((rows, 128), F32),
        ((rows, channels), BF16),
        ((rows, channels), BF16),
        ((rows, channels), F32),
        ((rows, channels), F32),
        ((rows, channels), BF16),
        ((units, 2 * PAD, PAD), BF16),
        ((rows, channels), F32),
        ((rows, channels), BF16),
    ]


def scratch_table():
    table = {}
    for block, rows, channels in (("enc", BODY, D), ("dec", BODY, D), ("crs", PAD, DC)):
        table[block] = kept_shapes(rows, channels)
    for kind, rows, channels in (("fine", BODY, D), ("coarse", PAD, DC)):
        table[kind] = [
            ((rows, channels), BF16),
            ((rows, channels), BF16),
            ((rows, channels), BF16),
            ((rows, channels), BF16),
            ((rows, 3 * channels), BF16),
            ((rows, channels), F32),
            ((rows, channels), F32),
            ((rows, channels), BF16),
        ]
    table["misc"] = [
        ((HOME, D), BF16),
        ((HOME, D), BF16),
        ((HOME, D), BF16),
        ((HOME, D), BF16),
        ((BODY, D), F32),
        ((BODY, D), F32),
        ((BODY, D), F32),
        ((PAD, 4 * D), F32),
        ((PAD, 128), F32),
        ((PAD, 4 * D), BF16),
        ((PAD, DC), F32),
        ((PAD, 128), F32),
        ((PAD, 4 * D), BF16),
        ((BODY, D), BF16),
        ((HOME, D), F32),
        ((HOME, D), F32),
        ((HOME * 4, 128), F32),
        ((2, HOME * 4, 128), BF16),
        ((4 * D, DC), BF16),
        ((2 * DC, DC), BF16),
        ((2, 2 * PAD, 128), BF16),
        ((PAD, 128), BF16),
        ((256, 256), BF16),
        ((8, SENT, D), BF16),
        ((8, SENT, D), BF16),
    ]
    return table


TABLE = scratch_table()
NAMES = tuple(TABLE)


def kernel(*refs):
    refs = list(refs)

    def take(n):
        head = refs[:n]
        del refs[:n]
        return head

    fields_in, cot_in = take(2)
    weights_in = take(len(WEIGHTS))
    moves_in = take(12)
    enc_gain, merge_gain, crs_gain, exp_gain, dec_gain = take(5)
    enc_scale, crs_scale, dec_scale = take(3)
    (out_hbm,) = take(1)
    fields_v, cot_v = take(2)
    weights = take(len(WEIGHTS))
    moves = take(12)
    spaces = {name: take(len(TABLE[name])) for name in NAMES}
    local_sem, out_sem, send_sem, recv_sem = take(4)

    lat, lon = lax.axis_index("lat"), lax.axis_index("lon")
    nlat, nlon = lax.axis_size("lat"), lax.axis_size("lon")

    loads = []
    waited = [0]

    def load(*pairs):
        for src, dst in pairs:
            copy = pltpu.make_async_copy(src, dst, local_sem.at[len(loads)])
            copy.start()
            loads.append(copy)

    def loaded(upto):
        while waited[0] < upto:
            loads[waited[0]].wait()
            waited[0] += 1

    def weight(*which):
        return [(weights_in[n], weights[n]) for n in which]

    def move(*which):
        return [(moves_in[n], moves[n]) for n in which]

    load((fields_in, fields_v))

    def device(dlat, dlon):
        return {
            "lat": lax.rem(lat + dlat + nlat, nlat),
            "lon": lax.rem(lon + dlon + nlon, nlon),
        }

    onward = (device(1, 0), device(0, 1), device(1, 1))
    back = (device(-1, 0), device(0, -1), device(-1, -1))
    barrier = pltpu.get_barrier_semaphore()
    for target in onward + back:
        pl.semaphore_signal(
            barrier, inc=1, device_id=target, device_id_type=pl.DeviceIdType.MESH
        )
    load(*move(0, 1), (cot_in, cot_v), *weight(0, 1, 2))

    (
        fields_b,
        fields_rest,
        cot_b,
        cot_rest,
        cot_f,
        gskip,
        planes,
        m_xhat,
        m_rstd,
        merged,
        e_xhat,
        e_rstd,
        dexp,
        out_b,
        out_home,
        grad_home,
        by_cell,
        out_cells,
        expand_t,
        keyval_t,
        bar_q,
        bar_k,
        sums,
        sent,
        received,
    ) = spaces["misc"]

    bar_q[0] = bar_queries(jnp.where(lat == 0, 1, 0))
    bar_q[1] = bar_queries(0)
    bar_k[...] = bar_keys()
    sums[...] = head_sums()

    started = {}

    def prepare(t, source, pick):
        sent[t] = mm(pick[...], source).astype(BF16)

    def launch(t, targets):
        started[t] = []
        for n in (0, 2, 1):
            start, size = PIECES[n]
            copy = pltpu.make_async_remote_copy(
                src_ref=sent.at[t, pl.ds(start, size)],
                dst_ref=received.at[t, pl.ds(start, size)],
                send_sem=send_sem.at[t, n],
                recv_sem=recv_sem.at[t, n],
                device_id=targets[n],
                device_id_type=pl.DeviceIdType.MESH,
            )
            copy.start()
            started[t].append(copy)

    def arrive(t):
        for copy in started[t]:
            copy.wait_recv()

    def flat(ref, to, rest):
        for n in range(4):
            part = ref[pl.ds(n, HOME, stride=4), :]
            rounded = part.astype(BF16)
            to[:, at_lanes(n, 128)] = rounded
            rest[:, at_lanes(n, 128)] = (part - rounded.astype(F32)).astype(BF16)

    outs = []

    def deliver(x, which):
        for n in range(4):
            by_cell[pl.ds(n, HOME, stride=4), :] = x[:, 128 * n : 128 * (n + 1)]
        out_cells[which] = by_cell[...].astype(BF16)
        copy = pltpu.make_async_copy(out_cells.at[which], out_hbm.at[which], out_sem.at[which])
        copy.start()
        outs.append(copy)

    encoder = Block(
        BODY, D, enc_gain, weights[0], weights[1], weights[2], enc_scale, spaces["enc"], sums
    )
    coarse = Block(
        PAD, DC, crs_gain, weights[4], weights[5], weights[6], crs_scale, spaces["crs"], sums
    )
    decoder = Block(
        BODY, D, dec_gain, weights[8], weights[9], weights[10], dec_scale, spaces["dec"], sums
    )
    merge_w, expand_w = weights[3], weights[7]
    coarse.wq_t, coarse.wo_t = (expand_w.at[:, pl.ds(n * DC, DC)] for n in range(2))
    coarse.wkv_t = keyval_t
    merge_t = (weights[4], weights[6])
    fn, fdmixed, fduq, fduk, fdqkv, fdn, fx, fb = spaces["fine"]
    cn, cdmixed, cduq, cduk, cdqkv, cdn, cx, cb = spaces["coarse"]

    def fine_bar(g):
        return bar_q[g // 2]

    def coarse_bar(g):
        return bar_q[0]

    def encode(windows):
        rows = encoder.rows_of(windows)
        encoder.project(windows, fn)
        encoder.attend(windows, fine_bar, bar_k[...])
        section = fx[rows, :] + encoder.branch(windows)
        fx[rows, :] = section
        fb[rows, :] = section.astype(BF16)

    def decode(windows):
        rows = decoder.rows_of(windows)
        for g in windows:
            decoder.norm_rows(g, fx[at_rows(g), :], fn)
        decoder.project(windows, fn)
        decoder.attend(windows, fine_bar, bar_k[...])
        out_b[rows, :] = (fx[rows, :] + decoder.branch(windows)).astype(BF16)
        decoder.attend_back(windows, fdmixed, fduq, fduk, fdqkv)
        decoder.project_back(windows, fduq, fduk, fdqkv, fdn)
        for g in windows:
            at = at_rows(g)
            x = cot_f[at, :] + decoder.norm_backward(g, fdn[at, :])
            gskip[at, :] = x
            fb[at, :] = x.astype(BF16)

    def encode_back(windows):
        encoder.mixed_back(windows, fb, fdmixed)
        encoder.attend_back(windows, fdmixed, fduq, fduk, fdqkv)
        encoder.project_back(windows, fduq, fduk, fdqkv, fdn)
        for g in windows:
            at = at_rows(g)
            x = gskip[at, :] + encoder.norm_backward(g, fdn[at, :])
            fb[at, :] = x.astype(BF16)

    loaded(2)
    flat(fields_v, fields_b, fields_rest)
    prepare(0, fields_b[...], moves[0])
    pl.semaphore_wait(barrier, 6)
    launch(0, onward)
    load(*move(2, 6, 7, 8), *weight(3, 4, 5, 6, 7), *move(9, 10, 11), *weight(8, 9, 10))
    load(*move(3, 4, 5))
    loaded(4)
    fx[...] = mm(moves[1][...], fields_b[...]) + mm(moves[1][...], fields_rest[...])
    flat(cot_v, cot_b, cot_rest)
    prepare(1, cot_b[...], moves[0])
    cot_f[...] = mm(moves[1][...], cot_b[...]) + mm(moves[1][...], cot_rest[...])
    loaded(7)
    encoder.norm_rows(3, fx[at_rows(3), :], fn)
    encode(range(3, 4))
    loaded(8)
    arrive(0)
    launch(1, onward)
    for g in range(3):
        at = at_rows(g)
        x = fx[at, :] + mm(moves[2][at, :], received[0])
        fx[at, :] = x
        encoder.norm_rows(g, x, fn)
    encode(range(1, 3))

    loaded(11)
    prepare(2, fb[PAD:, :], moves[6])
    launch(2, onward)
    encode(range(0, 1))
    planes[...] = mm(moves[7][...], fb[...])
    arrive(1)
    cot = cot_f[...] + mm(moves[2][...], received[1])
    cot_f[...] = cot
    out_b[...] = cot.astype(BF16)
    loaded(16)
    turn(expand_w, expand_t)
    turn(weights[5].at[:, pl.ds(0, DC)], keyval_t.at[pl.ds(0, DC), :])
    arrive(2)
    total = jnp.zeros((PAD, D), F32)
    for p in range(4):
        x = planes[at_rows(p), :] + mm(moves[8][at_rows(p), :], received[2])
        planes[at_rows(p), :] = x
        total += x
    mean = jnp.sum(total, axis=-1, keepdims=True) * (1.0 / (4 * D))
    total = jnp.zeros((PAD, D), F32)
    for p in range(4):
        centred = planes[at_rows(p), :] - mean
        total += centred * centred
    rstd = lax.rsqrt(jnp.sum(total, axis=-1, keepdims=True) * (1.0 / (4 * D)) + EPS)
    m_rstd[...] = jnp.broadcast_to(rstd, (PAD, 128))
    for p in range(4):
        lanes = at_lanes(p, D)
        xhat = (planes[at_rows(p), :] - mean) * rstd
        m_xhat[:, lanes] = xhat
        merged[:, lanes] = (xhat * merge_gain[:, lanes]).astype(BF16)
    cx[...] = mm(merged[...], merge_w[...])
    coarse.norm_rows(0, cx[...], cn)
    coarse.project(coarse.every, cn)
    coarse.attend(coarse.every, coarse_bar, bar_k[...])
    x = cx[...] + coarse.branch(coarse.every)
    centred = x - row_mean(x)
    rstd = lax.rsqrt(row_mean(centred * centred) + EPS)
    xhat = centred * rstd
    e_xhat[...] = xhat
    e_rstd[...] = jnp.broadcast_to(rstd, (PAD, 128))
    cb[...] = (xhat * exp_gain[...]).astype(BF16)
    for p in range(4):
        fb[at_rows(p), :] = mm(cb[...], expand_w[:, at_lanes(p, D)]).astype(BF16)

    loaded(len(loads))
    prepare(3, fb[...], moves[9])
    launch(3, back)
    fx[...] = fx[...] + mm(moves[10][...], fb[...])
    decoder.mixed_back(decoder.every, out_b, fdmixed)
    decode(range(0, 1))
    arrive(3)
    later = pl.ds(PAD, 3 * PAD)
    fx[later, :] = fx[later, :] + mm(moves[11][later, :], received[3])
    decode(range(1, 4))

    prepare(5, fb[PAD:, :], moves[6])
    launch(5, onward)
    planes[...] = mm(moves[7][...], fb[...])
    prepare(4, out_b[: 3 * PAD, :], moves[3])
    turn(weights[6], coarse.wo_t)
    turn(weights[4], coarse.wq_t)
    turn(weights[5].at[:, pl.ds(DC, DC)], keyval_t.at[pl.ds(DC, DC), :])
    for n in range(2):
        turn(merge_w.at[pl.ds(n * DC, DC), :], merge_t[n])
    arrive(5)
    launch(4, back)
    for p in range(4):
        x = planes[at_rows(p), :] + mm(moves[8][at_rows(p), :], received[5])
        dexp[:, at_lanes(p, D)] = x.astype(BF16)
    dy = mm(dexp[...], expand_t[...]) * exp_gain[...]
    xhat = e_xhat[...]
    x = e_rstd[:, :1] * (dy - row_mean(dy) - xhat * row_mean(dy * xhat))
    cx[...] = x
    cb[...] = x.astype(BF16)
    coarse.mixed_back(coarse.every, cb, cdmixed)
    coarse.attend_back(coarse.every, cdmixed, cduq, cduk, cdqkv)
    coarse.project_back(coarse.every, cduq, cduk, cdqkv, cdn)
    cb[...] = (cx[...] + coarse.norm_backward(0, cdn[...])).astype(BF16)
    for p in range(4):
        planes[at_rows(p), :] = mm(cb[...], merge_t[p // 2][:, at_lanes(p % 2, D)])
    total = jnp.zeros((PAD, D), F32)
    weighed = jnp.zeros((PAD, D), F32)
    for p in range(4):
        lanes = at_lanes(p, D)
        dy = planes[at_rows(p), :] * merge_gain[:, lanes]
        total += dy
        weighed += dy * m_xhat[:, lanes]
    mean = jnp.sum(total, axis=-1, keepdims=True) * (1.0 / (4 * D))
    tilt = jnp.sum(weighed, axis=-1, keepdims=True) * (1.0 / (4 * D))
    rstd = m_rstd[:, :1]
    for p in range(4):
        lanes = at_lanes(p, D)
        dy = planes[at_rows(p), :] * merge_gain[:, lanes]
        fb[at_rows(p), :] = (rstd * (dy - mean - m_xhat[:, lanes] * tilt)).astype(BF16)

    prepare(6, fb[...], moves[9])
    launch(6, back)
    x = gskip[...] + mm(moves[10][...], fb[...])
    gskip[...] = x
    fb[at_rows(0), :] = x[:PAD].astype(BF16)
    out_home[...] = mm(moves[4][...], out_b[...])
    encode_back(range(0, 1))
    arrive(6)
    x = gskip[later, :] + mm(moves[11][later, :], received[6])
    gskip[later, :] = x
    fb[later, :] = x.astype(BF16)
    encode_back(range(1, 3))

    prepare(7, fb[: 3 * PAD, :], moves[3])
    launch(7, back)
    encode_back(range(3, 4))
    arrive(4)
    deliver(out_home[...] + mm(moves[5][...], received[4]), 0)
    grad_home[...] = mm(moves[4][...], fb[...])
    arrive(7)
    deliver(grad_home[...] + mm(moves[5][...], received[7]), 1)
    for t in started:
        for copy in started[t]:
            copy.wait_send()
    for copy in outs:
        copy.wait()


def shards(
    fields,
    cotangent,
    encoder_gain,
    encoder_query,
    encoder_keyval,
    encoder_output,
    encoder_scale,
    merge_gain,
    merge_weight,
    coarse_gain,
    coarse_query,
    coarse_keyval,
    coarse_output,
    coarse_scale,
    expand_gain,
    expand_weight,
    decoder_gain,
    decoder_query,
    decoder_keyval,
    decoder_output,
    decoder_scale,
):
    shape = fields.shape
    weights = (
        encoder_query,
        encoder_keyval,
        encoder_output,
        merge_weight,
        coarse_query,
        coarse_keyval,
        coarse_output,
        expand_weight,
        decoder_query,
        decoder_keyval,
        decoder_output,
    )
    moves = [jnp.asarray(m) for m in all_moves()]
    gains = [
        g.reshape(1, -1)
        for g in (encoder_gain, merge_gain, coarse_gain, expand_gain, decoder_gain)
    ]
    scales = (encoder_scale, coarse_scale, decoder_scale)
    flat = (HOME * 4, 128)
    anywhere = pl.BlockSpec(memory_space=pl.ANY)
    in_vmem = pl.BlockSpec(memory_space=pltpu.VMEM)
    in_smem = pl.BlockSpec(memory_space=pltpu.SMEM)
    scratch = [pltpu.VMEM(flat, F32)] * 2
    scratch += [pltpu.VMEM(w.shape, BF16) for w in weights]
    scratch += [pltpu.VMEM(m.shape, BF16) for m in moves]
    for name in NAMES:
        scratch += [pltpu.VMEM(s, t) for s, t in TABLE[name]]
    scratch += [
        pltpu.SemaphoreType.DMA((2 + len(weights) + len(moves),)),
        pltpu.SemaphoreType.DMA((2,)),
        pltpu.SemaphoreType.DMA((8, 3)),
        pltpu.SemaphoreType.DMA((8, 3)),
    ]
    results = pl.pallas_call(
        kernel,
        out_shape=jax.ShapeDtypeStruct((2,) + flat, BF16),
        in_specs=[anywhere] * (2 + len(weights) + len(moves)) + [in_vmem] * 5 + [in_smem] * 3,
        out_specs=anywhere,
        scratch_shapes=scratch,
        compiler_params=pltpu.CompilerParams(
            collective_id=0, has_side_effects=True, vmem_limit_bytes=60 * 1024 * 1024
        ),
    )(
        fields.reshape(flat),
        cotangent.reshape(flat),
        *weights,
        *moves,
        *gains,
        *scales,
    )
    return tuple(results[n].astype(F32).reshape(shape) for n in range(2))


def solution(mesh):
    along = P("lat", "lon", None, None)
    return jax.shard_map(
        shards,
        mesh=mesh,
        in_specs=(along, along) + (P(),) * 19,
        out_specs=(along, along),
        check_vma=False,
    )
```

```python
import functools

import jax
import jax.numpy as jnp
import numpy as np
from jax import lax
from jax.experimental import pallas as pl
from jax.experimental.pallas import tpu as pltpu
from jax.sharding import PartitionSpec as P

WLAT = 6
WLON = 12
EPS = 1e-05
ROWS, COLS = 12, 24
HOME = ROWS * COLS
PAD = 80
BODY = 4 * PAD
CELLS = WLAT * WLON
PIECES = ((0, 64), (96, 64), (64, 32))
SENT = 160
D = 512
DC = 1024
F32 = jnp.float32
BF16 = jnp.bfloat16
LOG2E = 1.4426950408889634


def fine_order(r, c):
    return PAD * (2 * (r // WLAT) + c // WLON) + (r % WLAT) * WLON + c % WLON


def plane_order(r, c):
    return PAD * (2 * (r % 2) + c % 2) + (r // 2) * WLON + c // 2


def home_order(r, c):
    return r * COLS + c


def piece_row(r, c):
    if r >= 9 and c < 18:
        return (r - 9) * 18 + c
    if r < 9 and c >= 18:
        return 96 + r * 6 + (c - 18)
    if r >= 9 and c >= 18:
        return 64 + (r - 9) * 6 + (c - 18)
    return None


def move_matrices(order_a, rows_a, order_b, rows_b):
    pick = np.zeros((SENT, rows_a), np.float32)
    own = np.zeros((rows_b, rows_a), np.float32)
    place = np.zeros((rows_b, SENT), np.float32)
    for r in range(ROWS):
        for c in range(COLS):
            piece = piece_row(r, c)
            if piece is not None:
                pick[piece, order_a(r, c)] = 1
            ra, ca = (r - 3) % ROWS, (c - 6) % COLS
            if r >= 3 and c >= 6:
                own[order_b(r, c), order_a(ra, ca)] = 1
            else:
                place[order_b(r, c), piece_row(ra, ca)] = 1
    return pick, own, place


def all_moves():
    first = move_matrices(home_order, HOME, fine_order, BODY)
    second = move_matrices(fine_order, BODY, plane_order, BODY)
    pick, own, place = first
    moves = [pick, own, place, place.T[:, : 3 * PAD], own.T, pick.T]
    pick, own, place = second
    moves += [pick[:, PAD:], own, place, place.T, own.T, pick.T]
    return [np.ascontiguousarray(m).astype(jnp.bfloat16) for m in moves]


def mm(a, b):
    return lax.dot_general(a, b, (((1,), (0,)), ((), ())), preferred_element_type=F32)


def mm_nt(a, b):
    return lax.dot_general(a, b, (((1,), (1,)), ((), ())), preferred_element_type=F32)


def mm_tn(a, b):
    return lax.dot_general(a, b, (((0,), (0,)), ((), ())), preferred_element_type=F32)


def row_mean(x):
    return jnp.mean(x, axis=-1, keepdims=True)


def at_rows(g, n=PAD):
    if isinstance(g, int):
        return pl.ds(g * n, n)
    return pl.ds(pl.multiple_of(g * n, n), n)


def at_lanes(j, n):
    if isinstance(j, int):
        return pl.ds(j * n, n)
    return pl.ds(pl.multiple_of(j * n, n), n)


def head_sums():
    shape = (256, 256)
    a = lax.broadcasted_iota(jnp.int32, shape, 0) // 64
    b = lax.broadcasted_iota(jnp.int32, shape, 1) // 64
    return jnp.where(a == b, 1.0, 0.0).astype(BF16)


def pair_masks():
    lane = lax.broadcasted_iota(jnp.int32, (PAD, 128), 1)
    return lane < 64


def stack_pair(x, low):
    zero = jnp.zeros_like(x)
    return jnp.concatenate([jnp.where(low, x, zero), jnp.where(low, zero, x)], axis=0)


def pick_pair(x, low):
    return jnp.where(low, x[:PAD], x[PAD:])


def beside(a, b):
    return jnp.concatenate([a, b], axis=1)


def bar_queries(first):
    shape = (2 * PAD, 128)
    q = lax.broadcasted_iota(jnp.int32, shape, 0)
    q = jnp.where(q >= PAD, q - PAD, q)
    lane = lax.broadcasted_iota(jnp.int32, shape, 1)
    upper = jnp.where(q < CELLS // 2, first, 0)
    lower = jnp.where(q < CELLS // 2, 0, first)
    value = jnp.where(lane == 0, upper, jnp.where(lane == 1, lower, 0))
    return jnp.where(lane == 2, 1, value).astype(F32).astype(BF16)


def bar_keys():
    shape = (PAD, 128)
    k = lax.broadcasted_iota(jnp.int32, shape, 0)
    lane = lax.broadcasted_iota(jnp.int32, shape, 1)
    upper = jnp.where(k < CELLS // 2, 1, 0)
    there = jnp.where(k < CELLS, 1, 0)
    value = jnp.where(lane == 0, there - upper, jnp.where(lane == 1, upper, 0))
    value = jnp.where(lane == 2, 1 - there, value)
    return (value * -1024).astype(F32).astype(BF16)


def turn(src, dst):
    rows, cols = src.shape
    for a in range(0, rows, 256):
        for b in range(0, cols, 256):
            dst[pl.ds(b, 256), pl.ds(a, 256)] = src[pl.ds(a, 256), pl.ds(b, 256)].T


class Block:
    def __init__(self, rows, channels, gain, wq, wkv, wo, scale, kept, sums):
        self.rows, self.channels = rows, channels
        self.gain, self.wq, self.wkv, self.wo, self.scale = gain, wq, wkv, wo, scale
        self.xhat, self.rstd, self.uq, self.uk, self.rq, self.rk = kept[:6]
        self.v, self.weights, self.inverse, self.mixed = kept[6:]
        self.sums = sums
        self.wq_t = self.wkv_t = self.wo_t = None
        self.pairs = channels // 128
        self.every = range(rows // PAD)

    def chunks(self):
        return [pl.ds(at, 512) for at in range(0, self.channels, 512)]

    def rows_of(self, windows):
        return pl.ds(PAD * windows.start, PAD * len(windows))

    def units(self, windows):
        return [(g, p) for g in windows for p in range(self.pairs)]

    def tiles(self, ref, units):
        return [ref[at_rows(g), at_lanes(p, 128)] for g, p in units]

    def norm_rows(self, g, x, n_ref):
        centred = x - row_mean(x)
        rstd = lax.rsqrt(row_mean(centred * centred) + EPS)
        xhat = centred * rstd
        self.xhat[at_rows(g), :] = xhat
        self.rstd[at_rows(g), :] = jnp.broadcast_to(rstd, (PAD, 128))
        n_ref[at_rows(g), :] = (xhat * self.gain[...]).astype(BF16)

    def head_total(self, x):
        sums = self.sums[...]
        return beside(mm(x[:, :256], sums), mm(x[:, 256:], sums))

    def project(self, windows, n_ref):
        rows = self.rows_of(windows)

        def unit(weight, at, u_ref, r_ref):
            raw = mm(n_ref[rows, :], weight[:, at]).astype(BF16).astype(F32)
            r = lax.rsqrt(self.head_total((raw * raw).astype(BF16)) + 1.0)
            r_ref[rows, at] = r
            u_ref[rows, at] = (raw * r).astype(BF16)

        for at in self.chunks():
            unit(self.wq, at, self.uq, self.rq)
            unit(self.wkv, at, self.uk, self.rk)
            behind = pl.ds(at.start + self.channels, 512)
            self.v[rows, at] = mm(n_ref[rows, :], self.wkv[:, behind]).astype(BF16)

    def scaled(self, x, p, factor):
        top, bottom = self.scale[2 * p] * factor, self.scale[2 * p + 1] * factor
        return jnp.concatenate([x[:PAD] * top, x[PAD:] * bottom], axis=0)

    def attend(self, windows, barred, bar_key):
        low = pair_masks()
        ones = jnp.ones((PAD, 128), BF16)
        units = self.units(windows)
        queries = [stack_pair(q, low) for q in self.tiles(self.uq, units)]
        keys, values = self.tiles(self.uk, units), self.tiles(self.v, units)
        scores = [
            mm_nt(beside(q, barred(g)), beside(k, bar_key))
            for q, k, (g, p) in zip(queries, keys, units)
        ]
        weights = [
            jnp.exp2(self.scaled(s, p, LOG2E)).astype(BF16)
            for s, (g, p) in zip(scores, units)
        ]
        both = [mm(w, beside(v, ones)) for w, v in zip(weights, values)]
        for n, (g, p) in enumerate(units):
            at = (at_rows(g), at_lanes(p, 128))
            self.weights[self.pairs * g + p] = weights[n]
            inverse = 1.0 / pick_pair(both[n][:, 128:], low)
            self.inverse[at] = inverse
            self.mixed[at] = (pick_pair(both[n][:, :128], low) * inverse).astype(BF16)

    def branch(self, windows):
        return mm(self.mixed[self.rows_of(windows), :], self.wo[...])

    def mixed_back(self, windows, grad_ref, dmixed_ref):
        rows = self.rows_of(windows)
        for at in self.chunks():
            if self.wo_t is None:
                back = mm_nt(grad_ref[rows, :], self.wo[at, :])
            else:
                back = mm(grad_ref[rows, :], self.wo_t[:, at])
            dmixed_ref[rows, at] = back.astype(BF16)

    def attend_back(self, windows, dmixed_ref, duq_ref, duk_ref, dqkv_ref):
        low = pair_masks()
        ones = jnp.ones((PAD, 128), BF16)
        units = self.units(windows)
        divided = [
            d.astype(F32) * i
            for d, i in zip(self.tiles(dmixed_ref, units), self.tiles(self.inverse, units))
        ]
        shift = [
            stack_pair((-(d * m.astype(F32))).astype(BF16), low)
            for d, m in zip(divided, self.tiles(self.mixed, units))
        ]
        douts = [stack_pair(d.astype(BF16), low) for d in divided]
        queries = [stack_pair(q, low) for q in self.tiles(self.uq, units)]
        keys, values = self.tiles(self.uk, units), self.tiles(self.v, units)
        weights = [self.weights[self.pairs * g + p] for g, p in units]
        dprobs = [
            mm_nt(beside(d, s), beside(v, ones)) for d, s, v in zip(douts, shift, values)
        ]
        dscores = [
            (w.astype(F32) * self.scaled(d, p, 1.0)).astype(BF16)
            for w, d, (g, p) in zip(weights, dprobs, units)
        ]
        dvalues = [mm_tn(w, d) for w, d in zip(weights, douts)]
        dkeys = [mm_tn(d, q) for d, q in zip(dscores, queries)]
        dqueries = [mm(d, k) for d, k in zip(dscores, keys)]
        for n, (g, p) in enumerate(units):
            at = (at_rows(g), at_lanes(p, 128))
            behind = at_lanes(p + 2 * self.pairs, 128)
            dqkv_ref[at_rows(g), behind] = dvalues[n].astype(BF16)
            duk_ref[at] = dkeys[n].astype(BF16)
            duq_ref[at] = pick_pair(dqueries[n], low).astype(BF16)

    def project_back(self, windows, duq_ref, duk_ref, dqkv_ref, dn_ref):
        channels = self.channels
        rows = self.rows_of(windows)
        for at in self.chunks():
            shifted = pl.ds(at.start + channels, 512)
            for u_ref, r_ref, du_ref, to in (
                (self.uq, self.rq, duq_ref, at),
                (self.uk, self.rk, duk_ref, shifted),
            ):
                u = u_ref[rows, at].astype(F32)
                du = du_ref[rows, at].astype(F32)
                inner = self.head_total((u * du).astype(BF16))
                dqkv_ref[rows, to] = (r_ref[rows, at] * (du - u * inner)).astype(BF16)
        for at in self.chunks():
            dquery, dkeyval = dqkv_ref[rows, :channels], dqkv_ref[rows, channels:]
            if self.wq_t is None:
                back = mm_nt(dquery, self.wq[at, :]) + mm_nt(dkeyval, self.wkv[at, :])
            else:
                back = mm(dquery, self.wq_t[:, at]) + mm(dkeyval, self.wkv_t[:, at])
            dn_ref[rows, at] = back

    def norm_backward(self, g, dn):
        dy = dn * self.gain[...]
        xhat = self.xhat[at_rows(g), :]
        rstd = self.rstd[at_rows(g), :][:, :1]
        return rstd * (dy - row_mean(dy) - xhat * row_mean(dy * xhat))


WEIGHTS = (
    "encoder_query",
    "encoder_keyval",
    "encoder_output",
    "merge_weight",
    "coarse_query",
    "coarse_keyval",
    "coarse_output",
    "expand_weight",
    "decoder_query",
    "decoder_keyval",
    "decoder_output",
)


def kept_shapes(rows, channels):
    units = rows // PAD * (channels // 128)
    return [
        ((rows, channels), F32),
        ((rows, 128), F32),
        ((rows, channels), BF16),
        ((rows, channels), BF16),
        ((rows, channels), F32),
        ((rows, channels), F32),
        ((rows, channels), BF16),
        ((units, 2 * PAD, PAD), BF16),
        ((rows, channels), F32),
        ((rows, channels), BF16),
    ]


def scratch_table():
    table = {}
    for block, rows, channels in (("enc", BODY, D), ("dec", BODY, D), ("crs", PAD, DC)):
        table[block] = kept_shapes(rows, channels)
    for kind, rows, channels in (("fine", BODY, D), ("coarse", PAD, DC)):
        table[kind] = [
            ((rows, channels), BF16),
            ((rows, channels), BF16),
            ((rows, channels), BF16),
            ((rows, channels), BF16),
            ((rows, 3 * channels), BF16),
            ((rows, channels), F32),
            ((rows, channels), F32),
            ((rows, channels), BF16),
        ]
    table["misc"] = [
        ((HOME, D), BF16),
        ((HOME, D), BF16),
        ((HOME, D), BF16),
        ((HOME, D), BF16),
        ((BODY, D), F32),
        ((BODY, D), F32),
        ((BODY, D), F32),
        ((PAD, 4 * D), F32),
        ((PAD, 128), F32),
        ((PAD, 4 * D), BF16),
        ((PAD, DC), F32),
        ((PAD, 128), F32),
        ((PAD, 4 * D), BF16),
        ((BODY, D), BF16),
        ((HOME, D), F32),
        ((HOME, D), F32),
        ((HOME * 4, 128), F32),
        ((2, HOME * 4, 128), BF16),
        ((4 * D, DC), BF16),
        ((2 * DC, DC), BF16),
        ((2, 2 * PAD, 128), BF16),
        ((PAD, 128), BF16),
        ((256, 256), BF16),
        ((8, SENT, D), BF16),
        ((8, SENT, D), BF16),
    ]
    return table


TABLE = scratch_table()
NAMES = tuple(TABLE)


def kernel(*refs):
    refs = list(refs)

    def take(n):
        head = refs[:n]
        del refs[:n]
        return head

    fields_in, cot_in = take(2)
    weights_in = take(len(WEIGHTS))
    moves_in = take(12)
    enc_gain, merge_gain, crs_gain, exp_gain, dec_gain = take(5)
    enc_scale, crs_scale, dec_scale = take(3)
    (out_hbm,) = take(1)
    fields_v, cot_v = take(2)
    weights = take(len(WEIGHTS))
    moves = take(12)
    spaces = {name: take(len(TABLE[name])) for name in NAMES}
    local_sem, out_sem, send_sem, recv_sem = take(4)

    lat, lon = lax.axis_index("lat"), lax.axis_index("lon")
    nlat, nlon = lax.axis_size("lat"), lax.axis_size("lon")

    loads = []
    waited = [0]

    def load(*pairs):
        for src, dst in pairs:
            copy = pltpu.make_async_copy(src, dst, local_sem.at[len(loads)])
            copy.start()
            loads.append(copy)

    def loaded(upto):
        while waited[0] < upto:
            loads[waited[0]].wait()
            waited[0] += 1

    def weight(*which):
        return [(weights_in[n], weights[n]) for n in which]

    def move(*which):
        return [(moves_in[n], moves[n]) for n in which]

    load((fields_in, fields_v))

    def device(dlat, dlon):
        return {
            "lat": lax.rem(lat + dlat + nlat, nlat),
            "lon": lax.rem(lon + dlon + nlon, nlon),
        }

    onward = (device(1, 0), device(0, 1), device(1, 1))
    back = (device(-1, 0), device(0, -1), device(-1, -1))
    barrier = pltpu.get_barrier_semaphore()
    for target in onward + back:
        pl.semaphore_signal(
            barrier, inc=1, device_id=target, device_id_type=pl.DeviceIdType.MESH
        )
    load(*move(0, 1), (cot_in, cot_v), *weight(0, 1, 2))

    (
        fields_b,
        fields_rest,
        cot_b,
        cot_rest,
        cot_f,
        gskip,
        planes,
        m_xhat,
        m_rstd,
        merged,
        e_xhat,
        e_rstd,
        dexp,
        out_b,
        out_home,
        grad_home,
        by_cell,
        out_cells,
        expand_t,
        keyval_t,
        bar_q,
        bar_k,
        sums,
        sent,
        received,
    ) = spaces["misc"]

    bar_q[0] = bar_queries(jnp.where(lat == 0, 1, 0))
    bar_q[1] = bar_queries(0)
    bar_k[...] = bar_keys()
    sums[...] = head_sums()

    started = {}

    def prepare(t, source, pick):
        sent[t] = mm(pick[...], source).astype(BF16)

    def launch(t, targets, pieces=(0, 2, 1)):
        started.setdefault(t, [])
        for n in pieces:
            start, size = PIECES[n]
            copy = pltpu.make_async_remote_copy(
                src_ref=sent.at[t, pl.ds(start, size)],
                dst_ref=received.at[t, pl.ds(start, size)],
                send_sem=send_sem.at[t, n],
                recv_sem=recv_sem.at[t, n],
                device_id=targets[n],
                device_id_type=pl.DeviceIdType.MESH,
            )
            copy.start()
            started[t].append(copy)

    def send(t, source, pick, targets):
        far, near = pl.ds(0, 96), pl.ds(96, 64)
        sent[t, far] = mm(pick[far, :], source).astype(BF16)
        launch(t, targets, (0, 2))
        sent[t, near] = mm(pick[near, :], source).astype(BF16)
        launch(t, targets, (1,))

    def arrive(t):
        for copy in started[t]:
            copy.wait_recv()

    def flat(ref, to, rest):
        for n in range(4):
            part = ref[pl.ds(n, HOME, stride=4), :]
            rounded = part.astype(BF16)
            to[:, at_lanes(n, 128)] = rounded
            rest[:, at_lanes(n, 128)] = (part - rounded.astype(F32)).astype(BF16)

    outs = []

    def deliver(own, t, which):
        half = HOME // 2
        for h in range(2):
            rows, cells = pl.ds(h * half, half), pl.ds(4 * h * half, 4 * half)
            x = own[rows, :] + mm(moves[5][rows, :], received[t])
            for n in range(4):
                at = pl.ds(4 * h * half + n, half, stride=4)
                by_cell[at, :] = x[:, 128 * n : 128 * (n + 1)]
            out_cells[which, cells] = by_cell[cells, :].astype(BF16)
            copy = pltpu.make_async_copy(
                out_cells.at[which, cells], out_hbm.at[which, cells], out_sem.at[which, h]
            )
            copy.start()
            outs.append(copy)

    encoder = Block(
        BODY, D, enc_gain, weights[0], weights[1], weights[2], enc_scale, spaces["enc"], sums
    )
    coarse = Block(
        PAD, DC, crs_gain, weights[4], weights[5], weights[6], crs_scale, spaces["crs"], sums
    )
    decoder = Block(
        BODY, D, dec_gain, weights[8], weights[9], weights[10], dec_scale, spaces["dec"], sums
    )
    merge_w, expand_w = weights[3], weights[7]
    coarse.wq_t, coarse.wo_t = (expand_w.at[:, pl.ds(n * DC, DC)] for n in range(2))
    coarse.wkv_t = keyval_t
    merge_t = (weights[4], weights[6])
    fn, fdmixed, fduq, fduk, fdqkv, fdn, fx, fb = spaces["fine"]
    cn, cdmixed, cduq, cduk, cdqkv, cdn, cx, cb = spaces["coarse"]

    def fine_bar(g):
        return bar_q[g // 2]

    def coarse_bar(g):
        return bar_q[0]

    def encode(windows):
        rows = encoder.rows_of(windows)
        encoder.project(windows, fn)
        encoder.attend(windows, fine_bar, bar_k[...])
        section = fx[rows, :] + encoder.branch(windows)
        fx[rows, :] = section
        fb[rows, :] = section.astype(BF16)

    def decode(windows):
        rows = decoder.rows_of(windows)
        for g in windows:
            decoder.norm_rows(g, fx[at_rows(g), :], fn)
        decoder.project(windows, fn)
        decoder.attend(windows, fine_bar, bar_k[...])
        out_b[rows, :] = (fx[rows, :] + decoder.branch(windows)).astype(BF16)
        decoder.attend_back(windows, fdmixed, fduq, fduk, fdqkv)
        decoder.project_back(windows, fduq, fduk, fdqkv, fdn)
        for g in windows:
            at = at_rows(g)
            x = cot_f[at, :] + decoder.norm_backward(g, fdn[at, :])
            gskip[at, :] = x
            fb[at, :] = x.astype(BF16)

    def encode_back(windows):
        encoder.mixed_back(windows, fb, fdmixed)
        encoder.attend_back(windows, fdmixed, fduq, fduk, fdqkv)
        encoder.project_back(windows, fduq, fduk, fdqkv, fdn)
        for g in windows:
            at = at_rows(g)
            x = gskip[at, :] + encoder.norm_backward(g, fdn[at, :])
            fb[at, :] = x.astype(BF16)

    loaded(2)
    flat(fields_v, fields_b, fields_rest)
    prepare(0, fields_b[...], moves[0])
    pl.semaphore_wait(barrier, 6)
    launch(0, onward)
    load(*move(2, 6, 7, 8), *weight(3, 4, 5, 6, 7), *move(9, 10, 11), *weight(8, 9, 10))
    load(*move(3, 4, 5))
    loaded(4)
    fx[...] = mm(moves[1][...], fields_b[...]) + mm(moves[1][...], fields_rest[...])
    flat(cot_v, cot_b, cot_rest)
    prepare(1, cot_b[...], moves[0])
    cot_f[...] = mm(moves[1][...], cot_b[...]) + mm(moves[1][...], cot_rest[...])
    loaded(7)
    encoder.norm_rows(3, fx[at_rows(3), :], fn)
    encode(range(3, 4))
    loaded(8)
    arrive(0)
    launch(1, onward)

    def enter_encoder(g):
        at = at_rows(g)
        x = fx[at, :] + mm(moves[2][at, :], received[0])
        fx[at, :] = x
        encoder.norm_rows(g, x, fn)

    enter_encoder(1)
    enter_encoder(2)
    encode(range(1, 3))

    loaded(11)
    send(2, fb[PAD:, :], moves[6], onward)
    enter_encoder(0)
    encode(range(0, 1))
    planes[...] = mm(moves[7][...], fb[...])
    arrive(1)
    cot = cot_f[...] + mm(moves[2][...], received[1])
    cot_f[...] = cot
    out_b[...] = cot.astype(BF16)
    loaded(16)
    turn(expand_w, expand_t)
    turn(weights[5].at[:, pl.ds(0, DC)], keyval_t.at[pl.ds(0, DC), :])
    arrive(2)
    total = jnp.zeros((PAD, D), F32)
    for p in range(4):
        x = planes[at_rows(p), :] + mm(moves[8][at_rows(p), :], received[2])
        planes[at_rows(p), :] = x
        total += x
    mean = jnp.sum(total, axis=-1, keepdims=True) * (1.0 / (4 * D))
    total = jnp.zeros((PAD, D), F32)
    for p in range(4):
        centred = planes[at_rows(p), :] - mean
        total += centred * centred
    rstd = lax.rsqrt(jnp.sum(total, axis=-1, keepdims=True) * (1.0 / (4 * D)) + EPS)
    m_rstd[...] = jnp.broadcast_to(rstd, (PAD, 128))
    for p in range(4):
        lanes = at_lanes(p, D)
        xhat = (planes[at_rows(p), :] - mean) * rstd
        m_xhat[:, lanes] = xhat
        merged[:, lanes] = (xhat * merge_gain[:, lanes]).astype(BF16)
    cx[...] = mm(merged[...], merge_w[...])
    coarse.norm_rows(0, cx[...], cn)
    coarse.project(coarse.every, cn)
    coarse.attend(coarse.every, coarse_bar, bar_k[...])
    x = cx[...] + coarse.branch(coarse.every)
    centred = x - row_mean(x)
    rstd = lax.rsqrt(row_mean(centred * centred) + EPS)
    xhat = centred * rstd
    e_xhat[...] = xhat
    e_rstd[...] = jnp.broadcast_to(rstd, (PAD, 128))
    cb[...] = (xhat * exp_gain[...]).astype(BF16)
    for p in range(4):
        fb[at_rows(p), :] = mm(cb[...], expand_w[:, at_lanes(p, D)]).astype(BF16)

    loaded(len(loads))
    send(3, fb[...], moves[9], back)
    fx[...] = fx[...] + mm(moves[10][...], fb[...])
    decoder.mixed_back(decoder.every, out_b, fdmixed)
    decode(range(0, 1))
    arrive(3)
    later = pl.ds(PAD, 3 * PAD)
    fx[later, :] = fx[later, :] + mm(moves[11][later, :], received[3])
    decode(range(1, 4))

    send(5, fb[PAD:, :], moves[6], onward)
    planes[...] = mm(moves[7][...], fb[...])
    prepare(4, out_b[: 3 * PAD, :], moves[3])
    turn(weights[6], coarse.wo_t)
    turn(weights[4], coarse.wq_t)
    turn(weights[5].at[:, pl.ds(DC, DC)], keyval_t.at[pl.ds(DC, DC), :])
    for n in range(2):
        turn(merge_w.at[pl.ds(n * DC, DC), :], merge_t[n])
    arrive(5)
    launch(4, back)
    for p in range(4):
        x = planes[at_rows(p), :] + mm(moves[8][at_rows(p), :], received[5])
        dexp[:, at_lanes(p, D)] = x.astype(BF16)
    dy = mm(dexp[...], expand_t[...]) * exp_gain[...]
    xhat = e_xhat[...]
    x = e_rstd[:, :1] * (dy - row_mean(dy) - xhat * row_mean(dy * xhat))
    cx[...] = x
    cb[...] = x.astype(BF16)
    coarse.mixed_back(coarse.every, cb, cdmixed)
    coarse.attend_back(coarse.every, cdmixed, cduq, cduk, cdqkv)
    coarse.project_back(coarse.every, cduq, cduk, cdqkv, cdn)
    cb[...] = (cx[...] + coarse.norm_backward(0, cdn[...])).astype(BF16)
    for p in range(4):
        planes[at_rows(p), :] = mm(cb[...], merge_t[p // 2][:, at_lanes(p % 2, D)])
    total = jnp.zeros((PAD, D), F32)
    weighed = jnp.zeros((PAD, D), F32)
    for p in range(4):
        lanes = at_lanes(p, D)
        dy = planes[at_rows(p), :] * merge_gain[:, lanes]
        total += dy
        weighed += dy * m_xhat[:, lanes]
    mean = jnp.sum(total, axis=-1, keepdims=True) * (1.0 / (4 * D))
    tilt = jnp.sum(weighed, axis=-1, keepdims=True) * (1.0 / (4 * D))
    rstd = m_rstd[:, :1]
    for p in range(4):
        lanes = at_lanes(p, D)
        dy = planes[at_rows(p), :] * merge_gain[:, lanes]
        fb[at_rows(p), :] = (rstd * (dy - mean - m_xhat[:, lanes] * tilt)).astype(BF16)

    send(6, fb[...], moves[9], back)
    x = gskip[...] + mm(moves[10][...], fb[...])
    gskip[...] = x
    fb[at_rows(0), :] = x[:PAD].astype(BF16)
    out_home[...] = mm(moves[4][...], out_b[...])
    encode_back(range(0, 1))
    arrive(6)

    def enter_gradient(windows):
        at = encoder.rows_of(windows)
        x = gskip[at, :] + mm(moves[11][at, :], received[6])
        gskip[at, :] = x
        fb[at, :] = x.astype(BF16)

    enter_gradient(range(1, 3))
    encode_back(range(1, 3))

    send(7, fb[: 3 * PAD, :], moves[3], back)
    enter_gradient(range(3, 4))
    encode_back(range(3, 4))
    arrive(4)
    deliver(out_home, 4, 0)
    grad_home[...] = mm(moves[4][...], fb[...])
    arrive(7)
    deliver(grad_home, 7, 1)
    for t in started:
        for copy in started[t]:
            copy.wait_send()
    for copy in outs:
        copy.wait()


def shards(
    fields,
    cotangent,
    encoder_gain,
    encoder_query,
    encoder_keyval,
    encoder_output,
    encoder_scale,
    merge_gain,
    merge_weight,
    coarse_gain,
    coarse_query,
    coarse_keyval,
    coarse_output,
    coarse_scale,
    expand_gain,
    expand_weight,
    decoder_gain,
    decoder_query,
    decoder_keyval,
    decoder_output,
    decoder_scale,
):
    shape = fields.shape
    weights = (
        encoder_query,
        encoder_keyval,
        encoder_output,
        merge_weight,
        coarse_query,
        coarse_keyval,
        coarse_output,
        expand_weight,
        decoder_query,
        decoder_keyval,
        decoder_output,
    )
    moves = [jnp.asarray(m) for m in all_moves()]
    gains = [
        g.reshape(1, -1)
        for g in (encoder_gain, merge_gain, coarse_gain, expand_gain, decoder_gain)
    ]
    scales = (encoder_scale, coarse_scale, decoder_scale)
    flat = (HOME * 4, 128)
    anywhere = pl.BlockSpec(memory_space=pl.ANY)
    in_vmem = pl.BlockSpec(memory_space=pltpu.VMEM)
    in_smem = pl.BlockSpec(memory_space=pltpu.SMEM)
    scratch = [pltpu.VMEM(flat, F32)] * 2
    scratch += [pltpu.VMEM(w.shape, BF16) for w in weights]
    scratch += [pltpu.VMEM(m.shape, BF16) for m in moves]
    for name in NAMES:
        scratch += [pltpu.VMEM(s, t) for s, t in TABLE[name]]
    scratch += [
        pltpu.SemaphoreType.DMA((2 + len(weights) + len(moves),)),
        pltpu.SemaphoreType.DMA((2, 2)),
        pltpu.SemaphoreType.DMA((8, 3)),
        pltpu.SemaphoreType.DMA((8, 3)),
    ]
    results = pl.pallas_call(
        kernel,
        out_shape=jax.ShapeDtypeStruct((2,) + flat, BF16),
        in_specs=[anywhere] * (2 + len(weights) + len(moves)) + [in_vmem] * 5 + [in_smem] * 3,
        out_specs=anywhere,
        scratch_shapes=scratch,
        compiler_params=pltpu.CompilerParams(
            collective_id=0, has_side_effects=True, vmem_limit_bytes=60 * 1024 * 1024
        ),
    )(
        fields.reshape(flat),
        cotangent.reshape(flat),
        *weights,
        *moves,
        *gains,
        *scales,
    )
    return tuple(results[n].astype(F32).reshape(shape) for n in range(2))


def solution(mesh):
    along = P("lat", "lon", None, None)
    return jax.shard_map(
        shards,
        mesh=mesh,
        in_specs=(along, along) + (P(),) * 19,
        out_specs=(along, along),
        check_vma=False,
    )
```

```python
import functools

import jax
import jax.numpy as jnp
import numpy as np
from jax import lax
from jax.experimental import pallas as pl
from jax.experimental.pallas import tpu as pltpu
from jax.sharding import PartitionSpec as P

WLAT = 6
WLON = 12
EPS = 1e-05
ROWS, COLS = 12, 24
HOME = ROWS * COLS
PAD = 80
BODY = 4 * PAD
CELLS = WLAT * WLON
PIECES = ((0, 64), (96, 64), (64, 32))
SENT = 160
D = 512
DC = 1024
F32 = jnp.float32
BF16 = jnp.bfloat16
LOG2E = 1.4426950408889634


def fine_order(r, c):
    return PAD * (2 * (r // WLAT) + c // WLON) + (r % WLAT) * WLON + c % WLON


def plane_order(r, c):
    return PAD * (2 * (r % 2) + c % 2) + (r // 2) * WLON + c // 2


def home_order(r, c):
    return r * COLS + c


def piece_row(r, c):
    if r >= 9 and c < 18:
        return (r - 9) * 18 + c
    if r < 9 and c >= 18:
        return 96 + r * 6 + (c - 18)
    if r >= 9 and c >= 18:
        return 64 + (r - 9) * 6 + (c - 18)
    return None


def move_matrices(order_a, rows_a, order_b, rows_b):
    pick = np.zeros((SENT, rows_a), np.float32)
    own = np.zeros((rows_b, rows_a), np.float32)
    place = np.zeros((rows_b, SENT), np.float32)
    for r in range(ROWS):
        for c in range(COLS):
            piece = piece_row(r, c)
            if piece is not None:
                pick[piece, order_a(r, c)] = 1
            ra, ca = (r - 3) % ROWS, (c - 6) % COLS
            if r >= 3 and c >= 6:
                own[order_b(r, c), order_a(ra, ca)] = 1
            else:
                place[order_b(r, c), piece_row(ra, ca)] = 1
    return pick, own, place


def all_moves():
    first = move_matrices(home_order, HOME, fine_order, BODY)
    second = move_matrices(fine_order, BODY, plane_order, BODY)
    pick, own, place = first
    moves = [pick, own, place, place.T[:, : 3 * PAD], own.T, pick.T]
    pick, own, place = second
    moves += [pick[:, PAD:], own, place, place.T, own.T, pick.T]
    return [np.ascontiguousarray(m).astype(jnp.bfloat16) for m in moves]


def mm(a, b):
    return lax.dot_general(a, b, (((1,), (0,)), ((), ())), preferred_element_type=F32)


def mm_nt(a, b):
    return lax.dot_general(a, b, (((1,), (1,)), ((), ())), preferred_element_type=F32)


def mm_tn(a, b):
    return lax.dot_general(a, b, (((0,), (0,)), ((), ())), preferred_element_type=F32)


def row_mean(x):
    return jnp.mean(x, axis=-1, keepdims=True)


def at_rows(g, n=PAD):
    if isinstance(g, int):
        return pl.ds(g * n, n)
    return pl.ds(pl.multiple_of(g * n, n), n)


def at_lanes(j, n):
    if isinstance(j, int):
        return pl.ds(j * n, n)
    return pl.ds(pl.multiple_of(j * n, n), n)


def head_sums():
    shape = (256, 256)
    a = lax.broadcasted_iota(jnp.int32, shape, 0) // 64
    b = lax.broadcasted_iota(jnp.int32, shape, 1) // 64
    return jnp.where(a == b, 1.0, 0.0).astype(BF16)


def pair_masks():
    lane = lax.broadcasted_iota(jnp.int32, (PAD, 128), 1)
    return lane < 64


def stack_pair(x, low):
    zero = jnp.zeros_like(x)
    return jnp.concatenate([jnp.where(low, x, zero), jnp.where(low, zero, x)], axis=0)


def pick_pair(x, low):
    return jnp.where(low, x[:PAD], x[PAD:])


def beside(a, b):
    return jnp.concatenate([a, b], axis=1)


def bar_queries(first):
    shape = (2 * PAD, 128)
    q = lax.broadcasted_iota(jnp.int32, shape, 0)
    q = jnp.where(q >= PAD, q - PAD, q)
    lane = lax.broadcasted_iota(jnp.int32, shape, 1)
    upper = jnp.where(q < CELLS // 2, first, 0)
    lower = jnp.where(q < CELLS // 2, 0, first)
    value = jnp.where(lane == 0, upper, jnp.where(lane == 1, lower, 0))
    return jnp.where(lane == 2, 1, value).astype(F32).astype(BF16)


def bar_keys():
    shape = (PAD, 128)
    k = lax.broadcasted_iota(jnp.int32, shape, 0)
    lane = lax.broadcasted_iota(jnp.int32, shape, 1)
    upper = jnp.where(k < CELLS // 2, 1, 0)
    there = jnp.where(k < CELLS, 1, 0)
    value = jnp.where(lane == 0, there - upper, jnp.where(lane == 1, upper, 0))
    value = jnp.where(lane == 2, 1 - there, value)
    return (value * -1024).astype(F32).astype(BF16)


def turn(src, dst):
    rows, cols = src.shape
    for a in range(0, rows, 256):
        for b in range(0, cols, 256):
            dst[pl.ds(b, 256), pl.ds(a, 256)] = src[pl.ds(a, 256), pl.ds(b, 256)].T


class Block:
    def __init__(self, rows, channels, gain, wq, wkv, wo, scale, kept, sums):
        self.rows, self.channels = rows, channels
        self.gain, self.wq, self.wkv, self.wo, self.scale = gain, wq, wkv, wo, scale
        self.xhat, self.rstd, self.uq, self.uk, self.rq, self.rk = kept[:6]
        self.v, self.weights, self.inverse, self.mixed = kept[6:]
        self.sums = sums
        self.wq_t = self.wkv_t = self.wo_t = None
        self.pairs = channels // 128
        self.every = range(rows // PAD)

    def chunks(self):
        return [pl.ds(at, 512) for at in range(0, self.channels, 512)]

    def rows_of(self, windows):
        return pl.ds(PAD * windows.start, PAD * len(windows))

    def units(self, windows):
        return [(g, p) for g in windows for p in range(self.pairs)]

    def tiles(self, ref, units):
        return [ref[at_rows(g), at_lanes(p, 128)] for g, p in units]

    def norm_rows(self, g, x, n_ref):
        centred = x - row_mean(x)
        rstd = lax.rsqrt(row_mean(centred * centred) + EPS)
        xhat = centred * rstd
        self.xhat[at_rows(g), :] = xhat
        self.rstd[at_rows(g), :] = jnp.broadcast_to(rstd, (PAD, 128))
        n_ref[at_rows(g), :] = (xhat * self.gain[...]).astype(BF16)

    def head_total(self, x):
        sums = self.sums[...]
        return beside(mm(x[:, :256], sums), mm(x[:, 256:], sums))

    def project(self, windows, n_ref):
        rows = self.rows_of(windows)

        def unit(weight, at, u_ref, r_ref):
            raw = mm(n_ref[rows, :], weight[:, at]).astype(BF16).astype(F32)
            r = lax.rsqrt(self.head_total((raw * raw).astype(BF16)) + 1.0)
            r_ref[rows, at] = r
            u_ref[rows, at] = (raw * r).astype(BF16)

        for at in self.chunks():
            unit(self.wq, at, self.uq, self.rq)
            unit(self.wkv, at, self.uk, self.rk)
            behind = pl.ds(at.start + self.channels, 512)
            self.v[rows, at] = mm(n_ref[rows, :], self.wkv[:, behind]).astype(BF16)

    def scaled(self, x, p, factor):
        top, bottom = self.scale[2 * p] * factor, self.scale[2 * p + 1] * factor
        return jnp.concatenate([x[:PAD] * top, x[PAD:] * bottom], axis=0)

    def attend(self, windows, barred, bar_key):
        low = pair_masks()
        ones = jnp.ones((PAD, 128), BF16)
        units = self.units(windows)
        queries = [stack_pair(q, low) for q in self.tiles(self.uq, units)]
        keys, values = self.tiles(self.uk, units), self.tiles(self.v, units)
        scores = [
            mm_nt(beside(q, barred(g)), beside(k, bar_key))
            for q, k, (g, p) in zip(queries, keys, units)
        ]
        weights = [
            jnp.exp2(self.scaled(s, p, LOG2E)).astype(BF16)
            for s, (g, p) in zip(scores, units)
        ]
        both = [mm(w, beside(v, ones)) for w, v in zip(weights, values)]
        for n, (g, p) in enumerate(units):
            at = (at_rows(g), at_lanes(p, 128))
            self.weights[self.pairs * g + p] = weights[n]
            inverse = 1.0 / pick_pair(both[n][:, 128:], low)
            self.inverse[at] = inverse
            self.mixed[at] = (pick_pair(both[n][:, :128], low) * inverse).astype(BF16)

    def branch(self, windows):
        return mm(self.mixed[self.rows_of(windows), :], self.wo[...])

    def mixed_back(self, windows, grad_ref, dmixed_ref):
        rows = self.rows_of(windows)
        for at in self.chunks():
            if self.wo_t is None:
                back = mm_nt(grad_ref[rows, :], self.wo[at, :])
            else:
                back = mm(grad_ref[rows, :], self.wo_t[:, at])
            dmixed_ref[rows, at] = back.astype(BF16)

    def attend_back(self, windows, dmixed_ref, duq_ref, duk_ref, dqkv_ref):
        low = pair_masks()
        ones = jnp.ones((PAD, 128), BF16)
        units = self.units(windows)
        divided = [
            d.astype(F32) * i
            for d, i in zip(self.tiles(dmixed_ref, units), self.tiles(self.inverse, units))
        ]
        shift = [
            stack_pair((-(d * m.astype(F32))).astype(BF16), low)
            for d, m in zip(divided, self.tiles(self.mixed, units))
        ]
        douts = [stack_pair(d.astype(BF16), low) for d in divided]
        queries = [stack_pair(q, low) for q in self.tiles(self.uq, units)]
        keys, values = self.tiles(self.uk, units), self.tiles(self.v, units)
        weights = [self.weights[self.pairs * g + p] for g, p in units]
        dprobs = [
            mm_nt(beside(d, s), beside(v, ones)) for d, s, v in zip(douts, shift, values)
        ]
        dscores = [
            (w.astype(F32) * self.scaled(d, p, 1.0)).astype(BF16)
            for w, d, (g, p) in zip(weights, dprobs, units)
        ]
        dvalues = [mm_tn(w, d) for w, d in zip(weights, douts)]
        dkeys = [mm_tn(d, q) for d, q in zip(dscores, queries)]
        dqueries = [mm(d, k) for d, k in zip(dscores, keys)]
        for n, (g, p) in enumerate(units):
            at = (at_rows(g), at_lanes(p, 128))
            behind = at_lanes(p + 2 * self.pairs, 128)
            dqkv_ref[at_rows(g), behind] = dvalues[n].astype(BF16)
            duk_ref[at] = dkeys[n].astype(BF16)
            duq_ref[at] = pick_pair(dqueries[n], low).astype(BF16)

    def project_back(self, windows, duq_ref, duk_ref, dqkv_ref, dn_ref):
        channels = self.channels
        rows = self.rows_of(windows)
        for at in self.chunks():
            shifted = pl.ds(at.start + channels, 512)
            for u_ref, r_ref, du_ref, to in (
                (self.uq, self.rq, duq_ref, at),
                (self.uk, self.rk, duk_ref, shifted),
            ):
                u = u_ref[rows, at].astype(F32)
                du = du_ref[rows, at].astype(F32)
                inner = self.head_total((u * du).astype(BF16))
                dqkv_ref[rows, to] = (r_ref[rows, at] * (du - u * inner)).astype(BF16)
        for at in self.chunks():
            dquery, dkeyval = dqkv_ref[rows, :channels], dqkv_ref[rows, channels:]
            if self.wq_t is None:
                back = mm_nt(dquery, self.wq[at, :]) + mm_nt(dkeyval, self.wkv[at, :])
            else:
                back = mm(dquery, self.wq_t[:, at]) + mm(dkeyval, self.wkv_t[:, at])
            dn_ref[rows, at] = back

    def norm_backward(self, g, dn):
        dy = dn * self.gain[...]
        xhat = self.xhat[at_rows(g), :]
        rstd = self.rstd[at_rows(g), :][:, :1]
        return rstd * (dy - row_mean(dy) - xhat * row_mean(dy * xhat))


WEIGHTS = (
    "encoder_query",
    "encoder_keyval",
    "encoder_output",
    "merge_weight",
    "coarse_query",
    "coarse_keyval",
    "coarse_output",
    "expand_weight",
    "decoder_query",
    "decoder_keyval",
    "decoder_output",
)


def kept_shapes(rows, channels):
    units = rows // PAD * (channels // 128)
    return [
        ((rows, channels), F32),
        ((rows, 128), F32),
        ((rows, channels), BF16),
        ((rows, channels), BF16),
        ((rows, channels), F32),
        ((rows, channels), F32),
        ((rows, channels), BF16),
        ((units, 2 * PAD, PAD), BF16),
        ((rows, channels), F32),
        ((rows, channels), BF16),
    ]


def scratch_table():
    table = {}
    for block, rows, channels in (("enc", BODY, D), ("dec", BODY, D), ("crs", PAD, DC)):
        table[block] = kept_shapes(rows, channels)
    for kind, rows, channels in (("fine", BODY, D), ("coarse", PAD, DC)):
        table[kind] = [
            ((rows, channels), BF16),
            ((rows, channels), BF16),
            ((rows, channels), BF16),
            ((rows, channels), BF16),
            ((rows, 3 * channels), BF16),
            ((rows, channels), F32),
            ((rows, channels), F32),
            ((rows, channels), BF16),
        ]
    table["misc"] = [
        ((HOME, D), BF16),
        ((HOME, D), BF16),
        ((HOME, D), BF16),
        ((HOME, D), BF16),
        ((BODY, D), F32),
        ((BODY, D), F32),
        ((BODY, D), F32),
        ((PAD, 4 * D), F32),
        ((PAD, 128), F32),
        ((PAD, 4 * D), BF16),
        ((PAD, DC), F32),
        ((PAD, 128), F32),
        ((PAD, 4 * D), BF16),
        ((BODY, D), BF16),
        ((HOME, D), F32),
        ((HOME, D), F32),
        ((HOME * 4, 128), F32),
        ((2, HOME * 4, 128), BF16),
        ((4 * D, DC), BF16),
        ((2 * DC, DC), BF16),
        ((2, 2 * PAD, 128), BF16),
        ((PAD, 128), BF16),
        ((256, 256), BF16),
        ((8, SENT, D), BF16),
        ((8, SENT, D), BF16),
    ]
    return table


TABLE = scratch_table()
NAMES = tuple(TABLE)


def kernel(*refs):
    refs = list(refs)

    def take(n):
        head = refs[:n]
        del refs[:n]
        return head

    fields_in, cot_in = take(2)
    weights_in = take(len(WEIGHTS))
    moves_in = take(12)
    enc_gain, merge_gain, crs_gain, exp_gain, dec_gain = take(5)
    enc_scale, crs_scale, dec_scale = take(3)
    (out_hbm,) = take(1)
    fields_v, cot_v = take(2)
    weights = take(len(WEIGHTS))
    moves = take(12)
    spaces = {name: take(len(TABLE[name])) for name in NAMES}
    local_sem, out_sem, send_sem, recv_sem = take(4)

    lat, lon = lax.axis_index("lat"), lax.axis_index("lon")
    nlat, nlon = lax.axis_size("lat"), lax.axis_size("lon")

    loads = []
    waited = [0]

    def load(*pairs):
        for src, dst in pairs:
            copy = pltpu.make_async_copy(src, dst, local_sem.at[len(loads)])
            copy.start()
            loads.append(copy)

    def loaded(upto):
        while waited[0] < upto:
            loads[waited[0]].wait()
            waited[0] += 1

    def weight(*which):
        return [(weights_in[n], weights[n]) for n in which]

    def move(*which):
        return [(moves_in[n], moves[n]) for n in which]

    load((fields_in, fields_v))

    def device(dlat, dlon):
        return {
            "lat": lax.rem(lat + dlat + nlat, nlat),
            "lon": lax.rem(lon + dlon + nlon, nlon),
        }

    onward = (device(1, 0), device(0, 1), device(1, 1))
    back = (device(-1, 0), device(0, -1), device(-1, -1))
    barrier = pltpu.get_barrier_semaphore()
    for target in onward + back:
        pl.semaphore_signal(
            barrier, inc=1, device_id=target, device_id_type=pl.DeviceIdType.MESH
        )
    load(*move(0, 1), (cot_in, cot_v), *weight(0, 1, 2))

    (
        fields_b,
        fields_rest,
        cot_b,
        cot_rest,
        cot_f,
        gskip,
        planes,
        m_xhat,
        m_rstd,
        merged,
        e_xhat,
        e_rstd,
        dexp,
        out_b,
        out_home,
        grad_home,
        by_cell,
        out_cells,
        expand_t,
        keyval_t,
        bar_q,
        bar_k,
        sums,
        sent,
        received,
    ) = spaces["misc"]

    bar_q[0] = bar_queries(jnp.where(lat == 0, 1, 0))
    bar_q[1] = bar_queries(0)
    bar_k[...] = bar_keys()
    sums[...] = head_sums()

    started = {}

    def prepare(t, source, pick):
        sent[t] = mm(pick[...], source).astype(BF16)

    def launch(t, targets, pieces=(0, 2, 1)):
        started.setdefault(t, [])
        for n in pieces:
            start, size = PIECES[n]
            copy = pltpu.make_async_remote_copy(
                src_ref=sent.at[t, pl.ds(start, size)],
                dst_ref=received.at[t, pl.ds(start, size)],
                send_sem=send_sem.at[t, n],
                recv_sem=recv_sem.at[t, n],
                device_id=targets[n],
                device_id_type=pl.DeviceIdType.MESH,
            )
            copy.start()
            started[t].append(copy)

    def send(t, source, pick, targets):
        far, near = pl.ds(0, 96), pl.ds(96, 64)
        sent[t, far] = mm(pick[far, :], source).astype(BF16)
        launch(t, targets, (0, 2))
        sent[t, near] = mm(pick[near, :], source).astype(BF16)
        launch(t, targets, (1,))

    def arrive(t):
        for copy in started[t]:
            copy.wait_recv()

    def flat(ref, to, rest):
        for n in range(4):
            part = ref[pl.ds(n, HOME, stride=4), :]
            rounded = part.astype(BF16)
            to[:, at_lanes(n, 128)] = rounded
            rest[:, at_lanes(n, 128)] = (part - rounded.astype(F32)).astype(BF16)

    outs = []

    def deliver(own, t, which):
        half = HOME // 2
        for h in range(2):
            rows, cells = pl.ds(h * half, half), pl.ds(4 * h * half, 4 * half)
            x = own[rows, :] + mm(moves[5][rows, :], received[t])
            for n in range(4):
                at = pl.ds(4 * h * half + n, half, stride=4)
                by_cell[at, :] = x[:, 128 * n : 128 * (n + 1)]
            out_cells[which, cells] = by_cell[cells, :].astype(BF16)
            copy = pltpu.make_async_copy(
                out_cells.at[which, cells], out_hbm.at[which, cells], out_sem.at[which, h]
            )
            copy.start()
            outs.append(copy)

    encoder = Block(
        BODY, D, enc_gain, weights[0], weights[1], weights[2], enc_scale, spaces["enc"], sums
    )
    coarse = Block(
        PAD, DC, crs_gain, weights[4], weights[5], weights[6], crs_scale, spaces["crs"], sums
    )
    decoder = Block(
        BODY, D, dec_gain, weights[8], weights[9], weights[10], dec_scale, spaces["dec"], sums
    )
    merge_w, expand_w = weights[3], weights[7]
    coarse.wq_t, coarse.wo_t = (expand_w.at[:, pl.ds(n * DC, DC)] for n in range(2))
    coarse.wkv_t = keyval_t
    merge_t = (weights[4], weights[6])
    fn, fdmixed, fduq, fduk, fdqkv, fdn, fx, fb = spaces["fine"]
    cn, cdmixed, cduq, cduk, cdqkv, cdn, cx, cb = spaces["coarse"]

    def fine_bar(g):
        return bar_q[g // 2]

    def coarse_bar(g):
        return bar_q[0]

    def encode(windows):
        rows = encoder.rows_of(windows)
        encoder.project(windows, fn)
        encoder.attend(windows, fine_bar, bar_k[...])
        section = fx[rows, :] + encoder.branch(windows)
        fx[rows, :] = section
        fb[rows, :] = section.astype(BF16)

    def decode(windows):
        rows = decoder.rows_of(windows)
        for g in windows:
            decoder.norm_rows(g, fx[at_rows(g), :], fn)
        decoder.project(windows, fn)
        decoder.attend(windows, fine_bar, bar_k[...])
        out_b[rows, :] = (fx[rows, :] + decoder.branch(windows)).astype(BF16)
        decoder.attend_back(windows, fdmixed, fduq, fduk, fdqkv)
        decoder.project_back(windows, fduq, fduk, fdqkv, fdn)
        for g in windows:
            at = at_rows(g)
            x = cot_f[at, :] + decoder.norm_backward(g, fdn[at, :])
            gskip[at, :] = x
            fb[at, :] = x.astype(BF16)

    def encode_back(windows):
        encoder.mixed_back(windows, fb, fdmixed)
        encoder.attend_back(windows, fdmixed, fduq, fduk, fdqkv)
        encoder.project_back(windows, fduq, fduk, fdqkv, fdn)
        for g in windows:
            at = at_rows(g)
            x = gskip[at, :] + encoder.norm_backward(g, fdn[at, :])
            fb[at, :] = x.astype(BF16)

    loaded(2)
    flat(fields_v, fields_b, fields_rest)
    prepare(0, fields_b[...], moves[0])
    pl.semaphore_wait(barrier, 6)
    launch(0, onward)
    load(*move(2, 6, 7, 8), *weight(3, 4, 5, 6, 7), *move(9, 10, 11), *weight(8, 9, 10))
    load(*move(3, 4, 5))
    loaded(4)
    fx[...] = mm(moves[1][...], fields_b[...]) + mm(moves[1][...], fields_rest[...])
    flat(cot_v, cot_b, cot_rest)
    prepare(1, cot_b[...], moves[0])
    cot_f[...] = mm(moves[1][...], cot_b[...]) + mm(moves[1][...], cot_rest[...])
    loaded(7)
    encoder.norm_rows(3, fx[at_rows(3), :], fn)
    encode(range(3, 4))
    loaded(8)
    arrive(0)

    def enter_encoder(g):
        at = at_rows(g)
        x = fx[at, :] + mm(moves[2][at, :], received[0])
        fx[at, :] = x
        encoder.norm_rows(g, x, fn)

    enter_encoder(1)
    enter_encoder(2)
    encode(range(1, 3))

    loaded(11)
    send(2, fb[PAD:, :], moves[6], onward)
    enter_encoder(0)
    encode(range(0, 1))
    planes[...] = mm(moves[7][...], fb[...])
    loaded(16)
    turn(expand_w, expand_t)
    turn(weights[5].at[:, pl.ds(0, DC)], keyval_t.at[pl.ds(0, DC), :])
    arrive(2)
    launch(1, onward)
    total = jnp.zeros((PAD, D), F32)
    for p in range(4):
        x = planes[at_rows(p), :] + mm(moves[8][at_rows(p), :], received[2])
        planes[at_rows(p), :] = x
        total += x
    mean = jnp.sum(total, axis=-1, keepdims=True) * (1.0 / (4 * D))
    total = jnp.zeros((PAD, D), F32)
    for p in range(4):
        centred = planes[at_rows(p), :] - mean
        total += centred * centred
    rstd = lax.rsqrt(jnp.sum(total, axis=-1, keepdims=True) * (1.0 / (4 * D)) + EPS)
    m_rstd[...] = jnp.broadcast_to(rstd, (PAD, 128))
    for p in range(4):
        lanes = at_lanes(p, D)
        xhat = (planes[at_rows(p), :] - mean) * rstd
        m_xhat[:, lanes] = xhat
        merged[:, lanes] = (xhat * merge_gain[:, lanes]).astype(BF16)
    cx[...] = mm(merged[...], merge_w[...])
    coarse.norm_rows(0, cx[...], cn)
    coarse.project(coarse.every, cn)
    coarse.attend(coarse.every, coarse_bar, bar_k[...])
    x = cx[...] + coarse.branch(coarse.every)
    centred = x - row_mean(x)
    rstd = lax.rsqrt(row_mean(centred * centred) + EPS)
    xhat = centred * rstd
    e_xhat[...] = xhat
    e_rstd[...] = jnp.broadcast_to(rstd, (PAD, 128))
    cb[...] = (xhat * exp_gain[...]).astype(BF16)
    for p in range(4):
        fb[at_rows(p), :] = mm(cb[...], expand_w[:, at_lanes(p, D)]).astype(BF16)

    loaded(len(loads))
    send(3, fb[...], moves[9], back)
    fx[...] = fx[...] + mm(moves[10][...], fb[...])
    arrive(1)
    cot = cot_f[...] + mm(moves[2][...], received[1])
    cot_f[...] = cot
    out_b[...] = cot.astype(BF16)
    decoder.mixed_back(decoder.every, out_b, fdmixed)
    decode(range(0, 1))
    arrive(3)
    later = pl.ds(PAD, 3 * PAD)
    fx[later, :] = fx[later, :] + mm(moves[11][later, :], received[3])
    decode(range(1, 4))

    send(5, fb[PAD:, :], moves[6], onward)
    planes[...] = mm(moves[7][...], fb[...])
    prepare(4, out_b[: 3 * PAD, :], moves[3])
    turn(weights[6], coarse.wo_t)
    turn(weights[4], coarse.wq_t)
    turn(weights[5].at[:, pl.ds(DC, DC)], keyval_t.at[pl.ds(DC, DC), :])
    for n in range(2):
        turn(merge_w.at[pl.ds(n * DC, DC), :], merge_t[n])
    arrive(5)
    launch(4, back)
    for p in range(4):
        x = planes[at_rows(p), :] + mm(moves[8][at_rows(p), :], received[5])
        dexp[:, at_lanes(p, D)] = x.astype(BF16)
    dy = mm(dexp[...], expand_t[...]) * exp_gain[...]
    xhat = e_xhat[...]
    x = e_rstd[:, :1] * (dy - row_mean(dy) - xhat * row_mean(dy * xhat))
    cx[...] = x
    cb[...] = x.astype(BF16)
    coarse.mixed_back(coarse.every, cb, cdmixed)
    coarse.attend_back(coarse.every, cdmixed, cduq, cduk, cdqkv)
    coarse.project_back(coarse.every, cduq, cduk, cdqkv, cdn)
    cb[...] = (cx[...] + coarse.norm_backward(0, cdn[...])).astype(BF16)
    for p in range(4):
        planes[at_rows(p), :] = mm(cb[...], merge_t[p // 2][:, at_lanes(p % 2, D)])
    total = jnp.zeros((PAD, D), F32)
    weighed = jnp.zeros((PAD, D), F32)
    for p in range(4):
        lanes = at_lanes(p, D)
        dy = planes[at_rows(p), :] * merge_gain[:, lanes]
        total += dy
        weighed += dy * m_xhat[:, lanes]
    mean = jnp.sum(total, axis=-1, keepdims=True) * (1.0 / (4 * D))
    tilt = jnp.sum(weighed, axis=-1, keepdims=True) * (1.0 / (4 * D))
    rstd = m_rstd[:, :1]
    for p in range(4):
        lanes = at_lanes(p, D)
        dy = planes[at_rows(p), :] * merge_gain[:, lanes]
        fb[at_rows(p), :] = (rstd * (dy - mean - m_xhat[:, lanes] * tilt)).astype(BF16)

    send(6, fb[...], moves[9], back)
    x = gskip[...] + mm(moves[10][...], fb[...])
    gskip[...] = x
    fb[at_rows(0), :] = x[:PAD].astype(BF16)
    out_home[...] = mm(moves[4][...], out_b[...])
    encode_back(range(0, 1))
    encoder.wq_t, encoder.wo_t = weights[8], weights[10]
    encoder.wkv_t = keyval_t.at[pl.ds(0, 2 * D), pl.ds(0, D)]
    turn(weights[0], encoder.wq_t)
    turn(weights[1], encoder.wkv_t)
    turn(weights[2], encoder.wo_t)
    arrive(6)

    def enter_gradient(windows):
        at = encoder.rows_of(windows)
        x = gskip[at, :] + mm(moves[11][at, :], received[6])
        gskip[at, :] = x
        fb[at, :] = x.astype(BF16)

    enter_gradient(range(1, 3))
    encode_back(range(1, 3))

    send(7, fb[: 3 * PAD, :], moves[3], back)
    enter_gradient(range(3, 4))
    encode_back(range(3, 4))
    arrive(4)
    deliver(out_home, 4, 0)
    grad_home[...] = mm(moves[4][...], fb[...])
    arrive(7)
    deliver(grad_home, 7, 1)
    for t in started:
        for copy in started[t]:
            copy.wait_send()
    for copy in outs:
        copy.wait()


def shards(
    fields,
    cotangent,
    encoder_gain,
    encoder_query,
    encoder_keyval,
    encoder_output,
    encoder_scale,
    merge_gain,
    merge_weight,
    coarse_gain,
    coarse_query,
    coarse_keyval,
    coarse_output,
    coarse_scale,
    expand_gain,
    expand_weight,
    decoder_gain,
    decoder_query,
    decoder_keyval,
    decoder_output,
    decoder_scale,
):
    shape = fields.shape
    weights = (
        encoder_query,
        encoder_keyval,
        encoder_output,
        merge_weight,
        coarse_query,
        coarse_keyval,
        coarse_output,
        expand_weight,
        decoder_query,
        decoder_keyval,
        decoder_output,
    )
    moves = [jnp.asarray(m) for m in all_moves()]
    gains = [
        g.reshape(1, -1)
        for g in (encoder_gain, merge_gain, coarse_gain, expand_gain, decoder_gain)
    ]
    scales = (encoder_scale, coarse_scale, decoder_scale)
    flat = (HOME * 4, 128)
    anywhere = pl.BlockSpec(memory_space=pl.ANY)
    in_vmem = pl.BlockSpec(memory_space=pltpu.VMEM)
    in_smem = pl.BlockSpec(memory_space=pltpu.SMEM)
    scratch = [pltpu.VMEM(flat, F32)] * 2
    scratch += [pltpu.VMEM(w.shape, BF16) for w in weights]
    scratch += [pltpu.VMEM(m.shape, BF16) for m in moves]
    for name in NAMES:
        scratch += [pltpu.VMEM(s, t) for s, t in TABLE[name]]
    scratch += [
        pltpu.SemaphoreType.DMA((2 + len(weights) + len(moves),)),
        pltpu.SemaphoreType.DMA((2, 2)),
        pltpu.SemaphoreType.DMA((8, 3)),
        pltpu.SemaphoreType.DMA((8, 3)),
    ]
    results = pl.pallas_call(
        kernel,
        out_shape=jax.ShapeDtypeStruct((2,) + flat, BF16),
        in_specs=[anywhere] * (2 + len(weights) + len(moves)) + [in_vmem] * 5 + [in_smem] * 3,
        out_specs=anywhere,
        scratch_shapes=scratch,
        compiler_params=pltpu.CompilerParams(
            collective_id=0, has_side_effects=True, vmem_limit_bytes=60 * 1024 * 1024
        ),
    )(
        fields.reshape(flat),
        cotangent.reshape(flat),
        *weights,
        *moves,
        *gains,
        *scales,
    )
    return tuple(results[n].astype(F32).reshape(shape) for n in range(2))


def solution(mesh):
    along = P("lat", "lon", None, None)
    return jax.shard_map(
        shards,
        mesh=mesh,
        in_specs=(along, along) + (P(),) * 19,
        out_specs=(along, along),
        check_vma=False,
    )
```

```python
import functools

import jax
import jax.numpy as jnp
import numpy as np
from jax import lax
from jax.experimental import pallas as pl
from jax.experimental.pallas import tpu as pltpu
from jax.sharding import PartitionSpec as P

WLAT = 6
WLON = 12
EPS = 1e-05
ROWS, COLS = 12, 24
HOME = ROWS * COLS
PAD = 80
BODY = 4 * PAD
CELLS = WLAT * WLON
PIECES = ((0, 64), (96, 64), (64, 32))
SENT = 160
D = 512
DC = 1024
F32 = jnp.float32
BF16 = jnp.bfloat16
LOG2E = 1.4426950408889634


def fine_order(r, c):
    return PAD * (2 * (r // WLAT) + c // WLON) + (r % WLAT) * WLON + c % WLON


def plane_order(r, c):
    return PAD * (2 * (r % 2) + c % 2) + (r // 2) * WLON + c // 2


def home_order(r, c):
    return r * COLS + c


def piece_row(r, c):
    if r >= 9 and c < 18:
        return (r - 9) * 18 + c
    if r < 9 and c >= 18:
        return 96 + r * 6 + (c - 18)
    if r >= 9 and c >= 18:
        return 64 + (r - 9) * 6 + (c - 18)
    return None


def move_matrices(order_a, rows_a, order_b, rows_b):
    pick = np.zeros((SENT, rows_a), np.float32)
    own = np.zeros((rows_b, rows_a), np.float32)
    place = np.zeros((rows_b, SENT), np.float32)
    for r in range(ROWS):
        for c in range(COLS):
            piece = piece_row(r, c)
            if piece is not None:
                pick[piece, order_a(r, c)] = 1
            ra, ca = (r - 3) % ROWS, (c - 6) % COLS
            if r >= 3 and c >= 6:
                own[order_b(r, c), order_a(ra, ca)] = 1
            else:
                place[order_b(r, c), piece_row(ra, ca)] = 1
    return pick, own, place


def all_moves():
    first = move_matrices(home_order, HOME, fine_order, BODY)
    second = move_matrices(fine_order, BODY, plane_order, BODY)
    pick, own, place = first
    moves = [pick, own, place, place.T[:, : 3 * PAD], own.T, pick.T]
    pick, own, place = second
    moves += [pick[:, PAD:], own, place, place.T, own.T, pick.T]
    return [np.ascontiguousarray(m).astype(jnp.bfloat16) for m in moves]


def mm(a, b):
    return lax.dot_general(a, b, (((1,), (0,)), ((), ())), preferred_element_type=F32)


def mm_nt(a, b):
    return lax.dot_general(a, b, (((1,), (1,)), ((), ())), preferred_element_type=F32)


def mm_tn(a, b):
    return lax.dot_general(a, b, (((0,), (0,)), ((), ())), preferred_element_type=F32)


def row_mean(x):
    return jnp.mean(x, axis=-1, keepdims=True)


def at_rows(g, n=PAD):
    if isinstance(g, int):
        return pl.ds(g * n, n)
    return pl.ds(pl.multiple_of(g * n, n), n)


def at_lanes(j, n):
    if isinstance(j, int):
        return pl.ds(j * n, n)
    return pl.ds(pl.multiple_of(j * n, n), n)


def head_sums():
    shape = (256, 256)
    a = lax.broadcasted_iota(jnp.int32, shape, 0) // 64
    b = lax.broadcasted_iota(jnp.int32, shape, 1) // 64
    return jnp.where(a == b, 1.0, 0.0).astype(BF16)


def pair_masks():
    lane = lax.broadcasted_iota(jnp.int32, (PAD, 128), 1)
    return lane < 64


def stack_pair(x, low):
    zero = jnp.zeros_like(x)
    return jnp.concatenate([jnp.where(low, x, zero), jnp.where(low, zero, x)], axis=0)


def pick_pair(x, low):
    return jnp.where(low, x[:PAD], x[PAD:])


def beside(a, b):
    return jnp.concatenate([a, b], axis=1)


def bar_queries(first):
    shape = (2 * PAD, 128)
    q = lax.broadcasted_iota(jnp.int32, shape, 0)
    q = jnp.where(q >= PAD, q - PAD, q)
    lane = lax.broadcasted_iota(jnp.int32, shape, 1)
    upper = jnp.where(q < CELLS // 2, first, 0)
    lower = jnp.where(q < CELLS // 2, 0, first)
    value = jnp.where(lane == 0, upper, jnp.where(lane == 1, lower, 0))
    return jnp.where(lane == 2, 1, value).astype(F32).astype(BF16)


def bar_keys():
    shape = (PAD, 128)
    k = lax.broadcasted_iota(jnp.int32, shape, 0)
    lane = lax.broadcasted_iota(jnp.int32, shape, 1)
    upper = jnp.where(k < CELLS // 2, 1, 0)
    there = jnp.where(k < CELLS, 1, 0)
    value = jnp.where(lane == 0, there - upper, jnp.where(lane == 1, upper, 0))
    value = jnp.where(lane == 2, 1 - there, value)
    return (value * -1024).astype(F32).astype(BF16)


def turn(src, dst):
    rows, cols = src.shape
    for a in range(0, rows, 256):
        for b in range(0, cols, 256):
            dst[pl.ds(b, 256), pl.ds(a, 256)] = src[pl.ds(a, 256), pl.ds(b, 256)].T


class Block:
    def __init__(self, rows, channels, gain, wq, wkv, wo, scale, kept, sums):
        self.rows, self.channels = rows, channels
        self.gain, self.wq, self.wkv, self.wo, self.scale = gain, wq, wkv, wo, scale
        self.xhat, self.rstd, self.uq, self.uk, self.rq, self.rk = kept[:6]
        self.v, self.weights, self.inverse, self.mixed = kept[6:]
        self.sums = sums
        self.wq_t = self.wkv_t = self.wo_t = None
        self.pairs = channels // 128
        self.every = range(rows // PAD)

    def chunks(self):
        return [pl.ds(at, 512) for at in range(0, self.channels, 512)]

    def rows_of(self, windows):
        return pl.ds(PAD * windows.start, PAD * len(windows))

    def units(self, windows):
        return [(g, p) for g in windows for p in range(self.pairs)]

    def tiles(self, ref, units):
        return [ref[at_rows(g), at_lanes(p, 128)] for g, p in units]

    def norm_rows(self, g, x, n_ref):
        centred = x - row_mean(x)
        rstd = lax.rsqrt(row_mean(centred * centred) + EPS)
        xhat = centred * rstd
        self.xhat[at_rows(g), :] = xhat
        self.rstd[at_rows(g), :] = jnp.broadcast_to(rstd, (PAD, 128))
        n_ref[at_rows(g), :] = (xhat * self.gain[...]).astype(BF16)

    def head_total(self, x):
        sums = self.sums[...]
        return beside(mm(x[:, :256], sums), mm(x[:, 256:], sums))

    def project(self, windows, n_ref):
        rows = self.rows_of(windows)

        def unit(weight, at, u_ref, r_ref):
            raw = mm(n_ref[rows, :], weight[:, at]).astype(BF16).astype(F32)
            r = lax.rsqrt(self.head_total((raw * raw).astype(BF16)) + 1.0)
            r_ref[rows, at] = r
            u_ref[rows, at] = (raw * r).astype(BF16)

        for at in self.chunks():
            unit(self.wq, at, self.uq, self.rq)
            unit(self.wkv, at, self.uk, self.rk)
            behind = pl.ds(at.start + self.channels, 512)
            self.v[rows, at] = mm(n_ref[rows, :], self.wkv[:, behind]).astype(BF16)

    def scaled(self, x, p, factor):
        top, bottom = self.scale[2 * p] * factor, self.scale[2 * p + 1] * factor
        return jnp.concatenate([x[:PAD] * top, x[PAD:] * bottom], axis=0)

    def attend(self, windows, barred, bar_key):
        low = pair_masks()
        ones = jnp.ones((PAD, 128), BF16)
        units = self.units(windows)
        queries = [stack_pair(q, low) for q in self.tiles(self.uq, units)]
        keys, values = self.tiles(self.uk, units), self.tiles(self.v, units)
        scores = [
            mm_nt(beside(q, barred(g)), beside(k, bar_key))
            for q, k, (g, p) in zip(queries, keys, units)
        ]
        weights = [
            jnp.exp2(self.scaled(s, p, LOG2E)).astype(BF16)
            for s, (g, p) in zip(scores, units)
        ]
        both = [mm(w, beside(v, ones)) for w, v in zip(weights, values)]
        for n, (g, p) in enumerate(units):
            at = (at_rows(g), at_lanes(p, 128))
            self.weights[self.pairs * g + p] = weights[n]
            inverse = 1.0 / pick_pair(both[n][:, 128:], low)
            self.inverse[at] = inverse
            self.mixed[at] = (pick_pair(both[n][:, :128], low) * inverse).astype(BF16)

    def branch(self, windows):
        return mm(self.mixed[self.rows_of(windows), :], self.wo[...])

    def mixed_back(self, windows, grad_ref, dmixed_ref):
        rows = self.rows_of(windows)
        for at in self.chunks():
            if self.wo_t is None:
                back = mm_nt(grad_ref[rows, :], self.wo[at, :])
            else:
                back = mm(grad_ref[rows, :], self.wo_t[:, at])
            dmixed_ref[rows, at] = back.astype(BF16)

    def attend_back(self, windows, dmixed_ref, duq_ref, duk_ref, dqkv_ref):
        low = pair_masks()
        ones = jnp.ones((PAD, 128), BF16)
        units = self.units(windows)
        divided = [
            d.astype(F32) * i
            for d, i in zip(self.tiles(dmixed_ref, units), self.tiles(self.inverse, units))
        ]
        shift = [
            stack_pair((-(d * m.astype(F32))).astype(BF16), low)
            for d, m in zip(divided, self.tiles(self.mixed, units))
        ]
        douts = [stack_pair(d.astype(BF16), low) for d in divided]
        queries = [stack_pair(q, low) for q in self.tiles(self.uq, units)]
        keys, values = self.tiles(self.uk, units), self.tiles(self.v, units)
        weights = [self.weights[self.pairs * g + p] for g, p in units]
        dprobs = [
            mm_nt(beside(d, s), beside(v, ones)) for d, s, v in zip(douts, shift, values)
        ]
        dscores = [
            (w.astype(F32) * self.scaled(d, p, 1.0)).astype(BF16)
            for w, d, (g, p) in zip(weights, dprobs, units)
        ]
        dvalues = [mm_tn(w, d) for w, d in zip(weights, douts)]
        dkeys = [mm_tn(d, q) for d, q in zip(dscores, queries)]
        dqueries = [mm(d, k) for d, k in zip(dscores, keys)]
        for n, (g, p) in enumerate(units):
            at = (at_rows(g), at_lanes(p, 128))
            behind = at_lanes(p + 2 * self.pairs, 128)
            dqkv_ref[at_rows(g), behind] = dvalues[n].astype(BF16)
            duk_ref[at] = dkeys[n].astype(BF16)
            duq_ref[at] = pick_pair(dqueries[n], low).astype(BF16)

    def project_back(self, windows, duq_ref, duk_ref, dqkv_ref, dn_ref):
        channels = self.channels
        rows = self.rows_of(windows)
        for at in self.chunks():
            shifted = pl.ds(at.start + channels, 512)
            for u_ref, r_ref, du_ref, to in (
                (self.uq, self.rq, duq_ref, at),
                (self.uk, self.rk, duk_ref, shifted),
            ):
                u = u_ref[rows, at].astype(F32)
                du = du_ref[rows, at].astype(F32)
                inner = self.head_total((u * du).astype(BF16))
                dqkv_ref[rows, to] = (r_ref[rows, at] * (du - u * inner)).astype(BF16)
        for at in self.chunks():
            dquery, dkeyval = dqkv_ref[rows, :channels], dqkv_ref[rows, channels:]
            if self.wq_t is None:
                back = mm_nt(dquery, self.wq[at, :]) + mm_nt(dkeyval, self.wkv[at, :])
            else:
                back = mm(dquery, self.wq_t[:, at]) + mm(dkeyval, self.wkv_t[:, at])
            dn_ref[rows, at] = back

    def norm_backward(self, g, dn):
        dy = dn * self.gain[...]
        xhat = self.xhat[at_rows(g), :]
        rstd = self.rstd[at_rows(g), :][:, :1]
        return rstd * (dy - row_mean(dy) - xhat * row_mean(dy * xhat))


WEIGHTS = (
    "encoder_query",
    "encoder_keyval",
    "encoder_output",
    "merge_weight",
    "coarse_query",
    "coarse_keyval",
    "coarse_output",
    "expand_weight",
    "decoder_query",
    "decoder_keyval",
    "decoder_output",
)


def kept_shapes(rows, channels):
    units = rows // PAD * (channels // 128)
    return [
        ((rows, channels), F32),
        ((rows, 128), F32),
        ((rows, channels), BF16),
        ((rows, channels), BF16),
        ((rows, channels), F32),
        ((rows, channels), F32),
        ((rows, channels), BF16),
        ((units, 2 * PAD, PAD), BF16),
        ((rows, channels), F32),
        ((rows, channels), BF16),
    ]


def scratch_table():
    table = {}
    for block, rows, channels in (("enc", BODY, D), ("dec", BODY, D), ("crs", PAD, DC)):
        table[block] = kept_shapes(rows, channels)
    for kind, rows, channels in (("fine", BODY, D), ("coarse", PAD, DC)):
        table[kind] = [
            ((rows, channels), BF16),
            ((rows, channels), BF16),
            ((rows, channels), BF16),
            ((rows, channels), BF16),
            ((rows, 3 * channels), BF16),
            ((rows, channels), F32),
            ((rows, channels), F32),
            ((rows, channels), BF16),
        ]
    table["misc"] = [
        ((HOME, D), BF16),
        ((HOME, D), BF16),
        ((HOME, D), BF16),
        ((HOME, D), BF16),
        ((BODY, D), F32),
        ((BODY, D), F32),
        ((BODY, D), F32),
        ((PAD, 4 * D), F32),
        ((PAD, 128), F32),
        ((PAD, 4 * D), BF16),
        ((PAD, DC), F32),
        ((PAD, 128), F32),
        ((PAD, 4 * D), BF16),
        ((BODY, D), BF16),
        ((HOME, D), F32),
        ((HOME, D), F32),
        ((HOME * 4, 128), F32),
        ((2, HOME * 4, 128), BF16),
        ((4 * D, DC), BF16),
        ((2 * DC, DC), BF16),
        ((2, 2 * PAD, 128), BF16),
        ((PAD, 128), BF16),
        ((256, 256), BF16),
        ((8, SENT, D), BF16),
        ((8, SENT, D), BF16),
    ]
    return table


TABLE = scratch_table()
NAMES = tuple(TABLE)


def kernel(*refs):
    refs = list(refs)

    def take(n):
        head = refs[:n]
        del refs[:n]
        return head

    fields_in, cot_in = take(2)
    weights_in = take(len(WEIGHTS))
    moves_in = take(12)
    enc_gain, merge_gain, crs_gain, exp_gain, dec_gain = take(5)
    enc_scale, crs_scale, dec_scale = take(3)
    (out_hbm,) = take(1)
    fields_v, cot_v = take(2)
    weights = take(len(WEIGHTS))
    moves = take(12)
    spaces = {name: take(len(TABLE[name])) for name in NAMES}
    local_sem, out_sem, send_sem, recv_sem = take(4)

    lat, lon = lax.axis_index("lat"), lax.axis_index("lon")
    nlat, nlon = lax.axis_size("lat"), lax.axis_size("lon")

    loads = []
    waited = [0]

    def load(*pairs):
        for src, dst in pairs:
            copy = pltpu.make_async_copy(src, dst, local_sem.at[len(loads)])
            copy.start()
            loads.append(copy)

    def loaded(upto):
        while waited[0] < upto:
            loads[waited[0]].wait()
            waited[0] += 1

    def weight(*which):
        return [(weights_in[n], weights[n]) for n in which]

    def move(*which):
        return [(moves_in[n], moves[n]) for n in which]

    load((fields_in, fields_v))

    def device(dlat, dlon):
        return {
            "lat": lax.rem(lat + dlat + nlat, nlat),
            "lon": lax.rem(lon + dlon + nlon, nlon),
        }

    onward = (device(1, 0), device(0, 1), device(1, 1))
    back = (device(-1, 0), device(0, -1), device(-1, -1))
    barrier = pltpu.get_barrier_semaphore()
    for target in onward + back:
        pl.semaphore_signal(
            barrier, inc=1, device_id=target, device_id_type=pl.DeviceIdType.MESH
        )
    load(*move(0, 1), (cot_in, cot_v), *weight(0, 1, 2))

    (
        fields_b,
        fields_rest,
        cot_b,
        cot_rest,
        cot_f,
        gskip,
        planes,
        m_xhat,
        m_rstd,
        merged,
        e_xhat,
        e_rstd,
        dexp,
        out_b,
        out_home,
        grad_home,
        by_cell,
        out_cells,
        expand_t,
        keyval_t,
        bar_q,
        bar_k,
        sums,
        sent,
        received,
    ) = spaces["misc"]

    bar_q[0] = bar_queries(jnp.where(lat == 0, 1, 0))
    bar_q[1] = bar_queries(0)
    bar_k[...] = bar_keys()
    sums[...] = head_sums()

    started = {}

    def prepare(t, source, pick):
        sent[t] = mm(pick[...], source).astype(BF16)

    def launch(t, targets, pieces=(0, 2, 1)):
        started.setdefault(t, [])
        for n in pieces:
            start, size = PIECES[n]
            copy = pltpu.make_async_remote_copy(
                src_ref=sent.at[t, pl.ds(start, size)],
                dst_ref=received.at[t, pl.ds(start, size)],
                send_sem=send_sem.at[t, n],
                recv_sem=recv_sem.at[t, n],
                device_id=targets[n],
                device_id_type=pl.DeviceIdType.MESH,
            )
            copy.start()
            started[t].append(copy)

    def send(t, source, pick, targets):
        far, near = pl.ds(0, 96), pl.ds(96, 64)
        sent[t, far] = mm(pick[far, :], source).astype(BF16)
        launch(t, targets, (0, 2))
        sent[t, near] = mm(pick[near, :], source).astype(BF16)
        launch(t, targets, (1,))

    def arrive(t):
        for copy in started[t]:
            copy.wait_recv()

    def flat(ref, to, rest):
        for n in range(4):
            part = ref[pl.ds(n, HOME, stride=4), :]
            rounded = part.astype(BF16)
            to[:, at_lanes(n, 128)] = rounded
            rest[:, at_lanes(n, 128)] = (part - rounded.astype(F32)).astype(BF16)

    outs = []

    def deliver(own, t, which):
        half = HOME // 2
        for h in range(2):
            rows, cells = pl.ds(h * half, half), pl.ds(4 * h * half, 4 * half)
            x = own[rows, :] + mm(moves[5][rows, :], received[t])
            for n in range(4):
                at = pl.ds(4 * h * half + n, half, stride=4)
                by_cell[at, :] = x[:, 128 * n : 128 * (n + 1)]
            out_cells[which, cells] = by_cell[cells, :].astype(BF16)
            copy = pltpu.make_async_copy(
                out_cells.at[which, cells], out_hbm.at[which, cells], out_sem.at[which, h]
            )
            copy.start()
            outs.append(copy)

    encoder = Block(
        BODY, D, enc_gain, weights[0], weights[1], weights[2], enc_scale, spaces["enc"], sums
    )
    coarse = Block(
        PAD, DC, crs_gain, weights[4], weights[5], weights[6], crs_scale, spaces["crs"], sums
    )
    decoder = Block(
        BODY, D, dec_gain, weights[8], weights[9], weights[10], dec_scale, spaces["dec"], sums
    )
    merge_w, expand_w = weights[3], weights[7]
    coarse.wq_t, coarse.wo_t = (expand_w.at[:, pl.ds(n * DC, DC)] for n in range(2))
    coarse.wkv_t = keyval_t
    merge_t = (weights[4], weights[6])
    fn, fdmixed, fduq, fduk, fdqkv, fdn, fx, fb = spaces["fine"]
    cn, cdmixed, cduq, cduk, cdqkv, cdn, cx, cb = spaces["coarse"]

    def fine_bar(g):
        return bar_q[g // 2]

    def coarse_bar(g):
        return bar_q[0]

    def encode(windows):
        rows = encoder.rows_of(windows)
        encoder.project(windows, fn)
        encoder.attend(windows, fine_bar, bar_k[...])
        section = fx[rows, :] + encoder.branch(windows)
        fx[rows, :] = section
        fb[rows, :] = section.astype(BF16)

    def decode(windows):
        for g in windows:
            decoder.norm_rows(g, fx[at_rows(g), :], fn)
        decoder.project(windows, fn)
        decoder.attend(windows, fine_bar, bar_k[...])
        decoder.attend_back(windows, fdmixed, fduq, fduk, fdqkv)
        decoder.project_back(windows, fduq, fduk, fdqkv, fdn)
        for g in windows:
            at = at_rows(g)
            x = cot_f[at, :] + decoder.norm_backward(g, fdn[at, :])
            gskip[at, :] = x
            fb[at, :] = x.astype(BF16)

    def encode_back(windows):
        encoder.mixed_back(windows, fb, fdmixed)
        encoder.attend_back(windows, fdmixed, fduq, fduk, fdqkv)
        encoder.project_back(windows, fduq, fduk, fdqkv, fdn)
        for g in windows:
            at = at_rows(g)
            x = gskip[at, :] + encoder.norm_backward(g, fdn[at, :])
            fb[at, :] = x.astype(BF16)

    loaded(2)
    flat(fields_v, fields_b, fields_rest)
    prepare(0, fields_b[...], moves[0])
    pl.semaphore_wait(barrier, 6)
    launch(0, onward)
    load(*move(2, 6, 7, 8), *weight(3, 4, 5, 6, 7), *move(9, 10, 11), *weight(8, 9, 10))
    load(*move(3, 4, 5))
    loaded(4)
    fx[...] = mm(moves[1][...], fields_b[...]) + mm(moves[1][...], fields_rest[...])
    flat(cot_v, cot_b, cot_rest)
    prepare(1, cot_b[...], moves[0])
    cot_f[...] = mm(moves[1][...], cot_b[...]) + mm(moves[1][...], cot_rest[...])
    loaded(7)
    encoder.norm_rows(3, fx[at_rows(3), :], fn)
    encode(range(3, 4))
    loaded(8)
    arrive(0)

    def enter_encoder(g):
        at = at_rows(g)
        x = fx[at, :] + mm(moves[2][at, :], received[0])
        fx[at, :] = x
        encoder.norm_rows(g, x, fn)

    enter_encoder(1)
    enter_encoder(2)
    encode(range(1, 3))

    loaded(11)
    send(2, fb[PAD:, :], moves[6], onward)
    enter_encoder(0)
    encode(range(0, 1))
    planes[...] = mm(moves[7][...], fb[...])
    loaded(16)
    turn(expand_w, expand_t)
    turn(weights[5].at[:, pl.ds(0, DC)], keyval_t.at[pl.ds(0, DC), :])
    arrive(2)
    launch(1, onward)
    total = jnp.zeros((PAD, D), F32)
    for p in range(4):
        x = planes[at_rows(p), :] + mm(moves[8][at_rows(p), :], received[2])
        planes[at_rows(p), :] = x
        total += x
    mean = jnp.sum(total, axis=-1, keepdims=True) * (1.0 / (4 * D))
    total = jnp.zeros((PAD, D), F32)
    for p in range(4):
        centred = planes[at_rows(p), :] - mean
        total += centred * centred
    rstd = lax.rsqrt(jnp.sum(total, axis=-1, keepdims=True) * (1.0 / (4 * D)) + EPS)
    m_rstd[...] = jnp.broadcast_to(rstd, (PAD, 128))
    for p in range(4):
        lanes = at_lanes(p, D)
        xhat = (planes[at_rows(p), :] - mean) * rstd
        m_xhat[:, lanes] = xhat
        merged[:, lanes] = (xhat * merge_gain[:, lanes]).astype(BF16)
    cx[...] = mm(merged[...], merge_w[...])
    coarse.norm_rows(0, cx[...], cn)
    coarse.project(coarse.every, cn)
    coarse.attend(coarse.every, coarse_bar, bar_k[...])
    x = cx[...] + coarse.branch(coarse.every)
    centred = x - row_mean(x)
    rstd = lax.rsqrt(row_mean(centred * centred) + EPS)
    xhat = centred * rstd
    e_xhat[...] = xhat
    e_rstd[...] = jnp.broadcast_to(rstd, (PAD, 128))
    cb[...] = (xhat * exp_gain[...]).astype(BF16)
    for p in range(4):
        fb[at_rows(p), :] = mm(cb[...], expand_w[:, at_lanes(p, D)]).astype(BF16)

    loaded(len(loads))
    send(3, fb[...], moves[9], back)
    fx[...] = fx[...] + mm(moves[10][...], fb[...])
    arrive(1)
    cot = cot_f[...] + mm(moves[2][...], received[1])
    cot_f[...] = cot
    out_b[...] = cot.astype(BF16)
    decoder.mixed_back(decoder.every, out_b, fdmixed)
    decode(range(0, 1))
    arrive(3)
    later = pl.ds(PAD, 3 * PAD)
    fx[later, :] = fx[later, :] + mm(moves[11][later, :], received[3])
    decode(range(1, 4))

    send(5, fb[PAD:, :], moves[6], onward)
    planes[...] = mm(moves[7][...], fb[...])
    out_b[...] = (fx[...] + decoder.branch(decoder.every)).astype(BF16)
    prepare(4, out_b[: 3 * PAD, :], moves[3])
    turn(weights[6], coarse.wo_t)
    turn(weights[4], coarse.wq_t)
    turn(weights[5].at[:, pl.ds(DC, DC)], keyval_t.at[pl.ds(DC, DC), :])
    for n in range(2):
        turn(merge_w.at[pl.ds(n * DC, DC), :], merge_t[n])
    arrive(5)
    launch(4, back)
    for p in range(4):
        x = planes[at_rows(p), :] + mm(moves[8][at_rows(p), :], received[5])
        dexp[:, at_lanes(p, D)] = x.astype(BF16)
    dy = mm(dexp[...], expand_t[...]) * exp_gain[...]
    xhat = e_xhat[...]
    x = e_rstd[:, :1] * (dy - row_mean(dy) - xhat * row_mean(dy * xhat))
    cx[...] = x
    cb[...] = x.astype(BF16)
    coarse.mixed_back(coarse.every, cb, cdmixed)
    coarse.attend_back(coarse.every, cdmixed, cduq, cduk, cdqkv)
    coarse.project_back(coarse.every, cduq, cduk, cdqkv, cdn)
    cb[...] = (cx[...] + coarse.norm_backward(0, cdn[...])).astype(BF16)
    for p in range(4):
        planes[at_rows(p), :] = mm(cb[...], merge_t[p // 2][:, at_lanes(p % 2, D)])
    total = jnp.zeros((PAD, D), F32)
    weighed = jnp.zeros((PAD, D), F32)
    for p in range(4):
        lanes = at_lanes(p, D)
        dy = planes[at_rows(p), :] * merge_gain[:, lanes]
        total += dy
        weighed += dy * m_xhat[:, lanes]
    mean = jnp.sum(total, axis=-1, keepdims=True) * (1.0 / (4 * D))
    tilt = jnp.sum(weighed, axis=-1, keepdims=True) * (1.0 / (4 * D))
    rstd = m_rstd[:, :1]
    for p in range(4):
        lanes = at_lanes(p, D)
        dy = planes[at_rows(p), :] * merge_gain[:, lanes]
        fb[at_rows(p), :] = (rstd * (dy - mean - m_xhat[:, lanes] * tilt)).astype(BF16)

    send(6, fb[...], moves[9], back)
    x = gskip[...] + mm(moves[10][...], fb[...])
    gskip[...] = x
    fb[at_rows(0), :] = x[:PAD].astype(BF16)
    out_home[...] = mm(moves[4][...], out_b[...])
    encode_back(range(0, 1))
    encoder.wq_t, encoder.wo_t = weights[8], weights[10]
    encoder.wkv_t = keyval_t.at[pl.ds(0, 2 * D), pl.ds(0, D)]
    turn(weights[0], encoder.wq_t)
    turn(weights[1], encoder.wkv_t)
    turn(weights[2], encoder.wo_t)
    arrive(6)

    def enter_gradient(windows):
        at = encoder.rows_of(windows)
        x = gskip[at, :] + mm(moves[11][at, :], received[6])
        gskip[at, :] = x
        fb[at, :] = x.astype(BF16)

    enter_gradient(range(1, 3))
    encode_back(range(1, 3))

    send(7, fb[: 3 * PAD, :], moves[3], back)
    enter_gradient(range(3, 4))
    encode_back(range(3, 4))
    arrive(4)
    deliver(out_home, 4, 0)
    grad_home[...] = mm(moves[4][...], fb[...])
    arrive(7)
    deliver(grad_home, 7, 1)
    for t in started:
        for copy in started[t]:
            copy.wait_send()
    for copy in outs:
        copy.wait()


def shards(
    fields,
    cotangent,
    encoder_gain,
    encoder_query,
    encoder_keyval,
    encoder_output,
    encoder_scale,
    merge_gain,
    merge_weight,
    coarse_gain,
    coarse_query,
    coarse_keyval,
    coarse_output,
    coarse_scale,
    expand_gain,
    expand_weight,
    decoder_gain,
    decoder_query,
    decoder_keyval,
    decoder_output,
    decoder_scale,
):
    shape = fields.shape
    weights = (
        encoder_query,
        encoder_keyval,
        encoder_output,
        merge_weight,
        coarse_query,
        coarse_keyval,
        coarse_output,
        expand_weight,
        decoder_query,
        decoder_keyval,
        decoder_output,
    )
    moves = [jnp.asarray(m) for m in all_moves()]
    gains = [
        g.reshape(1, -1)
        for g in (encoder_gain, merge_gain, coarse_gain, expand_gain, decoder_gain)
    ]
    scales = (encoder_scale, coarse_scale, decoder_scale)
    flat = (HOME * 4, 128)
    anywhere = pl.BlockSpec(memory_space=pl.ANY)
    in_vmem = pl.BlockSpec(memory_space=pltpu.VMEM)
    in_smem = pl.BlockSpec(memory_space=pltpu.SMEM)
    scratch = [pltpu.VMEM(flat, F32)] * 2
    scratch += [pltpu.VMEM(w.shape, BF16) for w in weights]
    scratch += [pltpu.VMEM(m.shape, BF16) for m in moves]
    for name in NAMES:
        scratch += [pltpu.VMEM(s, t) for s, t in TABLE[name]]
    scratch += [
        pltpu.SemaphoreType.DMA((2 + len(weights) + len(moves),)),
        pltpu.SemaphoreType.DMA((2, 2)),
        pltpu.SemaphoreType.DMA((8, 3)),
        pltpu.SemaphoreType.DMA((8, 3)),
    ]
    results = pl.pallas_call(
        kernel,
        out_shape=jax.ShapeDtypeStruct((2,) + flat, BF16),
        in_specs=[anywhere] * (2 + len(weights) + len(moves)) + [in_vmem] * 5 + [in_smem] * 3,
        out_specs=anywhere,
        scratch_shapes=scratch,
        compiler_params=pltpu.CompilerParams(
            collective_id=0, has_side_effects=True, vmem_limit_bytes=60 * 1024 * 1024
        ),
    )(
        fields.reshape(flat),
        cotangent.reshape(flat),
        *weights,
        *moves,
        *gains,
        *scales,
    )
    return tuple(results[n].astype(F32).reshape(shape) for n in range(2))


def solution(mesh):
    along = P("lat", "lon", None, None)
    return jax.shard_map(
        shards,
        mesh=mesh,
        in_specs=(along, along) + (P(),) * 19,
        out_specs=(along, along),
        check_vma=False,
    )
```
